32 devices in a mesh: wide: 16 (over z, x, core), narrow: 2 (over y).
Axes of the slice: x: 2, y: 2, z: 4, core: 2. Of those that a mesh axis runs over, the one named last changes fastest.
Arguments:
- three_index: bfloat16 [16, 3072, 1024], P('wide', None, 'narrow'), may hold values from -0.59765625 to 0.59765625
- orbital_map: int32 [16], replicated, may hold values from 0 to 15, each once
- occ_energy: float32 [16], replicated, may hold values from -2 to -0.3
- vir_energy: float32 [1024], replicated, may hold values from 0.2 to 3
- pair_kept: int32 [6, 16], P(None, 'wide'), may hold values 0 or 1
Outputs:
- density: float32 [16, 3072, 1024], P('wide', None, 'narrow')
The draws below stay inside these ranges and needn't reach their ends.
Inputs may be any that keep to these rules, and one draw needn't show every extreme that they name: `orbital_map`: each of the 16 orbitals once.
All inputs are finite; a program needn't handle non-finite values. No bound on the sum of `pair_kept` on one device may be relied on, other than what follows from the above.
Results may differ from the reference program's by a relative error of at most 0.0015.
Values may be sent and summed in bfloat16 or wider, within the bound.
No kernel may reach another device: no remote copies, remote signals or barrier semaphores. Data moves between devices by JAX's collectives and lax.ppermute only.
A program may use at most 192 MiB of HBM per device.

```python
import jax
import jax.numpy as jnp
from jax import lax

NAUX = 3072
NVIR = 1024
OCC_DEV = 1
ROUNDS = 5
BLOCKS = 16
OCC = 16
N_WIDE = 16


def touch_ends(array, key, low, top_value):
    longest = array.shape.index(max(array.shape))
    spots = []
    for shift in (0, 1):
        where = [jax.random.randint(jax.random.fold_in(key, axis), (), 0, length) for axis, length in enumerate(array.shape)]
        where[longest] = (where[longest] + shift) % array.shape[longest]
        spots.append(tuple(where))
    return array.at[spots[0]].set(low).at[spots[1]].set(top_value)


def levels(rng, dims, split, least, high):
    level = 1.0
    for dim, parts in split:
        steps = jax.random.uniform(jax.random.fold_in(jax.random.fold_in(rng, 6), dim), (parts,), jnp.float32, least / len(split), high / len(split))
        level = level * jnp.repeat(jnp.exp(steps), dims[dim] // parts).reshape((-1,) + (1,) * (len(dims) - 1 - dim))
    return level


def scatter_about(key, dims, deviation, reach, split=(), kind=jnp.bfloat16):
    drawn = deviation * jax.random.normal(key, dims, jnp.float32)
    if split:
        drawn = drawn * levels(key, dims, split, -0.22, 0.18)
    return jnp.clip(drawn, -reach, reach).astype(kind)


def setup_inputs(seed: int = 0) -> dict:
    key_list = jax.random.split(jax.random.key(seed), 6)
    return {
        "three_index": scatter_about(key_list[0], (OCC, NAUX, NVIR), 0.1, 0.59765625, ((0, 16), (2, 2))),
        "orbital_map": jax.random.permutation(key_list[1], OCC).astype(jnp.int32),
        "occ_energy": jnp.clip(jax.random.uniform(key_list[2], (OCC,), jnp.float32, -2.0, -0.3), -2.0, -0.3),
        "vir_energy": jnp.clip(jax.random.uniform(key_list[3], (NVIR,), jnp.float32, 0.2, 3.0), 0.2, 3.0),
        "pair_kept": touch_ends((jax.random.randint(key_list[4], (ROUNDS + 1, BLOCKS), 0, 4) < 3).astype(jnp.int32), jax.random.fold_in(key_list[4], 1), 0, 1),
    }


def amplitudes(left, right, left_energy, right_energy, vir_energy, weight):
    coulomb = jnp.einsum("ipa,jpb->ijab", left.astype(jnp.float32), right.astype(jnp.float32))
    denominator = (vir_energy[:, None] + vir_energy[None, :])[None, None] - (left_energy[:, None] + right_energy[None, :])[:, :, None, None]
    rounded = lax.optimization_barrier((weight * coulomb / denominator).astype(jnp.bfloat16))
    return rounded.astype(jnp.float32)


def reference(three_index, orbital_map, occ_energy, vir_energy, pair_kept):
    blocks = three_index.reshape(N_WIDE, OCC_DEV, NAUX, NVIR)
    energies = occ_energy[orbital_map].reshape(N_WIDE, OCC_DEV)
    weights = pair_kept.astype(jnp.float32)

    def one_block(index):
        own_rows = blocks[index].astype(jnp.float32)
        own_energy = energies[index]
        forward = jnp.zeros((OCC_DEV, NAUX, NVIR), jnp.float32)
        for round_index in range(ROUNDS + 1):
            partner = (index - round_index) % N_WIDE
            right = blocks[partner].astype(jnp.float32)
            amplitude = amplitudes(own_rows, right, own_energy, energies[partner], vir_energy, weights[round_index, index])
            forward = forward + jnp.einsum("ijab,jpb->ipa", amplitude, right)
        backward = jnp.zeros((OCC_DEV, NAUX, NVIR), jnp.float32)
        for round_index in range(1, ROUNDS + 1):
            partner = (index + round_index) % N_WIDE
            left = blocks[partner].astype(jnp.float32)
            amplitude = amplitudes(left, own_rows, energies[partner], own_energy, vir_energy, weights[round_index, partner])
            backward = backward + jnp.einsum("ijab,ipa->jpb", amplitude, left)
        return forward + backward

    result = lax.map(one_block, jnp.arange(N_WIDE, dtype=jnp.int32))
    return result.reshape(N_WIDE * OCC_DEV, NAUX, NVIR)
```

```python
import jax
import jax.numpy as jnp
import numpy as np
from jax import lax
from jax.experimental import pallas as pl
from jax.experimental.pallas import tpu as pltpu
from jax.sharding import PartitionSpec as P

ROUNDS = 5
VMEM = 56 * 1024 * 1024


def passed_along(array, axis, by):
    length = lax.axis_size(axis)
    return lax.ppermute(array, axis, [(i, (i + by) % length) for i in range(length)])


def block_energy(orbital_map, occ_energy, block_id, occ_count):
    orbits = lax.dynamic_slice_in_dim(orbital_map, block_id * occ_count, occ_count)
    labels = jnp.arange(occ_energy.shape[0], dtype=jnp.int32)
    chosen = orbits[:, None] == labels[None, :]
    return jnp.sum(jnp.where(chosen, occ_energy[None, :], 0.0), axis=1)


def amplitudes(gathered, visiting, left_energy, right_energy, vir_all, vir_local, weight):
    coulomb = jnp.einsum("ipa,jpb->ijab", gathered, visiting, preferred_element_type=jnp.float32)
    denominator = (vir_all[:, None] + vir_local[None, :])[None, None] - (
        left_energy[:, None] + right_energy[None, :]
    )[:, :, None, None]
    return (weight * coulomb / denominator).astype(jnp.bfloat16)


def ring_plan(three_index, orbital_map, occ_energy, vir_energy, pair_kept):
    occ_count = three_index.shape[0]
    vir_count = three_index.shape[2]
    blocks = lax.axis_size("wide")
    own_block = lax.axis_index("wide")
    vir_local = lax.dynamic_slice_in_dim(
        vir_energy, lax.axis_index("narrow") * vir_count, vir_count
    )
    own_energy = block_energy(orbital_map, occ_energy, own_block, occ_count)
    weights = pair_kept.astype(jnp.float32)
    gathered = lax.all_gather(three_index, "narrow", axis=2, tiled=True)
    amplitude = amplitudes(
        gathered, three_index, own_energy, own_energy, vir_energy, vir_local, weights[0, 0]
    )
    forward = jnp.einsum(
        "ijab,jpb->ipa", amplitude, three_index, preferred_element_type=jnp.float32
    )
    visiting = three_index
    stored_amps = []
    for round_index in range(1, ROUNDS + 1):
        visiting = passed_along(visiting, "wide", 1)
        partner = (own_block - round_index) % blocks
        partner_energy = block_energy(orbital_map, occ_energy, partner, occ_count)
        amplitude = amplitudes(
            gathered,
            visiting,
            own_energy,
            partner_energy,
            vir_energy,
            vir_local,
            weights[round_index, 0],
        )
        forward = forward + jnp.einsum(
            "ijab,jpb->ipa", amplitude, visiting, preferred_element_type=jnp.float32
        )
        stored_amps.append(amplitude)
    carried = None
    for round_index in range(1, ROUNDS + 1):
        backward = jnp.einsum(
            "ijab,ipa->jpb",
            stored_amps[round_index - 1],
            gathered,
            preferred_element_type=jnp.float32,
        )
        if round_index > 1:
            carried = passed_along(carried, "wide", 1) + backward
        else:
            carried = backward
    returned = passed_along(carried, "wide", -ROUNDS)
    scattered = lax.psum_scatter(forward, "narrow", scatter_dimension=2, tiled=True)
    return scattered + returned


class Routes:
    def __init__(self, blocks):
        self.blocks = blocks
        self.own = list(range(blocks))
        lead = [self.leads(w) for w in range(blocks)]
        self.lead = np.array(lead)
        self.swap = [(w, w ^ 1) for w in range(blocks)]

        def hop(step, by_lead):
            pairs = []
            for w in range(blocks):
                along_z = lead[w] == by_lead
                pairs.append((w, self.along_z(w, step) if along_z else self.across_x(w)))
            return pairs

        self.pairs = [hop(1, True), hop(1, False), hop(-1, True), hop(-1, False), hop(-1, True)]

    def place(self, w):
        return w // 4, (w // 2) % 2, w % 2

    def leads(self, w):
        _, x, core = self.place(w)
        return x == core

    def along_z(self, w, step):
        z, x, core = self.place(w)
        z = (z + (step if x == 1 else -step)) % (self.blocks // 4)
        return (z * 2 + x) * 2 + core

    def across_x(self, w):
        z, x, core = self.place(w)
        return (z * 2 + 1 - x) * 2 + 1 - core

    def moved(self, ids, pairs):
        out = [0] * self.blocks
        for source, target in pairs:
            out[target] = ids[source]
        return out

    def chosen(self, ids_lead, ids_other):
        return [a if lead else b for lead, a, b in zip(self.lead, ids_lead, ids_other)]


class Slab:
    def __init__(self, array, ids):
        self.array = array
        self.ids = ids


def tile_of(length, most):
    size = min(length, most)
    while length % size:
        size -= 8
    return size


def amplitude_kernel(scalars, rows, slab, vir_rows, vir_cols, out):
    coulomb = jnp.dot(rows[...], slab[...], preferred_element_type=jnp.float32)
    denominator = (vir_rows[...] + vir_cols[...]) - scalars[0, 0]
    out[...] = (scalars[0, 1] * coulomb / denominator).astype(out.dtype)


def amplitude_call(scalars, turned, slab, vir_rows, vir_cols):
    rows, aux = turned.shape
    cols = slab.shape[1]
    tile = tile_of(rows, 256)
    return pl.pallas_call(
        amplitude_kernel,
        grid=(rows // tile,),
        in_specs=[
            pl.BlockSpec(memory_space=pltpu.SMEM),
            pl.BlockSpec((tile, aux), lambda i: (i, 0)),
            pl.BlockSpec((aux, cols), lambda i: (0, 0)),
            pl.BlockSpec((tile, 1), lambda i: (i, 0)),
            pl.BlockSpec((1, cols), lambda i: (0, 0)),
        ],
        out_specs=pl.BlockSpec((tile, cols), lambda i: (i, 0)),
        out_shape=jax.ShapeDtypeStruct((rows, cols), jnp.bfloat16),
        compiler_params=pltpu.CompilerParams(vmem_limit_bytes=VMEM),
        cost_estimate=pl.CostEstimate(
            flops=2 * rows * aux * cols,
            bytes_accessed=2 * (rows * aux + aux * cols + rows * cols),
            transcendentals=0,
        ),
    )(scalars, turned, slab, vir_rows, vir_cols)


def density_call(slabs, amps, parts, out_dtype):
    count = len(slabs)
    aux, depth = slabs[0].shape
    cols = amps[0].shape[0]
    tile = tile_of(aux, 256)

    def kernel(*refs):
        out = refs[-1]
        total = None
        for ref in refs[2 * count : -1]:
            part = ref[...].astype(jnp.float32)
            total = part if total is None else total + part
        for slab, amp in zip(refs[:count], refs[count : 2 * count]):
            term = lax.dot_general(
                slab[...], amp[...], (((1,), (1,)), ((), ())), preferred_element_type=jnp.float32
            )
            total = term if total is None else total + term
        out[...] = total.astype(out.dtype)

    bytes_in = sum(x.size * x.dtype.itemsize for x in (*slabs, *amps, *parts))
    return pl.pallas_call(
        kernel,
        grid=(aux // tile,),
        in_specs=[pl.BlockSpec((tile, depth), lambda i: (i, 0))] * count
        + [pl.BlockSpec((cols, depth), lambda i: (0, 0))] * count
        + [pl.BlockSpec((tile, cols), lambda i: (i, 0))] * len(parts),
        out_specs=pl.BlockSpec((tile, cols), lambda i: (i, 0)),
        out_shape=jax.ShapeDtypeStruct((aux, cols), out_dtype),
        compiler_params=pltpu.CompilerParams(vmem_limit_bytes=VMEM),
        cost_estimate=pl.CostEstimate(
            flops=2 * aux * depth * cols * count,
            bytes_accessed=bytes_in + aux * cols * jnp.dtype(out_dtype).itemsize,
            transcendentals=0,
        ),
    )(*slabs, *amps, *parts)


def paired_plan(three_index, orbital_map, occ_energy, vir_energy, pair_kept):
    blocks = lax.axis_size("wide")
    routes = Routes(blocks)
    here = lax.axis_index("wide")
    side = lax.axis_index("narrow")
    vir_count = three_index.shape[2]
    lead = jnp.asarray(routes.lead)[here]

    def moved(slab, pairs):
        return Slab(lax.ppermute(slab.array, "wide", pairs), routes.moved(slab.ids, pairs))

    def swapped(slab):
        return moved(slab, routes.swap)

    def chosen(slab_lead, slab_other):
        return Slab(
            jnp.where(lead, slab_lead.array, slab_other.array),
            routes.chosen(slab_lead.ids, slab_other.ids),
        )

    def sibling(array):
        return lax.ppermute(array, "narrow", [(0, 1), (1, 0)])

    labels = jnp.arange(occ_energy.shape[0], dtype=jnp.int32)
    picked = orbital_map[:, None] == labels[None, :]
    energy = jnp.sum(jnp.where(picked, occ_energy[None, :], 0.0), axis=1)
    kept = lax.all_gather(pair_kept.astype(jnp.float32), "wide", axis=1, tiled=True)

    def scalars(slab):
        block = jnp.asarray(np.array(slab.ids, np.int32))[here]
        ahead = (here - block) % blocks
        behind = (block - here) % blocks
        weight = jnp.where(
            ahead <= ROUNDS,
            kept[jnp.minimum(ahead, ROUNDS), here],
            kept[jnp.minimum(behind, ROUNDS), block],
        )
        return jnp.stack([energy[here] + energy[block], weight]).reshape(1, 2)

    vir_near = lax.dynamic_slice_in_dim(vir_energy, side * vir_count, vir_count)
    vir_far = lax.dynamic_slice_in_dim(vir_energy, (1 - side) * vir_count, vir_count)
    near_rows, near_cols = vir_near[:, None], vir_near[None, :]
    far_rows, far_cols = vir_far[:, None], vir_far[None, :]

    own = Slab(three_index[0], routes.own)
    r1 = moved(own, routes.pairs[0])
    own_far = Slab(sibling(own.array), routes.own)
    mate = swapped(own)
    s1 = swapped(r1)
    r2 = moved(chosen(r1, own), routes.pairs[1])
    s2 = swapped(r2)
    r3 = moved(chosen(mate, r2), routes.pairs[2])
    s3 = swapped(r3)
    r4 = moved(chosen(r3, s2), routes.pairs[3])
    s4 = swapped(r4)
    mate_far = swapped(own_far)
    r5 = moved(chosen(own, mate), routes.pairs[4])
    s5 = swapped(r5)
    r6 = moved(chosen(own_far, mate_far), routes.pairs[4])
    s6 = swapped(r6)

    turned = own.array.T
    turned_far = own_far.array.T

    def near_amp(slab):
        return amplitude_call(scalars(slab), turned, slab.array, near_rows, near_cols)

    def far_amp(slab):
        return amplitude_call(scalars(slab), turned_far, slab.array, far_rows, near_cols)

    def near_amp_of_far(slab):
        return amplitude_call(scalars(slab), turned, slab.array, near_rows, far_cols)

    early = [r1, s1, r2, s2, r3, s3, s4]
    outgoing = density_call(
        [s.array for s in early], [far_amp(s) for s in early], [], jnp.bfloat16
    )
    incoming = sibling(outgoing)
    held = early + [own, mate, r5, s5]
    held_far = [own_far, mate_far]
    partial = density_call(
        [s.array for s in held + held_far],
        [near_amp(s) for s in held] + [near_amp_of_far(s) for s in held_far],
        [],
        jnp.float32,
    )
    late = [r6, s6]
    density = density_call(
        [s.array for s in late],
        [near_amp_of_far(s) for s in late],
        [partial, incoming],
        jnp.float32,
    )
    return density[None]


def solution(mesh):
    wide, narrow = mesh.shape["wide"], mesh.shape["narrow"]
    paired = narrow == 2 and wide % 4 == 0 and wide > 2 * ROUNDS + 1 and ROUNDS == 5

    def per_device(three_index, *rest):
        if paired and three_index.shape[0] == 1:
            return paired_plan(three_index, *rest)
        return ring_plan(three_index, *rest)

    placed = (P("wide", None, "narrow"), P(), P(), P(), P(None, "wide"))
    return jax.shard_map(
        per_device, mesh=mesh, in_specs=placed, out_specs=P("wide", None, "narrow"), check_vma=False
    )
```

```python
import jax
import jax.numpy as jnp
import numpy as np
from jax import lax
from jax.experimental import pallas as pl
from jax.experimental.pallas import tpu as pltpu
from jax.sharding import PartitionSpec as P

ROUNDS = 5
VMEM = 56 * 1024 * 1024


def passed_along(array, axis, by):
    length = lax.axis_size(axis)
    return lax.ppermute(array, axis, [(i, (i + by) % length) for i in range(length)])


def block_energy(orbital_map, occ_energy, block_id, occ_count):
    orbits = lax.dynamic_slice_in_dim(orbital_map, block_id * occ_count, occ_count)
    labels = jnp.arange(occ_energy.shape[0], dtype=jnp.int32)
    chosen = orbits[:, None] == labels[None, :]
    return jnp.sum(jnp.where(chosen, occ_energy[None, :], 0.0), axis=1)


def amplitudes(gathered, visiting, left_energy, right_energy, vir_all, vir_local, weight):
    coulomb = jnp.einsum("ipa,jpb->ijab", gathered, visiting, preferred_element_type=jnp.float32)
    denominator = (vir_all[:, None] + vir_local[None, :])[None, None] - (
        left_energy[:, None] + right_energy[None, :]
    )[:, :, None, None]
    return (weight * coulomb / denominator).astype(jnp.bfloat16)


def ring_plan(three_index, orbital_map, occ_energy, vir_energy, pair_kept):
    occ_count = three_index.shape[0]
    vir_count = three_index.shape[2]
    blocks = lax.axis_size("wide")
    own_block = lax.axis_index("wide")
    vir_local = lax.dynamic_slice_in_dim(
        vir_energy, lax.axis_index("narrow") * vir_count, vir_count
    )
    own_energy = block_energy(orbital_map, occ_energy, own_block, occ_count)
    weights = pair_kept.astype(jnp.float32)
    gathered = lax.all_gather(three_index, "narrow", axis=2, tiled=True)
    amplitude = amplitudes(
        gathered, three_index, own_energy, own_energy, vir_energy, vir_local, weights[0, 0]
    )
    forward = jnp.einsum(
        "ijab,jpb->ipa", amplitude, three_index, preferred_element_type=jnp.float32
    )
    visiting = three_index
    stored_amps = []
    for round_index in range(1, ROUNDS + 1):
        visiting = passed_along(visiting, "wide", 1)
        partner = (own_block - round_index) % blocks
        partner_energy = block_energy(orbital_map, occ_energy, partner, occ_count)
        amplitude = amplitudes(
            gathered,
            visiting,
            own_energy,
            partner_energy,
            vir_energy,
            vir_local,
            weights[round_index, 0],
        )
        forward = forward + jnp.einsum(
            "ijab,jpb->ipa", amplitude, visiting, preferred_element_type=jnp.float32
        )
        stored_amps.append(amplitude)
    carried = None
    for round_index in range(1, ROUNDS + 1):
        backward = jnp.einsum(
            "ijab,ipa->jpb",
            stored_amps[round_index - 1],
            gathered,
            preferred_element_type=jnp.float32,
        )
        if round_index > 1:
            carried = passed_along(carried, "wide", 1) + backward
        else:
            carried = backward
    returned = passed_along(carried, "wide", -ROUNDS)
    scattered = lax.psum_scatter(forward, "narrow", scatter_dimension=2, tiled=True)
    return scattered + returned


class Routes:
    def __init__(self, blocks):
        self.blocks = blocks
        everyone = range(blocks)
        self.lead = [self.place(w)[1] == self.place(w)[2] for w in everyone]
        self.swap = [(w, w ^ 1) for w in everyone]
        self.onward = [(w, self.along_z(w, 1)) for w in everyone]
        self.backward = [(w, self.along_z(w, -1)) for w in everyone]
        self.across = [(w, self.across_x(w)) for w in everyone]
        self.last = [pair[0 if lead else 1] for lead, *pair in zip(self.lead, self.backward, self.across)]

    def place(self, w):
        return w // 4, (w // 2) % 2, w % 2

    def along_z(self, w, step):
        z, x, core = self.place(w)
        z = (z + (step if x == 1 else -step)) % (self.blocks // 4)
        return (z * 2 + x) * 2 + core

    def across_x(self, w):
        z, x, core = self.place(w)
        return (z * 2 + 1 - x) * 2 + 1 - core

    def moved(self, ids, pairs):
        out = [0] * self.blocks
        for source, target in pairs:
            out[target] = ids[source]
        return out


class Slab:
    def __init__(self, array, ids):
        self.array = array
        self.ids = ids


def tile_of(length, most):
    size = min(length, most)
    while length % size:
        size -= 8
    return size


def amplitude_kernel(scalars, rows, slab, vir_rows, vir_cols, out):
    coulomb = jnp.dot(rows[...], slab[...], preferred_element_type=jnp.float32)
    denominator = (vir_rows[...] + vir_cols[...]) - scalars[0, 0]
    out[...] = (scalars[0, 1] * coulomb / denominator).astype(out.dtype)


def amplitude_call(scalars, turned, slab, vir_rows, vir_cols, first, count):
    aux = turned.shape[1]
    cols = slab.shape[1]
    tile = cols
    return pl.pallas_call(
        amplitude_kernel,
        grid=(count,),
        in_specs=[
            pl.BlockSpec(memory_space=pltpu.SMEM),
            pl.BlockSpec((tile, aux), lambda i: (first + i, 0)),
            pl.BlockSpec((aux, cols), lambda i: (0, 0)),
            pl.BlockSpec((tile, 1), lambda i: (first + i, 0)),
            pl.BlockSpec((1, cols), lambda i: (0, 0)),
        ],
        out_specs=pl.BlockSpec((tile, cols), lambda i: (i, 0)),
        out_shape=jax.ShapeDtypeStruct((count * tile, cols), jnp.bfloat16),
        compiler_params=pltpu.CompilerParams(vmem_limit_bytes=VMEM),
        cost_estimate=pl.CostEstimate(
            flops=2 * count * tile * aux * cols,
            bytes_accessed=2 * (count * tile * aux + aux * cols + count * tile * cols),
            transcendentals=0,
        ),
    )(scalars, turned, slab, vir_rows, vir_cols)


def density_call(terms, parts, out_dtype, rows=None):
    count = len(terms)
    aux, depth = terms[0][0].shape if terms else parts[0].shape
    cols = depth
    begin, length = rows or (0, aux)
    tile = tile_of(length, 512)
    skip = begin // tile

    def kernel(*refs):
        out = refs[-1]
        total = None
        for ref in refs[2 * count : -1]:
            part = ref[...].astype(jnp.float32)
            total = part if total is None else total + part
        for slab, amp in zip(refs[:count], refs[count : 2 * count]):
            term = lax.dot_general(
                slab[...], amp[...], (((1,), (1,)), ((), ())), preferred_element_type=jnp.float32
            )
            total = term if total is None else total + term
        out[...] = total.astype(out.dtype)

    def rows_of(array):
        shift = skip if array.shape[0] == aux else 0
        return pl.BlockSpec((tile, array.shape[1]), lambda i: (i + shift, 0))

    def amp_block(index):
        return pl.BlockSpec((cols, depth), lambda i: (index, 0))

    bytes_in = sum(t[0].size * 2 + cols * depth * 2 for t in terms)
    bytes_in += sum(p.size * p.dtype.itemsize for p in parts)
    return pl.pallas_call(
        kernel,
        grid=(length // tile,),
        in_specs=[rows_of(t[0]) for t in terms]
        + [amp_block(t[2]) for t in terms]
        + [rows_of(p) for p in parts],
        out_specs=pl.BlockSpec((tile, cols), lambda i: (i, 0)),
        out_shape=jax.ShapeDtypeStruct((length, cols), out_dtype),
        compiler_params=pltpu.CompilerParams(vmem_limit_bytes=VMEM),
        cost_estimate=pl.CostEstimate(
            flops=2 * length * depth * cols * count,
            bytes_accessed=bytes_in * length // aux + length * cols * jnp.dtype(out_dtype).itemsize,
            transcendentals=0,
        ),
    )(*[t[0] for t in terms], *[t[1] for t in terms], *parts)


def kept_ahead(pair_kept, blocks):
    run = pair_kept.astype(jnp.float32).reshape(1, ROUNDS + 1)
    while run.shape[0] < ROUNDS + 1:
        have = run.shape[0]
        take = min(have, ROUNDS + 1 - have)
        run = jnp.concatenate([run, passed_along(run[:take], "wide", -have)])
    return jnp.diagonal(run)


def paired_plan(three_index, orbital_map, occ_energy, vir_energy, pair_kept):
    blocks = lax.axis_size("wide")
    routes = Routes(blocks)
    here = lax.axis_index("wide")
    side = lax.axis_index("narrow")
    aux, vir_count = three_index.shape[1:]
    lead = jnp.asarray(np.array(routes.lead))[here]

    def moved(slab, pairs):
        return Slab(lax.ppermute(slab.array, "wide", pairs), routes.moved(slab.ids, pairs))

    def swapped(slab):
        return moved(slab, routes.swap)

    def sibling(array):
        return lax.ppermute(array, "narrow", [(0, 1), (1, 0)])

    def after(slab, *others):
        return Slab(lax.optimization_barrier((slab.array, *others))[0], slab.ids)

    labels = jnp.arange(occ_energy.shape[0], dtype=jnp.int32)
    picked = orbital_map[:, None] == labels[None, :]
    energy = jnp.sum(jnp.where(picked, occ_energy[None, :], 0.0), axis=1)
    behind = pair_kept[:, 0].astype(jnp.float32)
    ahead = kept_ahead(pair_kept, blocks)

    vir_near = lax.dynamic_slice_in_dim(vir_energy, side * vir_count, vir_count)
    vir_far = lax.dynamic_slice_in_dim(vir_energy, (1 - side) * vir_count, vir_count)
    vir_rows = jnp.concatenate([vir_near, vir_far])[:, None]
    near_cols, far_cols = vir_near[None, :], vir_far[None, :]

    own = Slab(three_index[0], list(range(blocks)))
    onward = moved(own, routes.onward)
    across = moved(own, routes.across)
    own_far = Slab(sibling(own.array), own.ids)
    mate = swapped(own)
    mate_far = swapped(own_far)
    turned = jnp.concatenate([own.array, own_far.array], axis=1).T

    def scalars(slab):
        block = jnp.asarray(np.array(slab.ids, np.int32))[here]
        back = (here - block) % blocks
        forth = (block - here) % blocks
        weight = jnp.where(
            back <= ROUNDS, behind[jnp.minimum(back, ROUNDS)], ahead[jnp.minimum(forth, ROUNDS)]
        )
        return jnp.stack([energy[here] + energy[block], weight]).reshape(1, 2)

    def amp(slab, cols=near_cols, first=0, count=2):
        return amplitude_call(scalars(slab), turned, slab.array, vir_rows, cols, first, count)

    near, far = 0, 1
    at_home = [
        (own.array, amp(own, count=1), near),
        (own_far.array, amp(own_far, far_cols, count=1), near),
        (mate.array, amp(mate, count=1), near),
        (mate_far.array, amp(mate_far, far_cols, count=1), near),
    ]
    onward = after(onward, *[t[1] for t in at_home])

    onward_across = moved(onward, routes.across)
    backward = moved(after(own, onward.array), routes.backward)
    first = [onward, across, swapped(onward), swapped(across)]
    first = [(s.array, amp(s)) for s in first]
    out_part = density_call([(*t, far) for t in first], [], jnp.float32)
    near_part = density_call([(*t, near) for t in first] + at_home, [], jnp.float32)
    backward = after(backward, out_part, near_part)

    second = [onward_across, swapped(onward_across), backward, swapped(backward)]
    last = moved(
        Slab(
            jnp.where(lead, onward_across.array, backward.array),
            [a if lead else b for lead, a, b in zip(routes.lead, onward_across.ids, backward.ids)],
        ),
        routes.last,
    )
    second = [(s.array, amp(s)) for s in second]
    out_part = density_call([(*t, far) for t in second], [out_part], jnp.float32)
    near_part = density_call([(*t, near) for t in second], [near_part], jnp.float32)
    last = after(last, out_part, near_part)

    last_far = amp(last, first=far, count=1)
    ranges = [(begin, aux // 2) for begin in range(0, aux, aux // 2)]
    incoming = []
    for rows in ranges:
        outgoing = density_call([(last.array, last_far, near)], [out_part], jnp.bfloat16, rows)
        incoming.append(sibling(outgoing))
    last_near = amp(last, first=near, count=1)
    near_part = density_call([(last.array, last_near, near)], [near_part], jnp.float32)
    density = near_part + jnp.concatenate(incoming).astype(jnp.float32)
    return density[None]


def solution(mesh):
    wide, narrow = mesh.shape["wide"], mesh.shape["narrow"]
    paired = narrow == 2 and wide % 4 == 0 and wide > 2 * ROUNDS + 1 and ROUNDS == 5

    def per_device(three_index, *rest):
        if paired and three_index.shape[0] == 1:
            return paired_plan(three_index, *rest)
        return ring_plan(three_index, *rest)

    placed = (P("wide", None, "narrow"), P(), P(), P(), P(None, "wide"))
    return jax.shard_map(
        per_device, mesh=mesh, in_specs=placed, out_specs=P("wide", None, "narrow"), check_vma=False
    )
```

```python
import jax
import jax.numpy as jnp
import numpy as np
from jax import lax
from jax.experimental import pallas as pl
from jax.experimental.pallas import tpu as pltpu
from jax.sharding import PartitionSpec as P

ROUNDS = 5
PIECES = 2
VMEM = 56 * 1024 * 1024


def passed_along(array, axis, by):
    length = lax.axis_size(axis)
    return lax.ppermute(array, axis, [(i, (i + by) % length) for i in range(length)])


def block_energy(orbital_map, occ_energy, block_id, occ_count):
    orbits = lax.dynamic_slice_in_dim(orbital_map, block_id * occ_count, occ_count)
    labels = jnp.arange(occ_energy.shape[0], dtype=jnp.int32)
    chosen = orbits[:, None] == labels[None, :]
    return jnp.sum(jnp.where(chosen, occ_energy[None, :], 0.0), axis=1)


def amplitudes(gathered, visiting, left_energy, right_energy, vir_all, vir_local, weight):
    coulomb = jnp.einsum("ipa,jpb->ijab", gathered, visiting, preferred_element_type=jnp.float32)
    denominator = (vir_all[:, None] + vir_local[None, :])[None, None] - (
        left_energy[:, None] + right_energy[None, :]
    )[:, :, None, None]
    return (weight * coulomb / denominator).astype(jnp.bfloat16)


def ring_plan(three_index, orbital_map, occ_energy, vir_energy, pair_kept):
    occ_count = three_index.shape[0]
    vir_count = three_index.shape[2]
    blocks = lax.axis_size("wide")
    own_block = lax.axis_index("wide")
    vir_local = lax.dynamic_slice_in_dim(
        vir_energy, lax.axis_index("narrow") * vir_count, vir_count
    )
    own_energy = block_energy(orbital_map, occ_energy, own_block, occ_count)
    weights = pair_kept.astype(jnp.float32)
    gathered = lax.all_gather(three_index, "narrow", axis=2, tiled=True)
    amplitude = amplitudes(
        gathered, three_index, own_energy, own_energy, vir_energy, vir_local, weights[0, 0]
    )
    forward = jnp.einsum(
        "ijab,jpb->ipa", amplitude, three_index, preferred_element_type=jnp.float32
    )
    visiting = three_index
    stored_amps = []
    for round_index in range(1, ROUNDS + 1):
        visiting = passed_along(visiting, "wide", 1)
        partner = (own_block - round_index) % blocks
        partner_energy = block_energy(orbital_map, occ_energy, partner, occ_count)
        amplitude = amplitudes(
            gathered,
            visiting,
            own_energy,
            partner_energy,
            vir_energy,
            vir_local,
            weights[round_index, 0],
        )
        forward = forward + jnp.einsum(
            "ijab,jpb->ipa", amplitude, visiting, preferred_element_type=jnp.float32
        )
        stored_amps.append(amplitude)
    carried = None
    for round_index in range(1, ROUNDS + 1):
        backward = jnp.einsum(
            "ijab,ipa->jpb",
            stored_amps[round_index - 1],
            gathered,
            preferred_element_type=jnp.float32,
        )
        if round_index > 1:
            carried = passed_along(carried, "wide", 1) + backward
        else:
            carried = backward
    returned = passed_along(carried, "wide", -ROUNDS)
    scattered = lax.psum_scatter(forward, "narrow", scatter_dimension=2, tiled=True)
    return scattered + returned


class Routes:
    def __init__(self, blocks):
        self.blocks = blocks
        everyone = range(blocks)
        self.lead = [self.place(w)[1] == self.place(w)[2] for w in everyone]
        self.swap = [(w, w ^ 1) for w in everyone]
        onward = [(w, self.along_z(w, 1)) for w in everyone]
        backward = [(w, self.along_z(w, -1)) for w in everyone]
        across = [(w, self.across_x(w)) for w in everyone]
        self.rounds = [
            self.either(onward, across),
            self.either(across, onward),
            self.either(backward, across),
            self.either(across, backward),
            self.either(backward, across),
        ]

    def place(self, w):
        return w // 4, (w // 2) % 2, w % 2

    def along_z(self, w, step):
        z, x, core = self.place(w)
        z = (z + (step if x == 1 else -step)) % (self.blocks // 4)
        return (z * 2 + x) * 2 + core

    def across_x(self, w):
        z, x, core = self.place(w)
        return (z * 2 + 1 - x) * 2 + 1 - core

    def either(self, of_lead, of_other):
        return [a if lead else b for lead, a, b in zip(self.lead, of_lead, of_other)]

    def moved(self, ids, pairs):
        out = [0] * self.blocks
        for source, target in pairs:
            out[target] = ids[source]
        return out


class Slab:
    def __init__(self, pieces, ids, far=False):
        self.pieces = list(pieces)
        self.ids = ids
        self.far = far


def copy_in(sources, place, sems, start):
    row = 0
    for index, source in enumerate(sources):
        rows = source.shape[0]
        copy = pltpu.make_async_copy(source, place.at[pl.ds(row, rows)], sems.at[index])
        copy.start() if start else copy.wait()
        row += rows


def amplitude_call(table, base, slabs, turned, vir_rows, vir_cols):
    count = len(slabs)
    pieces = len(slabs[0].pieces)
    rows, aux = turned.shape
    cols = slabs[0].pieces[0].shape[1]
    tile = cols
    blocks = rows // tile

    def kernel(scalars, *refs):
        sources = [refs[s * pieces : (s + 1) * pieces] for s in range(count)]
        row_ref, vir_row_ref, vir_col_ref, out, held, sems = refs[count * pieces :]
        s, j = pl.program_id(0), pl.program_id(1)
        slot = s % 2

        def fetch(which, start):
            for index in range(count):

                @pl.when(which == index)
                def _(index=index):
                    copy_in(sources[index], held.at[index % 2], sems.at[index % 2], start)

        @pl.when(jnp.logical_and(s == 0, j == 0))
        def _():
            fetch(s, True)

        @pl.when(j == 0)
        def _():
            fetch(s, False)
            fetch(s + 1, True)

        coulomb = jnp.dot(row_ref[...], held[slot], preferred_element_type=jnp.float32)
        denominator = (vir_row_ref[...] + vir_col_ref[0]) - scalars[base + s, 0]
        out[0] = (scalars[base + s, 1] * coulomb / denominator).astype(out.dtype)

    def block(s, j):
        return jnp.where(s % 2 == 1, blocks - 1 - j, j)

    return pl.pallas_call(
        kernel,
        grid=(count, blocks),
        in_specs=[pl.BlockSpec(memory_space=pltpu.SMEM)]
        + [pl.BlockSpec(memory_space=pl.ANY)] * (count * pieces)
        + [
            pl.BlockSpec((tile, aux), lambda s, j: (block(s, j), 0)),
            pl.BlockSpec((tile, 1), lambda s, j: (block(s, j), 0)),
            pl.BlockSpec((1, 1, cols), lambda s, j: (s, 0, 0)),
        ],
        out_specs=pl.BlockSpec((1, tile, cols), lambda s, j: (s, block(s, j), 0)),
        out_shape=jax.ShapeDtypeStruct((count, rows, cols), jnp.bfloat16),
        scratch_shapes=[
            pltpu.VMEM((2, aux, cols), jnp.bfloat16),
            pltpu.SemaphoreType.DMA((2, pieces)),
        ],
        compiler_params=pltpu.CompilerParams(vmem_limit_bytes=VMEM),
        cost_estimate=pl.CostEstimate(
            flops=2 * count * rows * aux * cols,
            bytes_accessed=2 * (count * rows * aux + count * aux * cols + count * rows * cols),
            transcendentals=0,
        ),
    )(table, *[p for s in slabs for p in s.pieces], turned, vir_rows, vir_cols)


def density_call(terms, parts, out_dtype, rows=None):
    count = len(terms)
    pieces = len(terms[0][0].pieces)
    piece_rows, depth = terms[0][0].pieces[0].shape
    aux = piece_rows * pieces
    cols = depth
    begin, length = rows or (0, aux)
    tile = 512
    while length % tile or begin % tile or piece_rows % tile:
        tile //= 2
    first, steps, in_piece = begin // tile, length // tile, piece_rows // tile
    counts = [len(part) for part in parts]
    parts = [p for part in parts for p in part]

    def kernel(*refs):
        sources = [refs[s * pieces : (s + 1) * pieces] for s in range(count)]
        refs = refs[count * pieces :]
        amps, part_refs = refs[:count], refs[count : count + len(parts)]
        out, left, right, left_sems, right_sems = refs[count + len(parts) :]
        step = pl.program_id(0)
        slot = step % 2

        def amp_copies():
            for s, (_, _, place, block) in enumerate(terms):
                yield pltpu.make_async_copy(
                    amps[s].at[place, pl.ds(block * cols, cols), :],
                    right.at[:, pl.ds(s * depth, depth)],
                    right_sems.at[s],
                )

        def fetch(which, start):
            at = which + first
            for piece in range(pieces):

                @pl.when(jnp.logical_and(which < steps, at // in_piece == piece))
                def _(piece=piece):
                    row = pl.multiple_of((at - piece * in_piece) * tile, tile)
                    for s in range(count):
                        copy = pltpu.make_async_copy(
                            sources[s][piece].at[pl.ds(row, tile), :],
                            left.at[which % 2, :, pl.ds(s * depth, depth)],
                            left_sems.at[which % 2, s],
                        )
                        copy.start() if start else copy.wait()

        @pl.when(step == 0)
        def _():
            for copy in amp_copies():
                copy.start()
            fetch(step, True)
            for copy in amp_copies():
                copy.wait()

        fetch(step, False)
        fetch(step + 1, True)
        total = lax.dot_general(
            left[slot], right[...], (((1,), (1,)), ((), ())), preferred_element_type=jnp.float32
        )
        at = 0
        for many in counts:
            part = part_refs[at][...]
            for index in range(1, many):
                part = jnp.where(step >= index * steps // many, part_refs[at + index][...], part)
            total = total + part.astype(jnp.float32)
            at += many
        out[...] = total.astype(out.dtype)

    def rows_of(many, index):
        within = steps // many
        return pl.BlockSpec((tile, cols), lambda i: (jnp.clip(i - index * within, 0, within - 1), 0))

    bytes_moved = 2 * count * (length * depth + cols * depth)
    bytes_moved += sum(length * cols * p.dtype.itemsize for p in parts)
    return pl.pallas_call(
        kernel,
        grid=(steps,),
        in_specs=[pl.BlockSpec(memory_space=pl.ANY)] * (count * pieces + count)
        + [rows_of(many, index) for many in counts for index in range(many)],
        out_specs=pl.BlockSpec((tile, cols), lambda i: (i, 0)),
        out_shape=jax.ShapeDtypeStruct((length, cols), out_dtype),
        scratch_shapes=[
            pltpu.VMEM((2, tile, count * depth), jnp.bfloat16),
            pltpu.VMEM((cols, count * depth), jnp.bfloat16),
            pltpu.SemaphoreType.DMA((2, count)),
            pltpu.SemaphoreType.DMA((count,)),
        ],
        compiler_params=pltpu.CompilerParams(vmem_limit_bytes=VMEM),
        cost_estimate=pl.CostEstimate(
            flops=2 * length * depth * cols * count,
            bytes_accessed=bytes_moved + length * cols * jnp.dtype(out_dtype).itemsize,
            transcendentals=0,
        ),
    )(*[p for t in terms for p in t[0].pieces], *[t[1] for t in terms], *parts)


def paired_plan(three_index, orbital_map, occ_energy, vir_energy, pair_kept):
    blocks = lax.axis_size("wide")
    routes = Routes(blocks)
    here = lax.axis_index("wide")
    side = lax.axis_index("narrow")
    aux, vir_count = three_index.shape[1:]
    piece_rows = aux // PIECES
    lead = jnp.asarray(np.array(routes.lead))[here]

    def moved(slab, pairs):
        sent = [lax.ppermute(p, "wide", pairs) for p in slab.pieces]
        return Slab(sent, routes.moved(slab.ids, pairs), slab.far)

    def swapped(slab):
        return moved(slab, routes.swap)

    def chosen(slab_lead, slab_other):
        pairs = zip(slab_lead.pieces, slab_other.pieces)
        return Slab(
            [jnp.where(lead, a, b) for a, b in pairs],
            routes.either(slab_lead.ids, slab_other.ids),
            slab_lead.far,
        )

    def sibling(array):
        return lax.ppermute(array, "narrow", [(0, 1), (1, 0)])

    def after(slab, other):
        pairs = zip(slab.pieces, other.pieces)
        return Slab([lax.optimization_barrier(pair)[0] for pair in pairs], slab.ids, slab.far)

    whole = three_index[0]
    own = Slab([whole[i * piece_rows : (i + 1) * piece_rows] for i in range(PIECES)], list(range(blocks)))
    r1 = moved(own, routes.rounds[0])
    own_far = Slab([sibling(p) for p in own.pieces], own.ids, True)
    mate = swapped(own)
    ahead = [passed_along(pair_kept[r].astype(jnp.float32), "wide", -r) for r in range(1, ROUNDS + 1)]
    r2 = moved(chosen(r1, own), routes.rounds[1])
    s1, s2 = swapped(r1), swapped(r2)
    mate_far = swapped(own_far)

    labels = jnp.arange(occ_energy.shape[0], dtype=jnp.int32)
    picked = orbital_map[:, None] == labels[None, :]
    energy = jnp.sum(jnp.where(picked, occ_energy[None, :], 0.0), axis=1)
    kept = jnp.concatenate([pair_kept[:, 0].astype(jnp.float32), *ahead])

    def table_of(slabs):
        ids = np.array([s.ids for s in slabs], np.int32).T
        back = (np.arange(blocks)[:, None] - ids) % blocks
        forth = (ids - np.arange(blocks)[:, None]) % blocks
        which = np.where(back <= ROUNDS, back, ROUNDS + forth)
        block, which = jnp.asarray(np.stack([ids, which]))[:, here]
        places = jnp.arange(blocks, dtype=jnp.int32)
        mine = jnp.sum(jnp.where(places == here, energy, 0.0))
        theirs = jnp.sum(jnp.where(block[:, None] == places[None, :], energy[None, :], 0.0), axis=1)
        spots = jnp.arange(kept.shape[0], dtype=jnp.int32)
        weight = jnp.sum(jnp.where(which[:, None] == spots[None, :], kept[None, :], 0.0), axis=1)
        return jnp.stack([mine + theirs, weight], axis=1)

    vir_near = lax.dynamic_slice_in_dim(vir_energy, side * vir_count, vir_count)
    vir_far = lax.dynamic_slice_in_dim(vir_energy, (1 - side) * vir_count, vir_count)
    vir_rows = jnp.concatenate([vir_near, vir_far])[:, None]
    turned = jnp.concatenate([whole, jnp.concatenate(own_far.pieces)], axis=1).T
    turned_near = whole.T

    def amps(table, base, slabs, both):
        cols = jnp.stack([vir_far if s.far else vir_near for s in slabs])[:, None, :]
        if both:
            return amplitude_call(table, base, slabs, turned, vir_rows, cols)
        return amplitude_call(table, base, slabs, turned_near, vir_near[:, None], cols)

    def terms(slabs, stack, block):
        return [(s, stack, place, block) for place, s in enumerate(slabs)]

    near, far = 0, 1
    r3 = moved(chosen(mate, r2), routes.rounds[2])
    r4_sent = chosen(r3, s2)
    home = [own, own_far, mate, mate_far]
    first = [r1, s1, r2, s2]
    r5_ids = routes.moved(routes.either(own.ids, mate.ids), routes.rounds[4])
    late_ids = [r5_ids, routes.moved(r5_ids, routes.swap)]
    s3 = swapped(r3)
    r4 = moved(r4_sent, routes.rounds[3])
    s4 = swapped(r4)
    second = [r3, s3]
    third = [s4]
    late = [Slab([], ids) for ids in late_ids * 2]
    table = table_of(home + first + second + third + late)
    at = 0
    home_amps = amps(table, at, home, False)
    at += len(home)
    first_amps = amps(table, at, first, True)
    at += len(first)

    half = aux // 2
    out_parts = [
        density_call(terms(first, first_amps, far), [], jnp.float32, (begin, half))
        for begin in range(0, aux, half)
    ]
    near_part = density_call(
        terms(home, home_amps, near) + terms(first, first_amps, near), [], jnp.float32
    )
    second_amps = amps(table, at, second, True)
    at += len(second)

    r5 = moved(after(chosen(own, mate), r4), routes.rounds[4])
    s5 = swapped(r5)
    third_amps = amps(table, at, after_all(third, near_part, second_amps), True)
    at += len(third)
    outgoing = terms(second, second_amps, far) + terms(third, third_amps, far)
    incoming = [
        sibling(density_call(outgoing, [[part]], jnp.bfloat16, (index * half, half)))
        for index, part in enumerate(out_parts)
    ]
    r6 = moved(after(chosen(own_far, mate_far), r5), routes.rounds[4])
    s6 = swapped(r6)
    near_part = density_call(
        terms(second, second_amps, near) + terms(third, third_amps, near), [[near_part]], jnp.float32
    )
    fourth = [r5, s5]
    fourth_amps = amps(table, at, fourth, False)
    at += len(fourth)
    near_part = density_call(terms(fourth, fourth_amps, near), [[near_part]], jnp.float32)

    fifth = [r6, s6]
    fifth_amps = amps(table, at, after_all(fifth, near_part), False)
    density = density_call(
        terms(fifth, fifth_amps, near), [[near_part], incoming], jnp.float32
    )
    return density[None]


def after_all(slabs, *others):
    pieces = [p for s in slabs for p in s.pieces]
    pieces = lax.optimization_barrier((*pieces, *others))[: len(pieces)]
    out = []
    for slab in slabs:
        count = len(slab.pieces)
        out.append(Slab(pieces[:count], slab.ids, slab.far))
        pieces = pieces[count:]
    return out


def solution(mesh):
    wide, narrow = mesh.shape["wide"], mesh.shape["narrow"]
    paired = narrow == 2 and wide % 4 == 0 and wide > 2 * ROUNDS + 1 and ROUNDS == 5

    def per_device(three_index, *rest):
        if paired and three_index.shape[0] == 1:
            return paired_plan(three_index, *rest)
        return ring_plan(three_index, *rest)

    placed = (P("wide", None, "narrow"), P(), P(), P(), P(None, "wide"))
    return jax.shard_map(
        per_device, mesh=mesh, in_specs=placed, out_specs=P("wide", None, "narrow"), check_vma=False
    )
```

```python
import jax
import jax.numpy as jnp
import numpy as np
from jax import lax
from jax.experimental import pallas as pl
from jax.experimental.pallas import tpu as pltpu
from jax.sharding import PartitionSpec as P

ROUNDS = 5
TAIL = 16
CHUNKS = 8
VMEM = 56 * 1024 * 1024


def passed_along(array, axis, by):
    length = lax.axis_size(axis)
    return lax.ppermute(array, axis, [(i, (i + by) % length) for i in range(length)])


def block_energy(orbital_map, occ_energy, block_id, occ_count):
    orbits = lax.dynamic_slice_in_dim(orbital_map, block_id * occ_count, occ_count)
    labels = jnp.arange(occ_energy.shape[0], dtype=jnp.int32)
    chosen = orbits[:, None] == labels[None, :]
    return jnp.sum(jnp.where(chosen, occ_energy[None, :], 0.0), axis=1)


def amplitudes(gathered, visiting, left_energy, right_energy, vir_all, vir_local, weight):
    coulomb = jnp.einsum("ipa,jpb->ijab", gathered, visiting, preferred_element_type=jnp.float32)
    denominator = (vir_all[:, None] + vir_local[None, :])[None, None] - (
        left_energy[:, None] + right_energy[None, :]
    )[:, :, None, None]
    return (weight * coulomb / denominator).astype(jnp.bfloat16)


def ring_plan(three_index, orbital_map, occ_energy, vir_energy, pair_kept):
    occ_count = three_index.shape[0]
    vir_count = three_index.shape[2]
    blocks = lax.axis_size("wide")
    own_block = lax.axis_index("wide")
    vir_local = lax.dynamic_slice_in_dim(
        vir_energy, lax.axis_index("narrow") * vir_count, vir_count
    )
    own_energy = block_energy(orbital_map, occ_energy, own_block, occ_count)
    weights = pair_kept.astype(jnp.float32)
    gathered = lax.all_gather(three_index, "narrow", axis=2, tiled=True)
    amplitude = amplitudes(
        gathered, three_index, own_energy, own_energy, vir_energy, vir_local, weights[0, 0]
    )
    forward = jnp.einsum(
        "ijab,jpb->ipa", amplitude, three_index, preferred_element_type=jnp.float32
    )
    visiting = three_index
    stored_amps = []
    for round_index in range(1, ROUNDS + 1):
        visiting = passed_along(visiting, "wide", 1)
        partner = (own_block - round_index) % blocks
        partner_energy = block_energy(orbital_map, occ_energy, partner, occ_count)
        amplitude = amplitudes(
            gathered,
            visiting,
            own_energy,
            partner_energy,
            vir_energy,
            vir_local,
            weights[round_index, 0],
        )
        forward = forward + jnp.einsum(
            "ijab,jpb->ipa", amplitude, visiting, preferred_element_type=jnp.float32
        )
        stored_amps.append(amplitude)
    carried = None
    for round_index in range(1, ROUNDS + 1):
        backward = jnp.einsum(
            "ijab,ipa->jpb",
            stored_amps[round_index - 1],
            gathered,
            preferred_element_type=jnp.float32,
        )
        if round_index > 1:
            carried = passed_along(carried, "wide", 1) + backward
        else:
            carried = backward
    returned = passed_along(carried, "wide", -ROUNDS)
    scattered = lax.psum_scatter(forward, "narrow", scatter_dimension=2, tiled=True)
    return scattered + returned


class Routes:
    def __init__(self, blocks):
        self.blocks = blocks
        everyone = range(blocks)
        self.lead = [self.place(w)[1] == self.place(w)[2] for w in everyone]
        self.swap = [(w, w ^ 1) for w in everyone]
        onward = [(w, self.along_z(w, 1)) for w in everyone]
        backward = [(w, self.along_z(w, -1)) for w in everyone]
        across = [(w, self.across_x(w)) for w in everyone]
        self.rounds = [
            self.either(across, onward),
            self.either(onward, across),
            self.either(across, backward),
            self.either(backward, across),
            self.either(backward, across),
        ]

    def place(self, w):
        return w // 4, (w // 2) % 2, w % 2

    def along_z(self, w, step):
        z, x, core = self.place(w)
        z = (z + (step if x == 1 else -step)) % (self.blocks // 4)
        return (z * 2 + x) * 2 + core

    def across_x(self, w):
        z, x, core = self.place(w)
        return (z * 2 + 1 - x) * 2 + 1 - core

    def either(self, of_lead, of_other):
        return [a if lead else b for lead, a, b in zip(self.lead, of_lead, of_other)]

    def moved(self, ids, pairs):
        out = [0] * self.blocks
        for source, target in pairs:
            out[target] = ids[source]
        return out


class Slab:
    def __init__(self, array, ids, far=0):
        self.pieces = list(array) if isinstance(array, (list, tuple)) else [array]
        self.array = self.pieces[0]
        self.ids = ids
        self.far = far


def pick(step, values):
    out = values[0]
    for index, value in enumerate(values):
        if index and value != values[0]:
            out = jnp.where(step == index, value, out)
    return out


def amplitude_call(jobs, table, lines, turned, vir_rows, vir_cols, earlier):
    slabs = []
    for slab, _ in jobs:
        if slab not in slabs:
            slabs.append(slab)
    count, blocks = len(slabs), len(turned)
    cols, aux = turned[0].shape
    held_rows = aux + TAIL
    pieces = [len(slab.pieces) for slab in slabs]
    begins = [sum(pieces[:s]) for s in range(count)]
    of_job = [slabs.index(slab) for slab, _ in jobs]
    block_of = [block for _, block in jobs]
    far_of = [slab.far for slab, _ in jobs]
    line_of = [lines[slab] for slab, _ in jobs]
    opens = [t for t in range(len(jobs)) if t == 0 or of_job[t] != of_job[t - 1]]
    half = cols // 2

    def kernel(scalars, *refs):
        sources, refs = refs[: sum(pieces)], refs[sum(pieces) :]
        row_sources, refs = refs[:blocks], refs[blocks + len(earlier) :]
        vir_row, vir_col, out, held, rows, held_sems, row_sems = refs
        step = pl.program_id(0)

        def slab_copies(s):
            row = 0
            for index in range(pieces[s]):
                source = sources[begins[s] + index]
                target = held.at[s % 2, pl.ds(row, source.shape[0]), :]
                yield pltpu.make_async_copy(source, target, held_sems.at[s % 2, index])
                row += source.shape[0]

        def row_copy(block):
            return pltpu.make_async_copy(row_sources[block], rows.at[block], row_sems.at[block])

        @pl.when(step == 0)
        def _():
            for copy in slab_copies(0):
                copy.start()
            for block in dict.fromkeys(block_of):
                row_copy(block).start()

        for s, t in enumerate(opens):

            @pl.when(step == t)
            def _(s=s):
                for copy in slab_copies(s):
                    copy.wait()
                if s + 1 < count:
                    for copy in slab_copies(s + 1):
                        copy.start()

        for block in dict.fromkeys(block_of):

            @pl.when(step == block_of.index(block))
            def _(block=block):
                row_copy(block).wait()

        slot = pick(step, [s % 2 for s in of_job])
        block = pick(step, block_of)
        line = pick(step, line_of)
        plan = held[slot, aux:, :128].astype(jnp.float32)
        lane = lax.broadcasted_iota(jnp.int32, plan.shape, 1).astype(jnp.float32)
        row = lax.broadcasted_iota(jnp.int32, plan.shape, 0)
        told = jnp.where(jnp.logical_and(row == 0, lane == scalars[line, 2]), plan, 0.0)
        weight = scalars[line, 1] + jnp.sum(told, keepdims=True)
        for begin in range(0, cols, half):
            part = pl.ds(begin, half)
            coulomb = jnp.dot(rows[block], held[slot, :aux, part], preferred_element_type=jnp.float32)
            denominator = (vir_row[0] + vir_col[0, :, part]) - scalars[line, 0]
            out[0, :, part] = (weight * coulomb / denominator).astype(out.dtype)

    return pl.pallas_call(
        kernel,
        grid=(len(jobs),),
        in_specs=[pl.BlockSpec(memory_space=pltpu.SMEM)]
        + [pl.BlockSpec(memory_space=pl.ANY)] * (sum(pieces) + blocks + len(earlier))
        + [
            pl.BlockSpec((1, cols, 1), lambda t: (pick(t, block_of), 0, 0)),
            pl.BlockSpec((1, 1, cols), lambda t: (pick(t, far_of), 0, 0)),
        ],
        out_specs=pl.BlockSpec((1, cols, cols), lambda t: (t, 0, 0)),
        out_shape=jax.ShapeDtypeStruct((len(jobs), cols, cols), jnp.bfloat16),
        scratch_shapes=[
            pltpu.VMEM((2, held_rows, cols), jnp.bfloat16),
            pltpu.VMEM((blocks, cols, aux), jnp.bfloat16),
            pltpu.SemaphoreType.DMA((2, max(pieces))),
            pltpu.SemaphoreType.DMA((blocks,)),
        ],
        compiler_params=pltpu.CompilerParams(vmem_limit_bytes=VMEM),
        cost_estimate=pl.CostEstimate(
            flops=2 * len(jobs) * cols * aux * cols,
            bytes_accessed=2 * cols * (blocks * aux + count * aux + len(jobs) * cols),
            transcendentals=0,
        ),
    )(table, *[p for s in slabs for p in s.pieces], *turned, *earlier, vir_rows, vir_cols)


def in_chunks(source, target, sems):
    rows = source.shape[0]
    size = -(-rows // CHUNKS // 16) * 16
    for index in range(CHUNKS):
        begin = index * size
        part = pl.ds(begin, min(size, rows - begin))
        yield pltpu.make_async_copy(source.at[part], target.at[part], sems.at[index])


def choice_call(flag, a, b, earlier, pieces=1):
    rows = a.shape[0]
    size = rows // pieces // 512 * 512 if pieces > 1 else rows
    begins = [index * size for index in range(pieces)] + [rows]
    shapes = [(end - begin, a.shape[1]) for begin, end in zip(begins, begins[1:])]

    def kernel(flag_ref, a_ref, b_ref, *refs):
        outs, sems = refs[len(earlier) : -1], refs[-1]

        def copies(source):
            for index, out in enumerate(outs):
                part = source.at[pl.ds(begins[index], out.shape[0])]
                yield from in_chunks(part, out, sems.at[index])

        for value, source in ((1, a_ref), (0, b_ref)):

            @pl.when(flag_ref[0] == value)
            def _(source=source):
                for copy in copies(source):
                    copy.start()
                for copy in copies(source):
                    copy.wait()

    return pl.pallas_call(
        kernel,
        in_specs=[pl.BlockSpec(memory_space=pltpu.SMEM)]
        + [pl.BlockSpec(memory_space=pl.ANY)] * (2 + len(earlier)),
        out_specs=[pl.BlockSpec(memory_space=pl.ANY)] * pieces,
        out_shape=[jax.ShapeDtypeStruct(shape, a.dtype) for shape in shapes],
        scratch_shapes=[pltpu.SemaphoreType.DMA((pieces, CHUNKS))],
        cost_estimate=pl.CostEstimate(flops=0, bytes_accessed=2 * a.size * a.dtype.itemsize, transcendentals=0),
    )(flag, a, b, *earlier)


def join_call(earlier):
    def kernel(*refs):
        refs[-1][...] = jnp.zeros_like(refs[-1])

    return pl.pallas_call(
        kernel,
        in_specs=[pl.BlockSpec(memory_space=pl.ANY)] * len(earlier),
        out_specs=pl.BlockSpec(memory_space=pltpu.VMEM),
        out_shape=jax.ShapeDtypeStruct((8, 128), jnp.float32),
    )(*earlier)


def density_call(terms, parts, out_dtype, aux, earlier, rows=None, copied=None):
    count = len(terms)
    extra = [] if copied is None else [copied]
    pieces = [len(t[0].pieces) for t in terms]
    begins = [sum(pieces[:s]) for s in range(count)]
    depth = terms[0][0].array.shape[1]
    cols = depth
    begin, length = rows or (0, aux)
    tile = 512
    while length % tile or begin % tile:
        tile //= 2
    steps = length // tile
    spans = []
    for part in parts:
        ends = np.cumsum([piece.shape[0] // tile for piece in part])
        spans.append([(int(end) - piece.shape[0] // tile, int(end)) for end, piece in zip(ends, part)])
    parts = [p for part in parts for p in part]

    def kernel(*refs):
        sources, refs = refs[: sum(pieces)], refs[sum(pieces) :]
        amps, refs = refs[:count], refs[count + len(earlier) :]
        source, refs = refs[: len(extra)], refs[len(extra) :]
        part_refs, out, refs = refs[: len(parts)], refs[len(parts)], refs[len(parts) + 1 :]
        target, (left, right, left_sems, right_sems, copy_sems) = refs[: len(extra)], refs[len(extra) :]
        step = pl.program_id(0)
        slot = step % 2

        def amp_copies():
            for s, (_, _, place) in enumerate(terms):
                yield pltpu.make_async_copy(
                    amps[s].at[place], right.at[:, pl.ds(s * depth, depth)], right_sems.at[s]
                )

        def slab_copies(which, start):
            for s in range(count):
                end = 0
                for index in range(pieces[s]):
                    source = sources[begins[s] + index]
                    first = end
                    end += source.shape[0] // tile

                    def act(source=source, first=first, s=s):
                        row = pl.multiple_of((begin // tile + which - first) * tile, tile)
                        copy = pltpu.make_async_copy(
                            source.at[pl.ds(row, tile), :],
                            left.at[which % 2, :, pl.ds(s * depth, depth)],
                            left_sems.at[which % 2, s],
                        )
                        copy.start() if start else copy.wait()

                    at = begin // tile + which
                    if pieces[s] == 1:
                        act()
                    else:
                        pl.when(jnp.logical_and(at >= first, at < end))(act)

        @pl.when(step == 0)
        def _():
            for copy in amp_copies():
                copy.start()
            slab_copies(step, True)
            for pair in zip(source, target):
                for copy in in_chunks(*pair, copy_sems):
                    copy.start()

        @pl.when(step + 1 < steps)
        def _():
            slab_copies(step + 1, True)

        @pl.when(step == 0)
        def _():
            for copy in amp_copies():
                copy.wait()

        slab_copies(step, False)
        total = lax.dot_general(
            left[slot], right[...], (((1,), (1,)), ((), ())), preferred_element_type=jnp.float32
        )
        at = 0
        for span in spans:
            part = part_refs[at][...]
            for index in range(1, len(span)):
                part = jnp.where(step >= span[index][0], part_refs[at + index][...], part)
            total = total + part.astype(jnp.float32)
            at += len(span)
        out[...] = total.astype(out.dtype)

        @pl.when(step == steps - 1)
        def _():
            for pair in zip(source, target):
                for copy in in_chunks(*pair, copy_sems):
                    copy.wait()

    def rows_of(start, end):
        return pl.BlockSpec((tile, cols), lambda i: (jnp.clip(i - start, 0, end - start - 1), 0))

    bytes_moved = 2 * count * (length * depth + cols * depth)
    bytes_moved += sum(length * cols * p.dtype.itemsize for p in parts)
    return pl.pallas_call(
        kernel,
        grid=(steps,),
        in_specs=[pl.BlockSpec(memory_space=pl.ANY)] * (sum(pieces) + count + len(earlier) + len(extra))
        + [rows_of(*ends) for span in spans for ends in span],
        out_specs=[pl.BlockSpec((tile, cols), lambda i: (i, 0))]
        + [pl.BlockSpec(memory_space=pl.ANY)] * len(extra),
        out_shape=[jax.ShapeDtypeStruct((length, cols), out_dtype)]
        + [jax.ShapeDtypeStruct(x.shape, x.dtype) for x in extra],
        scratch_shapes=[
            pltpu.VMEM((2, tile, count * depth), jnp.bfloat16),
            pltpu.VMEM((cols, count * depth), jnp.bfloat16),
            pltpu.SemaphoreType.DMA((2, count)),
            pltpu.SemaphoreType.DMA((count,)),
            pltpu.SemaphoreType.DMA((CHUNKS,)),
        ],
        compiler_params=pltpu.CompilerParams(vmem_limit_bytes=VMEM),
        cost_estimate=pl.CostEstimate(
            flops=2 * length * depth * cols * count,
            bytes_accessed=(bytes_moved + length * cols * jnp.dtype(out_dtype).itemsize),
            transcendentals=0,
        ),
    )(*[p for t in terms for p in t[0].pieces], *[t[1] for t in terms], *earlier, *extra, *parts)


def paired_plan(three_index, orbital_map, occ_energy, vir_energy, pair_kept):
    blocks = lax.axis_size("wide")
    routes = Routes(blocks)
    here = lax.axis_index("wide")
    side = lax.axis_index("narrow")
    aux, vir_count = three_index.shape[1:]

    def moved(slab, pairs):
        sent = [lax.ppermute(piece, "wide", pairs) for piece in slab.pieces]
        return Slab(sent, routes.moved(slab.ids, pairs), slab.far)

    def swapped(slab):
        return moved(slab, routes.swap)

    flag = jnp.asarray(np.array(routes.lead, np.int32))[here].reshape(1)

    def chosen(of_lead, of_other, *earlier, pieces=1):
        return Slab(
            choice_call(flag, of_lead.array, of_other.array, earlier, pieces),
            routes.either(of_lead.ids, of_other.ids),
            of_lead.far,
        )

    def sibling(array):
        return lax.ppermute(array, "narrow", [(0, 1), (1, 0)])

    plan = jnp.zeros((TAIL, vir_count), jnp.bfloat16)
    plan = plan.at[0, : ROUNDS + 1].set(pair_kept[:, 0].astype(jnp.bfloat16))
    own = Slab(jnp.concatenate([three_index[0], plan]), list(range(blocks)))

    r1 = moved(own, routes.rounds[0])
    own_far = Slab(sibling(own.array), own.ids, 1)
    mate = swapped(own)
    s1 = swapped(r1)
    sent2 = chosen(own, r1, mate.array)
    r2 = moved(sent2, routes.rounds[1])

    labels = jnp.arange(occ_energy.shape[0], dtype=jnp.int32)
    picked = orbital_map[:, None] == labels[None, :]
    energy = jnp.sum(jnp.where(picked, occ_energy[None, :], 0.0), axis=1)

    def table_of(ids):
        ids = np.array(ids, np.int32).T
        places = np.arange(blocks)[:, None]
        back, forth = (places - ids) % blocks, (ids - places) % blocks
        behind = back <= ROUNDS
        known = np.stack([ids, np.where(behind, back, -1), np.where(behind, -1, forth)])
        block, mine, theirs = jnp.asarray(known.astype(np.int32))[:, here]
        places = jnp.arange(blocks, dtype=jnp.int32)[None, :]
        both = jnp.where(places == here, energy[None, :], 0.0)
        both = both + jnp.where(places == block[:, None], energy[None, :], 0.0)
        entries = jnp.arange(ROUNDS + 1, dtype=jnp.int32)[None, :]
        kept = pair_kept[:, 0].astype(jnp.float32)[None, :]
        weight = jnp.sum(jnp.where(entries == mine[:, None], kept, 0.0), axis=1)
        return jnp.stack([jnp.sum(both, axis=1), weight, theirs.astype(jnp.float32)], axis=1)

    vir = jnp.stack(
        [lax.dynamic_slice_in_dim(vir_energy, s * vir_count, vir_count) for s in (side, 1 - side)]
    )
    vir_rows, vir_cols = vir[:, :, None], vir[:, None, :]

    r3_ids = routes.moved(routes.either(r2.ids, own.ids), routes.rounds[2])
    r4_ids = routes.moved(r3_ids, routes.rounds[3])
    r5_ids = routes.moved(own.ids, routes.rounds[4])
    all_ids = [own.ids, mate.ids, r1.ids, s1.ids, r2.ids, routes.moved(r2.ids, routes.swap)]
    all_ids += [r3_ids, routes.moved(r3_ids, routes.swap), r4_ids, r5_ids, routes.moved(r5_ids, routes.swap)]
    table = table_of(all_ids)
    near, far = 0, 1
    rows_near = three_index[0].T
    stacks = {}

    def amps(jobs, turned, *earlier):
        lines = {slab: all_ids.index(slab.ids) for slab, _ in jobs}
        stack = amplitude_call(jobs, table, lines, turned, vir_rows, vir_cols, earlier)
        for place, job in enumerate(jobs):
            stacks[job] = (stack, place)
        return stack

    def density(slabs, block, parts, dtype, *earlier, rows=None, copied=None):
        terms = [(slab, *stacks[slab, block]) for slab in slabs]
        out, *copy = density_call(terms, parts, dtype, aux, earlier, rows, copied)
        return (out, *copy) if copy else out

    f32, bf16 = jnp.float32, jnp.bfloat16
    done = amps([(s, near) for s in (own, mate, r1, s1)], [rows_near], sent2.array)
    mate_far = swapped(own_far)

    sent3 = chosen(r2, own, done)
    r3 = moved(sent3, routes.rounds[2])
    s2 = swapped(r2)
    rows_far = own_far.array[:aux].T
    part = density([own, mate, r1, s1], near, [], f32, sent3.array)
    jobs = [(r1, far), (s1, far), (r2, near), (r2, far), (s2, far), (s2, near)]
    jobs += [(own_far, near), (mate_far, near)]
    done = amps(jobs, [rows_near, rows_far], part)

    r3 = chosen(r3, r3, done)
    r4 = moved(r3, routes.rounds[3])
    s3 = swapped(r3)
    jobs = [(r3, near), (r3, far), (s3, far), (s3, near)]
    done = amps(jobs, [rows_near, rows_far], done)
    slabs = [own_far, mate_far, r2, s2, r3, s3]
    part, again = density(slabs, near, [[part]], f32, done, copied=own.array)
    r5 = moved(Slab(again, own.ids), routes.rounds[4])

    done = amps([(r4, far)], [rows_near, rows_far], part)
    slabs = [r1, s1, r2, s2, r3, s3, r4]
    half = aux // 2
    sent0, again = density(slabs, far, [], bf16, done, rows=(0, half), copied=own_far.array)
    sent1 = density(slabs, far, [], bf16, sent0, rows=(half, half))
    r6 = moved(Slab(again, own.ids, 1), routes.rounds[4])
    incoming = [sibling(sent0), sibling(sent1)]
    done = amps([(r4, near)], [rows_near], sent1)

    r5 = chosen(r5, r5, done, pieces=3)
    s5 = swapped(r5)
    done = amps([(r5, near)], [rows_near], r5.array)
    done = join_call([incoming[0], done])
    done = amps([(s5, near)], [rows_near], done)
    part = density([r4, r5, s5], near, [[part]], f32, done)
    r6 = chosen(r6, r6, part, pieces=3)
    s6 = swapped(r6)
    done = amps([(r6, near)], [rows_near], r6.array)
    done = join_call([incoming[1], done])
    done = amps([(s6, near)], [rows_near], done)
    return density([r6, s6], near, [[part], incoming], f32, done)[None]


def solution(mesh):
    wide, narrow = mesh.shape["wide"], mesh.shape["narrow"]
    paired = narrow == 2 and wide % 4 == 0 and wide > 2 * ROUNDS + 1 and ROUNDS == 5

    def per_device(three_index, *rest):
        if paired and three_index.shape[0] == 1:
            return paired_plan(three_index, *rest)
        return ring_plan(three_index, *rest)

    placed = (P("wide", None, "narrow"), P(), P(), P(), P(None, "wide"))
    return jax.shard_map(
        per_device, mesh=mesh, in_specs=placed, out_specs=P("wide", None, "narrow"), check_vma=False
    )
```

```python
import jax
import jax.numpy as jnp
import numpy as np
from jax import lax
from jax.experimental import pallas as pl
from jax.experimental.pallas import tpu as pltpu
from jax.sharding import PartitionSpec as P

ROUNDS = 5
TAIL = 16
CHUNK = 512
VMEM = 56 * 1024 * 1024


def passed_along(array, axis, by):
    length = lax.axis_size(axis)
    return lax.ppermute(array, axis, [(i, (i + by) % length) for i in range(length)])


def block_energy(orbital_map, occ_energy, block_id, occ_count):
    orbits = lax.dynamic_slice_in_dim(orbital_map, block_id * occ_count, occ_count)
    labels = jnp.arange(occ_energy.shape[0], dtype=jnp.int32)
    chosen = orbits[:, None] == labels[None, :]
    return jnp.sum(jnp.where(chosen, occ_energy[None, :], 0.0), axis=1)


def amplitudes(gathered, visiting, left_energy, right_energy, vir_all, vir_local, weight):
    coulomb = jnp.einsum("ipa,jpb->ijab", gathered, visiting, preferred_element_type=jnp.float32)
    denominator = (vir_all[:, None] + vir_local[None, :])[None, None] - (
        left_energy[:, None] + right_energy[None, :]
    )[:, :, None, None]
    return (weight * coulomb / denominator).astype(jnp.bfloat16)


def ring_plan(three_index, orbital_map, occ_energy, vir_energy, pair_kept):
    occ_count = three_index.shape[0]
    vir_count = three_index.shape[2]
    blocks = lax.axis_size("wide")
    own_block = lax.axis_index("wide")
    vir_local = lax.dynamic_slice_in_dim(
        vir_energy, lax.axis_index("narrow") * vir_count, vir_count
    )
    own_energy = block_energy(orbital_map, occ_energy, own_block, occ_count)
    weights = pair_kept.astype(jnp.float32)
    gathered = lax.all_gather(three_index, "narrow", axis=2, tiled=True)
    amplitude = amplitudes(
        gathered, three_index, own_energy, own_energy, vir_energy, vir_local, weights[0, 0]
    )
    forward = jnp.einsum(
        "ijab,jpb->ipa", amplitude, three_index, preferred_element_type=jnp.float32
    )
    visiting = three_index
    stored_amps = []
    for round_index in range(1, ROUNDS + 1):
        visiting = passed_along(visiting, "wide", 1)
        partner = (own_block - round_index) % blocks
        partner_energy = block_energy(orbital_map, occ_energy, partner, occ_count)
        amplitude = amplitudes(
            gathered,
            visiting,
            own_energy,
            partner_energy,
            vir_energy,
            vir_local,
            weights[round_index, 0],
        )
        forward = forward + jnp.einsum(
            "ijab,jpb->ipa", amplitude, visiting, preferred_element_type=jnp.float32
        )
        stored_amps.append(amplitude)
    carried = None
    for round_index in range(1, ROUNDS + 1):
        backward = jnp.einsum(
            "ijab,ipa->jpb",
            stored_amps[round_index - 1],
            gathered,
            preferred_element_type=jnp.float32,
        )
        if round_index > 1:
            carried = passed_along(carried, "wide", 1) + backward
        else:
            carried = backward
    returned = passed_along(carried, "wide", -ROUNDS)
    scattered = lax.psum_scatter(forward, "narrow", scatter_dimension=2, tiled=True)
    return scattered + returned


class Routes:
    def __init__(self, blocks):
        self.blocks = blocks
        everyone = range(blocks)
        self.lead = [self.place(w)[1] == self.place(w)[2] for w in everyone]
        self.swap = [(w, w ^ 1) for w in everyone]
        onward = [(w, self.along_z(w, 1)) for w in everyone]
        backward = [(w, self.along_z(w, -1)) for w in everyone]
        across = [(w, self.across_x(w)) for w in everyone]
        self.rounds = [
            self.either(across, onward),
            self.either(onward, across),
            self.either(across, backward),
            self.either(backward, across),
            self.either(backward, across),
        ]

    def place(self, w):
        return w // 4, (w // 2) % 2, w % 2

    def along_z(self, w, step):
        z, x, core = self.place(w)
        z = (z + (step if x == 1 else -step)) % (self.blocks // 4)
        return (z * 2 + x) * 2 + core

    def across_x(self, w):
        z, x, core = self.place(w)
        return (z * 2 + 1 - x) * 2 + 1 - core

    def either(self, of_lead, of_other):
        return [a if lead else b for lead, a, b in zip(self.lead, of_lead, of_other)]

    def moved(self, ids, pairs):
        out = [0] * self.blocks
        for source, target in pairs:
            out[target] = ids[source]
        return out


class Slab:
    def __init__(self, array, ids, far=0):
        self.pieces = list(array) if isinstance(array, (list, tuple)) else [array]
        self.array = self.pieces[0]
        self.ids = ids
        self.far = far


def pick(step, values):
    out = values[0]
    for index, value in enumerate(values):
        if index and value != values[0]:
            out = jnp.where(step == index, value, out)
    return out


def amplitude_call(jobs, table, lines, turned, vir_rows, vir_cols, earlier):
    slabs = []
    for slab, _ in jobs:
        if slab not in slabs:
            slabs.append(slab)
    count, blocks = len(slabs), len(turned)
    cols, aux = turned[0].shape
    held_rows = aux + TAIL
    pieces = [len(slab.pieces) for slab in slabs]
    begins = [sum(pieces[:s]) for s in range(count)]
    of_job = [slabs.index(slab) for slab, _ in jobs]
    block_of = [block for _, block in jobs]
    far_of = [slab.far for slab, _ in jobs]
    line_of = [lines[slab] for slab, _ in jobs]
    opens = [t for t in range(len(jobs)) if t == 0 or of_job[t] != of_job[t - 1]]
    half = cols // 2

    def kernel(scalars, *refs):
        sources, refs = refs[: sum(pieces)], refs[sum(pieces) :]
        row_sources, refs = refs[:blocks], refs[blocks + len(earlier) :]
        vir_row, vir_col, out, held, rows, held_sems, row_sems = refs
        step = pl.program_id(0)

        def slab_copies(s):
            row = 0
            for index in range(pieces[s]):
                source = sources[begins[s] + index]
                target = held.at[s % 2, pl.ds(row, source.shape[0]), :]
                yield pltpu.make_async_copy(source, target, held_sems.at[s % 2, index])
                row += source.shape[0]

        def row_copy(block):
            return pltpu.make_async_copy(row_sources[block], rows.at[block], row_sems.at[block])

        @pl.when(step == 0)
        def _():
            for copy in slab_copies(0):
                copy.start()
            for block in dict.fromkeys(block_of):
                row_copy(block).start()

        for s, t in enumerate(opens):

            @pl.when(step == t)
            def _(s=s):
                for copy in slab_copies(s):
                    copy.wait()
                if s + 1 < count:
                    for copy in slab_copies(s + 1):
                        copy.start()

        for block in dict.fromkeys(block_of):

            @pl.when(step == block_of.index(block))
            def _(block=block):
                row_copy(block).wait()

        slot = pick(step, [s % 2 for s in of_job])
        block = pick(step, block_of)
        line = pick(step, line_of)
        plan = held[slot, aux:, :128].astype(jnp.float32)
        lane = lax.broadcasted_iota(jnp.int32, plan.shape, 1).astype(jnp.float32)
        row = lax.broadcasted_iota(jnp.int32, plan.shape, 0)
        told = jnp.where(jnp.logical_and(row == 0, lane == scalars[line, 2]), plan, 0.0)
        weight = scalars[line, 1] + jnp.sum(told, keepdims=True)
        for begin in range(0, cols, half):
            part = pl.ds(begin, half)
            coulomb = jnp.dot(rows[block], held[slot, :aux, part], preferred_element_type=jnp.float32)
            denominator = (vir_row[0] + vir_col[0, :, part]) - scalars[line, 0]
            out[0, :, part] = (weight * coulomb / denominator).astype(out.dtype)

    return pl.pallas_call(
        kernel,
        grid=(len(jobs),),
        in_specs=[pl.BlockSpec(memory_space=pltpu.SMEM)]
        + [pl.BlockSpec(memory_space=pl.ANY)] * (sum(pieces) + blocks + len(earlier))
        + [
            pl.BlockSpec((1, cols, 1), lambda t: (pick(t, block_of), 0, 0)),
            pl.BlockSpec((1, 1, cols), lambda t: (pick(t, far_of), 0, 0)),
        ],
        out_specs=pl.BlockSpec((1, cols, cols), lambda t: (t, 0, 0)),
        out_shape=jax.ShapeDtypeStruct((len(jobs), cols, cols), jnp.bfloat16),
        scratch_shapes=[
            pltpu.VMEM((2, held_rows, cols), jnp.bfloat16),
            pltpu.VMEM((blocks, cols, aux), jnp.bfloat16),
            pltpu.SemaphoreType.DMA((2, max(pieces))),
            pltpu.SemaphoreType.DMA((blocks,)),
        ],
        compiler_params=pltpu.CompilerParams(vmem_limit_bytes=VMEM),
        cost_estimate=pl.CostEstimate(
            flops=2 * len(jobs) * cols * aux * cols,
            bytes_accessed=2 * cols * (blocks * aux + count * aux + len(jobs) * cols),
            transcendentals=0,
        ),
    )(table, *[p for s in slabs for p in s.pieces], *turned, *earlier, vir_rows, vir_cols)


def chunks_of(rows):
    return [(begin, min(CHUNK, rows - begin)) for begin in range(0, rows, CHUNK)]


def copies_in(sources, held, sems):
    row, index = 0, 0
    for source in sources:
        for begin, size in chunks_of(source.shape[0]):
            yield pltpu.make_async_copy(
                source.at[pl.ds(begin, size)], held.at[pl.ds(row + begin, size)], sems.at[index]
            )
            index += 1
        row += source.shape[0]


def copies_out(held, targets, sems):
    row, index = 0, 0
    for target in targets:
        for begin, size in chunks_of(target.shape[0]):
            yield pltpu.make_async_copy(
                held.at[pl.ds(row + begin, size)], target.at[pl.ds(begin, size)], sems.at[index]
            )
            index += 1
        row += target.shape[0]


def copy_scratch(rows, cols):
    count = len(chunks_of(rows)) + 1
    return [
        pltpu.VMEM((rows, cols), jnp.bfloat16),
        pltpu.SemaphoreType.DMA((count,)),
        pltpu.SemaphoreType.DMA((count,)),
    ]


def copy_through(sources, targets, held, in_sems, out_sems):
    for copy in copies_in(sources, held, in_sems):
        copy.start()
    for copy in copies_in(sources, held, in_sems):
        copy.wait()
    for copy in copies_out(held, targets, out_sems):
        copy.start()
    for copy in copies_out(held, targets, out_sems):
        copy.wait()


def append_call(array, tail):
    def kernel(array_ref, tail_ref, out, held, in_sems, out_sems):
        copy_through([array_ref, tail_ref], [out], held, in_sems, out_sems)

    rows, cols = array.shape[0] + tail.shape[0], array.shape[1]
    return pl.pallas_call(
        kernel,
        in_specs=[pl.BlockSpec(memory_space=pl.ANY)] * 2,
        out_specs=pl.BlockSpec(memory_space=pl.ANY),
        out_shape=jax.ShapeDtypeStruct((rows, cols), array.dtype),
        scratch_shapes=copy_scratch(rows, cols),
        compiler_params=pltpu.CompilerParams(vmem_limit_bytes=VMEM),
    )(array, tail)


def choice_call(flag, a, b, earlier, pieces=1, keep=False):
    rows, cols = a.shape
    size = rows // pieces // CHUNK * CHUNK if pieces > 1 else rows
    begins = [index * size for index in range(pieces)] + [rows]
    shapes = [(end - begin, cols) for begin, end in zip(begins, begins[1:])]
    kept = [(rows, cols)] if keep else []

    def kernel(flag_ref, a_ref, b_ref, *refs):
        outs, kept_outs = refs[len(earlier) :][:pieces], refs[len(earlier) + pieces : -3]
        scratch = refs[-3:]
        if keep:
            copy_through([a_ref], kept_outs, *scratch)
        for value, source in ((1, a_ref), (0, b_ref)):

            @pl.when(flag_ref[0] == value)
            def _(source=source):
                copy_through([source], outs, *scratch)

    return pl.pallas_call(
        kernel,
        in_specs=[pl.BlockSpec(memory_space=pltpu.SMEM)]
        + [pl.BlockSpec(memory_space=pl.ANY)] * (2 + len(earlier)),
        out_specs=[pl.BlockSpec(memory_space=pl.ANY)] * (pieces + len(kept)),
        out_shape=[jax.ShapeDtypeStruct(shape, a.dtype) for shape in shapes + kept],
        scratch_shapes=copy_scratch(rows, cols),
        compiler_params=pltpu.CompilerParams(vmem_limit_bytes=VMEM),
        cost_estimate=pl.CostEstimate(flops=0, bytes_accessed=2 * a.size * a.dtype.itemsize, transcendentals=0),
    )(flag, a, b, *earlier)


def join_call(earlier):
    def kernel(*refs):
        refs[-1][...] = jnp.zeros_like(refs[-1])

    return pl.pallas_call(
        kernel,
        in_specs=[pl.BlockSpec(memory_space=pl.ANY)] * len(earlier),
        out_specs=pl.BlockSpec(memory_space=pltpu.VMEM),
        out_shape=jax.ShapeDtypeStruct((8, 128), jnp.float32),
    )(*earlier)


def density_call(terms, parts, out_dtype, aux, earlier, rows=None, copied=None):
    count = len(terms)
    extra = [] if copied is None else [copied]
    pieces = [len(t[0].pieces) for t in terms]
    begins = [sum(pieces[:s]) for s in range(count)]
    depth = terms[0][0].array.shape[1]
    cols = depth
    begin, length = rows or (0, aux)
    tile = 512
    while length % tile or begin % tile:
        tile //= 2
    steps = length // tile
    spans = []
    for part in parts:
        ends = np.cumsum([piece.shape[0] // tile for piece in part])
        spans.append([(int(end) - piece.shape[0] // tile, int(end)) for end, piece in zip(ends, part)])
    parts = [p for part in parts for p in part]

    def kernel(*refs):
        sources, refs = refs[: sum(pieces)], refs[sum(pieces) :]
        amps, refs = refs[:count], refs[count + len(earlier) :]
        source, refs = refs[: len(extra)], refs[len(extra) :]
        part_refs, out, refs = refs[: len(parts)], refs[len(parts)], refs[len(parts) + 1 :]
        target, refs = refs[: len(extra)], refs[len(extra) :]
        (left, right, left_sems, right_sems), scratch = refs[:4], refs[4:]
        step = pl.program_id(0)
        slot = step % 2

        def amp_copies():
            for s, (_, _, place) in enumerate(terms):
                yield pltpu.make_async_copy(
                    amps[s].at[place], right.at[:, pl.ds(s * depth, depth)], right_sems.at[s]
                )

        def slab_copies(which, start):
            for s in range(count):
                end = 0
                for index in range(pieces[s]):
                    source = sources[begins[s] + index]
                    first = end
                    end += source.shape[0] // tile

                    def act(source=source, first=first, s=s):
                        row = pl.multiple_of((begin // tile + which - first) * tile, tile)
                        copy = pltpu.make_async_copy(
                            source.at[pl.ds(row, tile), :],
                            left.at[which % 2, :, pl.ds(s * depth, depth)],
                            left_sems.at[which % 2, s],
                        )
                        copy.start() if start else copy.wait()

                    at = begin // tile + which
                    if pieces[s] == 1:
                        act()
                    else:
                        pl.when(jnp.logical_and(at >= first, at < end))(act)

        @pl.when(step == 0)
        def _():
            for copy in amp_copies():
                copy.start()
            slab_copies(step, True)
            if extra:
                for copy in copies_in(source, scratch[0], scratch[1]):
                    copy.start()

        @pl.when(step + 1 < steps)
        def _():
            slab_copies(step + 1, True)

        @pl.when(step == 0)
        def _():
            for copy in amp_copies():
                copy.wait()

        slab_copies(step, False)
        total = lax.dot_general(
            left[slot], right[...], (((1,), (1,)), ((), ())), preferred_element_type=jnp.float32
        )
        at = 0
        for span in spans:
            part = part_refs[at][...]
            for index in range(1, len(span)):
                part = jnp.where(step >= span[index][0], part_refs[at + index][...], part)
            total = total + part.astype(jnp.float32)
            at += len(span)
        out[...] = total.astype(out.dtype)

        if extra:

            @pl.when(step == 1)
            def _():
                for copy in copies_in(source, scratch[0], scratch[1]):
                    copy.wait()
                for copy in copies_out(scratch[0], target, scratch[2]):
                    copy.start()

            @pl.when(step == steps - 1)
            def _():
                for copy in copies_out(scratch[0], target, scratch[2]):
                    copy.wait()

    def rows_of(start, end):
        return pl.BlockSpec((tile, cols), lambda i: (jnp.clip(i - start, 0, end - start - 1), 0))

    bytes_moved = 2 * count * (length * depth + cols * depth)
    bytes_moved += sum(length * cols * p.dtype.itemsize for p in parts)
    return pl.pallas_call(
        kernel,
        grid=(steps,),
        in_specs=[pl.BlockSpec(memory_space=pl.ANY)] * (sum(pieces) + count + len(earlier) + len(extra))
        + [rows_of(*ends) for span in spans for ends in span],
        out_specs=[pl.BlockSpec((tile, cols), lambda i: (i, 0))]
        + [pl.BlockSpec(memory_space=pl.ANY)] * len(extra),
        out_shape=[jax.ShapeDtypeStruct((length, cols), out_dtype)]
        + [jax.ShapeDtypeStruct(x.shape, x.dtype) for x in extra],
        scratch_shapes=[
            pltpu.VMEM((2, tile, count * depth), jnp.bfloat16),
            pltpu.VMEM((cols, count * depth), jnp.bfloat16),
            pltpu.SemaphoreType.DMA((2, count)),
            pltpu.SemaphoreType.DMA((count,)),
            *(copy_scratch(*copied.shape) if extra else []),
        ],
        compiler_params=pltpu.CompilerParams(vmem_limit_bytes=VMEM),
        cost_estimate=pl.CostEstimate(
            flops=2 * length * depth * cols * count,
            bytes_accessed=(bytes_moved + length * cols * jnp.dtype(out_dtype).itemsize),
            transcendentals=0,
        ),
    )(*[p for t in terms for p in t[0].pieces], *[t[1] for t in terms], *earlier, *extra, *parts)


def paired_plan(three_index, orbital_map, occ_energy, vir_energy, pair_kept):
    blocks = lax.axis_size("wide")
    routes = Routes(blocks)
    here = lax.axis_index("wide")
    side = lax.axis_index("narrow")
    aux, vir_count = three_index.shape[1:]

    def moved(slab, pairs):
        sent = [lax.ppermute(piece, "wide", pairs) for piece in slab.pieces]
        return Slab(sent, routes.moved(slab.ids, pairs), slab.far)

    def swapped(slab):
        return moved(slab, routes.swap)

    flag = jnp.asarray(np.array(routes.lead, np.int32))[here].reshape(1)

    def chosen(of_lead, of_other, *earlier, pieces=1):
        return Slab(
            choice_call(flag, of_lead.array, of_other.array, earlier, pieces),
            routes.either(of_lead.ids, of_other.ids),
            of_lead.far,
        )

    def sibling(array):
        return lax.ppermute(array, "narrow", [(0, 1), (1, 0)])

    plan = jnp.zeros((TAIL, vir_count), jnp.bfloat16)
    plan = plan.at[0, : ROUNDS + 1].set(pair_kept[:, 0].astype(jnp.bfloat16))
    own = Slab(append_call(three_index[0], plan), list(range(blocks)))

    r1 = moved(own, routes.rounds[0])
    own_far = Slab(sibling(own.array), own.ids, 1)
    mate = swapped(own)
    s1 = swapped(r1)
    sent2 = chosen(own, r1, mate.array)
    r2 = moved(sent2, routes.rounds[1])

    labels = jnp.arange(occ_energy.shape[0], dtype=jnp.int32)
    picked = orbital_map[:, None] == labels[None, :]
    energy = jnp.sum(jnp.where(picked, occ_energy[None, :], 0.0), axis=1)

    def table_of(ids):
        ids = np.array(ids, np.int32).T
        places = np.arange(blocks)[:, None]
        back, forth = (places - ids) % blocks, (ids - places) % blocks
        behind = back <= ROUNDS
        known = np.stack([ids, np.where(behind, back, -1), np.where(behind, -1, forth)])
        block, mine, theirs = jnp.asarray(known.astype(np.int32))[:, here]
        places = jnp.arange(blocks, dtype=jnp.int32)[None, :]
        both = jnp.where(places == here, energy[None, :], 0.0)
        both = both + jnp.where(places == block[:, None], energy[None, :], 0.0)
        entries = jnp.arange(ROUNDS + 1, dtype=jnp.int32)[None, :]
        kept = pair_kept[:, 0].astype(jnp.float32)[None, :]
        weight = jnp.sum(jnp.where(entries == mine[:, None], kept, 0.0), axis=1)
        return jnp.stack([jnp.sum(both, axis=1), weight, theirs.astype(jnp.float32)], axis=1)

    vir = jnp.stack(
        [lax.dynamic_slice_in_dim(vir_energy, s * vir_count, vir_count) for s in (side, 1 - side)]
    )
    vir_rows, vir_cols = vir[:, :, None], vir[:, None, :]

    r3_ids = routes.moved(routes.either(r2.ids, own.ids), routes.rounds[2])
    r4_ids = routes.moved(r3_ids, routes.rounds[3])
    r5_ids = routes.moved(own.ids, routes.rounds[4])
    all_ids = [own.ids, mate.ids, r1.ids, s1.ids, r2.ids, routes.moved(r2.ids, routes.swap)]
    all_ids += [r3_ids, routes.moved(r3_ids, routes.swap), r4_ids, r5_ids, routes.moved(r5_ids, routes.swap)]
    table = table_of(all_ids)
    near, far = 0, 1
    rows_near = own.array[:aux].T
    stacks = {}

    def amps(jobs, turned, *earlier):
        lines = {slab: all_ids.index(slab.ids) for slab, _ in jobs}
        stack = amplitude_call(jobs, table, lines, turned, vir_rows, vir_cols, earlier)
        for place, job in enumerate(jobs):
            stacks[job] = (stack, place)
        return stack

    def density(slabs, block, parts, dtype, *earlier, rows=None, copied=None):
        terms = [(slab, *stacks[slab, block]) for slab in slabs]
        out, *copy = density_call(terms, parts, dtype, aux, earlier, rows, copied)
        return (out, *copy) if copy else out

    f32, bf16 = jnp.float32, jnp.bfloat16
    done = amps([(s, near) for s in (own, mate, r1, s1)], [rows_near], sent2.array)

    sent, kept = choice_call(flag, r2.array, own.array, [done], keep=True)
    r2 = Slab(kept, r2.ids)
    sent3 = Slab(sent, routes.either(r2.ids, own.ids))
    r3 = moved(sent3, routes.rounds[2])
    s2 = swapped(r2)
    rows_far = own_far.array[:aux].T
    part, again = density([own, mate, r1, s1], near, [], f32, sent3.array, copied=own_far.array)
    mate_far = swapped(Slab(again, own.ids, 1))
    jobs = [(r1, far), (s1, far), (r2, near), (r2, far), (s2, far), (s2, near)]
    done = amps(jobs, [rows_near, rows_far], part)

    r3 = chosen(r3, r3, done)
    r4 = moved(r3, routes.rounds[3])
    s3 = swapped(r3)
    jobs = [(own_far, near), (mate_far, near), (r3, near), (r3, far), (s3, far), (s3, near)]
    done = amps(jobs, [rows_near, rows_far], done)
    slabs = [own_far, mate_far, r2, s2, r3, s3]
    part, again = density(slabs, near, [[part]], f32, done, copied=own.array)
    r5 = moved(Slab(again, own.ids), routes.rounds[4])

    done = amps([(r4, far)], [rows_near, rows_far], part)
    slabs = [r1, s1, r2, s2, r3, s3, r4]
    half = aux // 2
    sent0, again = density(slabs, far, [], bf16, done, rows=(0, half), copied=own_far.array)
    sent1 = density(slabs, far, [], bf16, sent0, rows=(half, half))
    r6 = moved(Slab(again, own.ids, 1), routes.rounds[4])
    incoming = [sibling(sent0), sibling(sent1)]
    done = amps([(r4, near)], [rows_near], sent1)

    r5 = chosen(r5, r5, done, pieces=3)
    s5 = swapped(r5)
    done = amps([(r5, near)], [rows_near], r5.array)
    done = join_call([incoming[0], done])
    done = amps([(s5, near)], [rows_near], done)
    part = density([r4, r5, s5], near, [[part]], f32, done)
    r6 = chosen(r6, r6, part, pieces=3)
    s6 = swapped(r6)
    done = amps([(r6, near)], [rows_near], r6.array)
    done = join_call([incoming[1], done])
    done = amps([(s6, near)], [rows_near], done)
    return density([r6, s6], near, [[part], incoming], f32, done)[None]


def solution(mesh):
    wide, narrow = mesh.shape["wide"], mesh.shape["narrow"]
    paired = narrow == 2 and wide % 4 == 0 and wide > 2 * ROUNDS + 1 and ROUNDS == 5

    def per_device(three_index, *rest):
        if paired and three_index.shape[0] == 1:
            return paired_plan(three_index, *rest)
        return ring_plan(three_index, *rest)

    placed = (P("wide", None, "narrow"), P(), P(), P(), P(None, "wide"))
    return jax.shard_map(
        per_device, mesh=mesh, in_specs=placed, out_specs=P("wide", None, "narrow"), check_vma=False
    )
```

```python
import jax
import jax.numpy as jnp
import numpy as np
from jax import lax
from jax.experimental import pallas as pl
from jax.experimental.pallas import tpu as pltpu
from jax.sharding import PartitionSpec as P

ROUNDS = 5
TAIL = 16
CHUNK = 512
PIECES = 3
VMEM = 56 * 1024 * 1024


def passed_along(array, axis, by):
    length = lax.axis_size(axis)
    return lax.ppermute(array, axis, [(i, (i + by) % length) for i in range(length)])


def block_energy(orbital_map, occ_energy, block_id, occ_count):
    orbits = lax.dynamic_slice_in_dim(orbital_map, block_id * occ_count, occ_count)
    labels = jnp.arange(occ_energy.shape[0], dtype=jnp.int32)
    chosen = orbits[:, None] == labels[None, :]
    return jnp.sum(jnp.where(chosen, occ_energy[None, :], 0.0), axis=1)


def amplitudes(gathered, visiting, left_energy, right_energy, vir_all, vir_local, weight):
    coulomb = jnp.einsum("ipa,jpb->ijab", gathered, visiting, preferred_element_type=jnp.float32)
    denominator = (vir_all[:, None] + vir_local[None, :])[None, None] - (
        left_energy[:, None] + right_energy[None, :]
    )[:, :, None, None]
    return (weight * coulomb / denominator).astype(jnp.bfloat16)


def ring_plan(three_index, orbital_map, occ_energy, vir_energy, pair_kept):
    occ_count = three_index.shape[0]
    vir_count = three_index.shape[2]
    blocks = lax.axis_size("wide")
    own_block = lax.axis_index("wide")
    vir_local = lax.dynamic_slice_in_dim(
        vir_energy, lax.axis_index("narrow") * vir_count, vir_count
    )
    own_energy = block_energy(orbital_map, occ_energy, own_block, occ_count)
    weights = pair_kept.astype(jnp.float32)
    gathered = lax.all_gather(three_index, "narrow", axis=2, tiled=True)
    amplitude = amplitudes(
        gathered, three_index, own_energy, own_energy, vir_energy, vir_local, weights[0, 0]
    )
    forward = jnp.einsum(
        "ijab,jpb->ipa", amplitude, three_index, preferred_element_type=jnp.float32
    )
    visiting = three_index
    stored_amps = []
    for round_index in range(1, ROUNDS + 1):
        visiting = passed_along(visiting, "wide", 1)
        partner = (own_block - round_index) % blocks
        partner_energy = block_energy(orbital_map, occ_energy, partner, occ_count)
        amplitude = amplitudes(
            gathered,
            visiting,
            own_energy,
            partner_energy,
            vir_energy,
            vir_local,
            weights[round_index, 0],
        )
        forward = forward + jnp.einsum(
            "ijab,jpb->ipa", amplitude, visiting, preferred_element_type=jnp.float32
        )
        stored_amps.append(amplitude)
    carried = None
    for round_index in range(1, ROUNDS + 1):
        backward = jnp.einsum(
            "ijab,ipa->jpb",
            stored_amps[round_index - 1],
            gathered,
            preferred_element_type=jnp.float32,
        )
        if round_index > 1:
            carried = passed_along(carried, "wide", 1) + backward
        else:
            carried = backward
    returned = passed_along(carried, "wide", -ROUNDS)
    scattered = lax.psum_scatter(forward, "narrow", scatter_dimension=2, tiled=True)
    return scattered + returned


class Routes:
    def __init__(self, blocks):
        self.blocks = blocks
        everyone = range(blocks)
        self.lead = [self.place(w)[1] == self.place(w)[2] for w in everyone]
        self.swap = [(w, w ^ 1) for w in everyone]
        onward = [(w, self.along_z(w, 1)) for w in everyone]
        backward = [(w, self.along_z(w, -1)) for w in everyone]
        across = [(w, self.across_x(w)) for w in everyone]
        self.rounds = [
            self.either(across, onward),
            self.either(onward, across),
            self.either(across, backward),
            self.either(backward, across),
            self.either(backward, across),
        ]

    def place(self, w):
        return w // 4, (w // 2) % 2, w % 2

    def along_z(self, w, step):
        z, x, core = self.place(w)
        z = (z + (step if x == 1 else -step)) % (self.blocks // 4)
        return (z * 2 + x) * 2 + core

    def across_x(self, w):
        z, x, core = self.place(w)
        return (z * 2 + 1 - x) * 2 + 1 - core

    def either(self, of_lead, of_other):
        return [a if lead else b for lead, a, b in zip(self.lead, of_lead, of_other)]

    def moved(self, ids, pairs):
        out = [0] * self.blocks
        for source, target in pairs:
            out[target] = ids[source]
        return out


class Slab:
    def __init__(self, array, ids, far=0):
        self.pieces = list(array) if isinstance(array, (list, tuple)) else [array]
        self.array = self.pieces[0]
        self.ids = ids
        self.far = far


def pick(step, values):
    out = values[0]
    for index, value in enumerate(values):
        if index and value != values[0]:
            out = jnp.where(step == index, value, out)
    return out


def amplitude_call(jobs, table, lines, turned, vir_rows, vir_cols, earlier):
    slabs = []
    for slab, _ in jobs:
        if slab not in slabs:
            slabs.append(slab)
    count, blocks = len(slabs), len(turned)
    cols, aux = turned[0].shape
    held_rows = aux + TAIL
    pieces = [len(slab.pieces) for slab in slabs]
    begins = [sum(pieces[:s]) for s in range(count)]
    of_job = [slabs.index(slab) for slab, _ in jobs]
    block_of = [block for _, block in jobs]
    far_of = [slab.far for slab, _ in jobs]
    line_of = [lines[slab] for slab, _ in jobs]
    opens = [t for t in range(len(jobs)) if t == 0 or of_job[t] != of_job[t - 1]]
    half = cols // 2

    def kernel(scalars, *refs):
        sources, refs = refs[: sum(pieces)], refs[sum(pieces) :]
        row_sources, refs = refs[:blocks], refs[blocks + len(earlier) :]
        vir_row, vir_col, out, held, rows, held_sems, row_sems = refs
        step = pl.program_id(0)

        def slab_copies(s):
            row = 0
            for index in range(pieces[s]):
                source = sources[begins[s] + index]
                target = held.at[s % 2, pl.ds(row, source.shape[0]), :]
                yield pltpu.make_async_copy(source, target, held_sems.at[s % 2, index])
                row += source.shape[0]

        def row_copy(block):
            return pltpu.make_async_copy(row_sources[block], rows.at[block], row_sems.at[block])

        @pl.when(step == 0)
        def _():
            for copy in slab_copies(0):
                copy.start()
            for block in dict.fromkeys(block_of):
                row_copy(block).start()

        for s, t in enumerate(opens):

            @pl.when(step == t)
            def _(s=s):
                for copy in slab_copies(s):
                    copy.wait()
                if s + 1 < count:
                    for copy in slab_copies(s + 1):
                        copy.start()

        for block in dict.fromkeys(block_of):

            @pl.when(step == block_of.index(block))
            def _(block=block):
                row_copy(block).wait()

        slot = pick(step, [s % 2 for s in of_job])
        block = pick(step, block_of)
        line = pick(step, line_of)
        plan = held[slot, aux:, :128].astype(jnp.float32)
        lane = lax.broadcasted_iota(jnp.int32, plan.shape, 1).astype(jnp.float32)
        row = lax.broadcasted_iota(jnp.int32, plan.shape, 0)
        told = jnp.where(jnp.logical_and(row == 0, lane == scalars[line, 2]), plan, 0.0)
        weight = scalars[line, 1] + jnp.sum(told, keepdims=True)
        for begin in range(0, cols, half):
            part = pl.ds(begin, half)
            coulomb = jnp.dot(rows[block], held[slot, :aux, part], preferred_element_type=jnp.float32)
            denominator = (vir_row[0] + vir_col[0, :, part]) - scalars[line, 0]
            out[0, :, part] = (weight * coulomb / denominator).astype(out.dtype)

    return pl.pallas_call(
        kernel,
        grid=(len(jobs),),
        in_specs=[pl.BlockSpec(memory_space=pltpu.SMEM)]
        + [pl.BlockSpec(memory_space=pl.ANY)] * (sum(pieces) + blocks + len(earlier))
        + [
            pl.BlockSpec((1, cols, 1), lambda t: (pick(t, block_of), 0, 0)),
            pl.BlockSpec((1, 1, cols), lambda t: (pick(t, far_of), 0, 0)),
        ],
        out_specs=pl.BlockSpec((1, cols, cols), lambda t: (t, 0, 0)),
        out_shape=jax.ShapeDtypeStruct((len(jobs), cols, cols), jnp.bfloat16),
        scratch_shapes=[
            pltpu.VMEM((2, held_rows, cols), jnp.bfloat16),
            pltpu.VMEM((blocks, cols, aux), jnp.bfloat16),
            pltpu.SemaphoreType.DMA((2, max(pieces))),
            pltpu.SemaphoreType.DMA((blocks,)),
        ],
        compiler_params=pltpu.CompilerParams(vmem_limit_bytes=VMEM),
        cost_estimate=pl.CostEstimate(
            flops=2 * len(jobs) * cols * aux * cols,
            bytes_accessed=2 * cols * (blocks * aux + count * aux + len(jobs) * cols),
            transcendentals=0,
        ),
    )(table, *[p for s in slabs for p in s.pieces], *turned, *earlier, vir_rows, vir_cols)


def chunks_of(rows):
    return [(begin, min(CHUNK, rows - begin)) for begin in range(0, rows, CHUNK)]


def copies_in(sources, held, sems):
    row, index = 0, 0
    for source in sources:
        for begin, size in chunks_of(source.shape[0]):
            yield pltpu.make_async_copy(
                source.at[pl.ds(begin, size)], held.at[pl.ds(row + begin, size)], sems.at[index]
            )
            index += 1
        row += source.shape[0]


def copies_out(held, targets, sems):
    row, index = 0, 0
    for target in targets:
        for begin, size in chunks_of(target.shape[0]):
            yield pltpu.make_async_copy(
                held.at[pl.ds(row + begin, size)], target.at[pl.ds(begin, size)], sems.at[index]
            )
            index += 1
        row += target.shape[0]


def copy_scratch(rows, cols):
    count = len(chunks_of(rows)) + 1
    return [
        pltpu.VMEM((rows, cols), jnp.bfloat16),
        pltpu.SemaphoreType.DMA((count,)),
        pltpu.SemaphoreType.DMA((count,)),
    ]


def copy_through(sources, targets, held, in_sems, out_sems):
    if [x.shape[0] for x in sources] != [x.shape[0] for x in targets]:
        loads, stores = [list(copies_in(sources, held, in_sems))], [list(copies_out(held, targets, out_sems))]
    else:
        loads = [[copy] for copy in copies_in(sources, held, in_sems)]
        stores = [[copy] for copy in copies_out(held, targets, out_sems)]
    for copies in loads:
        for copy in copies:
            copy.start()
    for before, behind in zip(loads, stores):
        for copy in before:
            copy.wait()
        for copy in behind:
            copy.start()
    for copies in stores:
        for copy in copies:
            copy.wait()


def append_call(array, tail):
    def kernel(array_ref, tail_ref, out, held, in_sems, out_sems):
        rows = array_ref.shape[0]
        targets = [out.at[pl.ds(0, rows)], out.at[pl.ds(rows, tail_ref.shape[0])]]
        copy_through([array_ref, tail_ref], targets, held, in_sems, out_sems)

    rows, cols = array.shape[0] + tail.shape[0], array.shape[1]
    return pl.pallas_call(
        kernel,
        in_specs=[pl.BlockSpec(memory_space=pl.ANY)] * 2,
        out_specs=pl.BlockSpec(memory_space=pl.ANY),
        out_shape=jax.ShapeDtypeStruct((rows, cols), array.dtype),
        scratch_shapes=copy_scratch(rows, cols),
        compiler_params=pltpu.CompilerParams(vmem_limit_bytes=VMEM),
    )(array, tail)


def choice_call(flag, a, b, earlier, pieces=1, keep=False):
    rows, cols = a.shape
    size = rows // pieces // CHUNK * CHUNK if pieces > 1 else rows
    begins = [index * size for index in range(pieces)] + [rows]
    shapes = [(end - begin, cols) for begin, end in zip(begins, begins[1:])]
    kept = [(rows, cols)] if keep else []

    def kernel(flag_ref, a_ref, b_ref, *refs):
        refs = refs[len(earlier) :]
        outs, kept_outs, scratch = refs[:pieces], refs[pieces : pieces + len(kept)], refs[pieces + len(kept) :]
        if keep:
            held, loads, stores, other_held, other_loads, other_stores = scratch
            leads = flag_ref[0] == 1
            ours = list(copies_in([a_ref], held, loads))
            theirs = list(copies_in([b_ref], other_held, other_loads))
            kept_copies = list(copies_out(held, kept_outs, stores))
            ours_out = list(copies_out(held, outs, other_stores))
            theirs_out = list(copies_out(other_held, outs, other_stores))
            for copy in ours:
                copy.start()

            @pl.when(jnp.logical_not(leads))
            def _():
                for copy in theirs:
                    copy.start()

            for load, store, also in zip(ours, kept_copies, ours_out):
                load.wait()
                store.start()
                pl.when(leads)(also.start)

            @pl.when(jnp.logical_not(leads))
            def _():
                for load, store in zip(theirs, theirs_out):
                    load.wait()
                    store.start()

            for store, also in zip(kept_copies, ours_out):
                store.wait()
                also.wait()
        else:
            for value, source in ((1, a_ref), (0, b_ref)):

                @pl.when(flag_ref[0] == value)
                def _(source=source):
                    parts = [source.at[pl.ds(at, out.shape[0])] for at, out in zip(begins, outs)]
                    copy_through(parts, outs, *scratch)

    return pl.pallas_call(
        kernel,
        in_specs=[pl.BlockSpec(memory_space=pltpu.SMEM)]
        + [pl.BlockSpec(memory_space=pl.ANY)] * (2 + len(earlier)),
        out_specs=[pl.BlockSpec(memory_space=pl.ANY)] * (pieces + len(kept)),
        out_shape=[jax.ShapeDtypeStruct(shape, a.dtype) for shape in shapes + kept],
        scratch_shapes=copy_scratch(rows, cols) * (1 + len(kept)),
        compiler_params=pltpu.CompilerParams(vmem_limit_bytes=VMEM),
        cost_estimate=pl.CostEstimate(flops=0, bytes_accessed=2 * a.size * a.dtype.itemsize, transcendentals=0),
    )(flag, a, b, *earlier)


def join_call(earlier):
    def kernel(*refs):
        refs[-1][...] = jnp.zeros_like(refs[-1])

    return pl.pallas_call(
        kernel,
        in_specs=[pl.BlockSpec(memory_space=pl.ANY)] * len(earlier),
        out_specs=pl.BlockSpec(memory_space=pltpu.VMEM),
        out_shape=jax.ShapeDtypeStruct((8, 128), jnp.float32),
    )(*earlier)


def density_call(terms, parts, out_dtype, aux, earlier, rows=None, copied=None):
    count = len(terms)
    depth = terms[0][0].array.shape[1]
    extra = list(copied or [])
    whole = [jax.ShapeDtypeStruct((sum(x.shape[0] for x in extra), depth), jnp.bfloat16)] if extra else []
    pieces = [len(t[0].pieces) for t in terms]
    begins = [sum(pieces[:s]) for s in range(count)]
    cols = depth
    begin, length = rows or (0, aux)
    tile = 512
    while length % tile or begin % tile:
        tile //= 2
    steps = length // tile
    spans = []
    for part in parts:
        ends = np.cumsum([piece.shape[0] // tile for piece in part])
        shift = begin // tile if ends[-1] == aux // tile else 0
        spans.append([(int(end) - piece.shape[0] // tile - shift, int(end) - shift) for end, piece in zip(ends, part)])
    parts = [p for part in parts for p in part]

    def kernel(*refs):
        sources, refs = refs[: sum(pieces)], refs[sum(pieces) :]
        amps, refs = refs[:count], refs[count + len(earlier) :]
        source, refs = refs[: len(extra)], refs[len(extra) :]
        part_refs, out, refs = refs[: len(parts)], refs[len(parts)], refs[len(parts) + 1 :]
        target, refs = refs[: len(whole)], refs[len(whole) :]
        (left, right, left_sems, right_sems), scratch = refs[:4], refs[4:]
        step = pl.program_id(0)
        slot = step % 2

        def amp_copies():
            for s, (_, _, place) in enumerate(terms):
                yield pltpu.make_async_copy(
                    amps[s].at[place], right.at[:, pl.ds(s * depth, depth)], right_sems.at[s]
                )

        def slab_copies(which, start):
            for s in range(count):
                end = 0
                for index in range(pieces[s]):
                    source = sources[begins[s] + index]
                    first = end
                    end += source.shape[0] // tile

                    def act(source=source, first=first, s=s):
                        row = pl.multiple_of((begin // tile + which - first) * tile, tile)
                        copy = pltpu.make_async_copy(
                            source.at[pl.ds(row, tile), :],
                            left.at[which % 2, :, pl.ds(s * depth, depth)],
                            left_sems.at[which % 2, s],
                        )
                        copy.start() if start else copy.wait()

                    at = begin // tile + which
                    if pieces[s] == 1:
                        act()
                    else:
                        pl.when(jnp.logical_and(at >= first, at < end))(act)

        @pl.when(step == 0)
        def _():
            for copy in amp_copies():
                copy.start()
            slab_copies(step, True)
            if extra:
                for copy in copies_in(source, scratch[0], scratch[1]):
                    copy.start()

        @pl.when(step + 1 < steps)
        def _():
            slab_copies(step + 1, True)

        @pl.when(step == 0)
        def _():
            for copy in amp_copies():
                copy.wait()

        slab_copies(step, False)
        total = lax.dot_general(
            left[slot], right[...], (((1,), (1,)), ((), ())), preferred_element_type=jnp.float32
        )
        at = 0
        for span in spans:
            part = part_refs[at][...]
            for index in range(1, len(span)):
                part = jnp.where(step >= span[index][0], part_refs[at + index][...], part)
            total = total + part.astype(jnp.float32)
            at += len(span)
        out[...] = total.astype(out.dtype)

        if extra:

            @pl.when(step == 1)
            def _():
                for copy in copies_in(source, scratch[0], scratch[1]):
                    copy.wait()
                for copy in copies_out(scratch[0], target, scratch[2]):
                    copy.start()

            @pl.when(step == steps - 1)
            def _():
                for copy in copies_out(scratch[0], target, scratch[2]):
                    copy.wait()

    def rows_of(start, end):
        return pl.BlockSpec((tile, cols), lambda i: (jnp.clip(i - start, 0, end - start - 1), 0))

    bytes_moved = 2 * count * (length * depth + cols * depth)
    bytes_moved += sum(length * cols * p.dtype.itemsize for p in parts)
    return pl.pallas_call(
        kernel,
        grid=(steps,),
        in_specs=[pl.BlockSpec(memory_space=pl.ANY)] * (sum(pieces) + count + len(earlier) + len(extra))
        + [rows_of(*ends) for span in spans for ends in span],
        out_specs=[pl.BlockSpec((tile, cols), lambda i: (i, 0))]
        + [pl.BlockSpec(memory_space=pl.ANY)] * len(whole),
        out_shape=[jax.ShapeDtypeStruct((length, cols), out_dtype)]
        + whole,
        scratch_shapes=[
            pltpu.VMEM((2, tile, count * depth), jnp.bfloat16),
            pltpu.VMEM((cols, count * depth), jnp.bfloat16),
            pltpu.SemaphoreType.DMA((2, count)),
            pltpu.SemaphoreType.DMA((count,)),
            *(copy_scratch(*whole[0].shape) if extra else []),
        ],
        compiler_params=pltpu.CompilerParams(vmem_limit_bytes=VMEM),
        cost_estimate=pl.CostEstimate(
            flops=2 * length * depth * cols * count,
            bytes_accessed=(bytes_moved + length * cols * jnp.dtype(out_dtype).itemsize),
            transcendentals=0,
        ),
    )(*[p for t in terms for p in t[0].pieces], *[t[1] for t in terms], *earlier, *extra, *parts)


def paired_plan(three_index, orbital_map, occ_energy, vir_energy, pair_kept):
    blocks = lax.axis_size("wide")
    routes = Routes(blocks)
    here = lax.axis_index("wide")
    side = lax.axis_index("narrow")
    aux, vir_count = three_index.shape[1:]

    def moved(slab, pairs):
        sent = [lax.ppermute(piece, "wide", pairs) for piece in slab.pieces]
        return Slab(sent, routes.moved(slab.ids, pairs), slab.far)

    def swapped(slab):
        return moved(slab, routes.swap)

    flag = jnp.asarray(np.array(routes.lead, np.int32))[here].reshape(1)

    def chosen(of_lead, of_other, *earlier, pieces=1):
        return Slab(
            choice_call(flag, of_lead.array, of_other.array, earlier, pieces),
            routes.either(of_lead.ids, of_other.ids),
            of_lead.far,
        )

    def sibling(array):
        return lax.ppermute(array, "narrow", [(0, 1), (1, 0)])

    plan = jnp.zeros((TAIL, vir_count), jnp.bfloat16)
    plan = plan.at[0, : ROUNDS + 1].set(pair_kept[:, 0].astype(jnp.bfloat16))
    own = Slab(append_call(three_index[0], plan), list(range(blocks)))

    r1 = moved(own, routes.rounds[0])
    split = choice_call(flag, own.array, own.array, [], pieces=2)
    own_far = Slab([sibling(piece) for piece in split], own.ids, 1)
    mate = swapped(own)

    labels = jnp.arange(occ_energy.shape[0], dtype=jnp.int32)
    picked = orbital_map[:, None] == labels[None, :]
    energy = jnp.sum(jnp.where(picked, occ_energy[None, :], 0.0), axis=1)

    def table_of(ids):
        ids = np.array(ids, np.int32).T
        places = np.arange(blocks)[:, None]
        back, forth = (places - ids) % blocks, (ids - places) % blocks
        behind = back <= ROUNDS
        known = np.stack([ids, np.where(behind, back, -1), np.where(behind, -1, forth)])
        block, mine, theirs = jnp.asarray(known.astype(np.int32))[:, here]
        places = jnp.arange(blocks, dtype=jnp.int32)[None, :]
        both = jnp.where(places == here, energy[None, :], 0.0)
        both = both + jnp.where(places == block[:, None], energy[None, :], 0.0)
        entries = jnp.arange(ROUNDS + 1, dtype=jnp.int32)[None, :]
        kept = pair_kept[:, 0].astype(jnp.float32)[None, :]
        weight = jnp.sum(jnp.where(entries == mine[:, None], kept, 0.0), axis=1)
        return jnp.stack([jnp.sum(both, axis=1), weight, theirs.astype(jnp.float32)], axis=1)

    vir = jnp.stack(
        [lax.dynamic_slice_in_dim(vir_energy, s * vir_count, vir_count) for s in (side, 1 - side)]
    )
    vir_rows, vir_cols = vir[:, :, None], vir[:, None, :]

    def moved_ids(ids_lead, ids_other, pairs):
        return routes.moved(routes.either(ids_lead, ids_other), pairs)

    def swapped_ids(ids):
        return routes.moved(ids, routes.swap)

    r2_ids = moved_ids(own.ids, r1.ids, routes.rounds[1])
    r3_ids = moved_ids(r2_ids, own.ids, routes.rounds[2])
    r4_ids = routes.moved(r3_ids, routes.rounds[3])
    r5_ids = routes.moved(own.ids, routes.rounds[4])
    all_ids = [own.ids, mate.ids]
    for ids in (r1.ids, r2_ids, r3_ids, r4_ids, r5_ids):
        all_ids += [ids, swapped_ids(ids)]
    table = table_of(all_ids)
    near, far = 0, 1
    rows_near = own.array[:aux].T
    stacks = {}

    def amps(jobs, turned, *earlier):
        lines = {slab: all_ids.index(slab.ids) for slab, _ in jobs}
        stack = amplitude_call(jobs, table, lines, turned, vir_rows, vir_cols, earlier)
        for place, job in enumerate(jobs):
            stacks[job] = (stack, place)
        return stack

    def density(slabs, block, parts, dtype, *earlier, rows=None, copied=None):
        terms = [(slab, *stacks[slab, block]) for slab in slabs]
        out, *copy = density_call(terms, parts, dtype, aux, earlier, rows, copied)
        return (out, *copy) if copy else out

    f32, bf16 = jnp.float32, jnp.bfloat16
    done = amps([(own, near), (mate, near)], [rows_near])

    sent2 = chosen(own, r1, own_far.pieces[0], done)
    r2 = moved(sent2, routes.rounds[1])
    s1 = swapped(r1)
    done = amps([(r1, near), (s1, near)], [rows_near], sent2.array)
    part = density([own, mate, r1, s1], near, [], f32, done)

    sent, kept = choice_call(flag, r2.array, own.array, [part, *own_far.pieces], keep=True)
    r2 = Slab(kept, r2.ids)
    sent3 = Slab(sent, routes.either(r2.ids, own.ids))
    r3 = moved(sent3, routes.rounds[2])
    s2 = swapped(r2)
    mate_far = swapped(own_far)
    rows_far = jnp.concatenate(own_far.pieces)[:aux].T
    jobs = [(r1, far), (s1, far), (r2, near), (r2, far), (s2, far), (s2, near)]
    jobs += [(own_far, near), (mate_far, near)]
    done = amps(jobs, [rows_near, rows_far], sent3.array)
    part = density([own_far, mate_far, r2, s2], near, [[part]], f32, done)

    r3 = chosen(r3, r3, part)
    r4 = moved(r3, routes.rounds[3])
    s3 = swapped(r3)
    out_part, again = density([r1, s1, r2, s2], far, [], f32, r3.array, copied=own.pieces)
    r5 = moved(Slab(again, own.ids), routes.rounds[4])
    jobs = [(r3, near), (r3, far), (s3, far), (s3, near)]
    done = amps(jobs, [rows_near, rows_far], out_part)
    part = density([r3, s3], near, [[part]], f32, done)

    done = amps([(r4, far)], [rows_near, rows_far], part)
    half = aux // 2
    slabs = [r3, s3, r4]
    sent0, again = density(
        slabs, far, [[out_part]], bf16, done, rows=(0, half), copied=own_far.pieces
    )
    r6 = moved(Slab(again, own.ids, 1), routes.rounds[4])
    sent1 = density(slabs, far, [[out_part]], bf16, sent0, rows=(half, half))
    incoming = [sibling(sent0), sibling(sent1)]
    done = amps([(r4, near)], [rows_near], sent1)

    r5 = chosen(r5, r5, done, pieces=PIECES)
    s5 = swapped(r5)
    done = amps([(r5, near)], [rows_near], *r5.pieces)
    done = join_call([incoming[0], done])
    done = amps([(s5, near)], [rows_near], done)
    part = density([r4, r5, s5], near, [[part]], f32, done)
    r6 = chosen(r6, r6, part, pieces=PIECES)
    s6 = swapped(r6)
    done = amps([(r6, near)], [rows_near], *r6.pieces)
    done = join_call([incoming[1], done])
    done = amps([(s6, near)], [rows_near], done)
    return density([r6, s6], near, [[part], incoming], f32, done)[None]


def solution(mesh):
    wide, narrow = mesh.shape["wide"], mesh.shape["narrow"]
    paired = narrow == 2 and wide % 4 == 0 and wide > 2 * ROUNDS + 1 and ROUNDS == 5

    def per_device(three_index, *rest):
        if paired and three_index.shape[0] == 1:
            return paired_plan(three_index, *rest)
        return ring_plan(three_index, *rest)

    placed = (P("wide", None, "narrow"), P(), P(), P(), P(None, "wide"))
    return jax.shard_map(
        per_device, mesh=mesh, in_specs=placed, out_specs=P("wide", None, "narrow"), check_vma=False
    )
```

```python
import jax
import jax.numpy as jnp
import numpy as np
from jax import lax
from jax.experimental import pallas as pl
from jax.experimental.pallas import tpu as pltpu
from jax.sharding import PartitionSpec as P

ROUNDS = 5
TAIL = 16
CHUNK = 512
PIECES = 3
VMEM = 56 * 1024 * 1024


def passed_along(array, axis, by):
    length = lax.axis_size(axis)
    return lax.ppermute(array, axis, [(i, (i + by) % length) for i in range(length)])


def block_energy(orbital_map, occ_energy, block_id, occ_count):
    orbits = lax.dynamic_slice_in_dim(orbital_map, block_id * occ_count, occ_count)
    labels = jnp.arange(occ_energy.shape[0], dtype=jnp.int32)
    chosen = orbits[:, None] == labels[None, :]
    return jnp.sum(jnp.where(chosen, occ_energy[None, :], 0.0), axis=1)


def amplitudes(gathered, visiting, left_energy, right_energy, vir_all, vir_local, weight):
    coulomb = jnp.einsum("ipa,jpb->ijab", gathered, visiting, preferred_element_type=jnp.float32)
    denominator = (vir_all[:, None] + vir_local[None, :])[None, None] - (
        left_energy[:, None] + right_energy[None, :]
    )[:, :, None, None]
    return (weight * coulomb / denominator).astype(jnp.bfloat16)


def ring_plan(three_index, orbital_map, occ_energy, vir_energy, pair_kept):
    occ_count = three_index.shape[0]
    vir_count = three_index.shape[2]
    blocks = lax.axis_size("wide")
    own_block = lax.axis_index("wide")
    vir_local = lax.dynamic_slice_in_dim(
        vir_energy, lax.axis_index("narrow") * vir_count, vir_count
    )
    own_energy = block_energy(orbital_map, occ_energy, own_block, occ_count)
    weights = pair_kept.astype(jnp.float32)
    gathered = lax.all_gather(three_index, "narrow", axis=2, tiled=True)
    amplitude = amplitudes(
        gathered, three_index, own_energy, own_energy, vir_energy, vir_local, weights[0, 0]
    )
    forward = jnp.einsum(
        "ijab,jpb->ipa", amplitude, three_index, preferred_element_type=jnp.float32
    )
    visiting = three_index
    stored_amps = []
    for round_index in range(1, ROUNDS + 1):
        visiting = passed_along(visiting, "wide", 1)
        partner = (own_block - round_index) % blocks
        partner_energy = block_energy(orbital_map, occ_energy, partner, occ_count)
        amplitude = amplitudes(
            gathered,
            visiting,
            own_energy,
            partner_energy,
            vir_energy,
            vir_local,
            weights[round_index, 0],
        )
        forward = forward + jnp.einsum(
            "ijab,jpb->ipa", amplitude, visiting, preferred_element_type=jnp.float32
        )
        stored_amps.append(amplitude)
    carried = None
    for round_index in range(1, ROUNDS + 1):
        backward = jnp.einsum(
            "ijab,ipa->jpb",
            stored_amps[round_index - 1],
            gathered,
            preferred_element_type=jnp.float32,
        )
        if round_index > 1:
            carried = passed_along(carried, "wide", 1) + backward
        else:
            carried = backward
    returned = passed_along(carried, "wide", -ROUNDS)
    scattered = lax.psum_scatter(forward, "narrow", scatter_dimension=2, tiled=True)
    return scattered + returned


class Routes:
    def __init__(self, blocks):
        self.blocks = blocks
        everyone = range(blocks)
        self.lead = [self.place(w)[1] == self.place(w)[2] for w in everyone]
        self.swap = [(w, w ^ 1) for w in everyone]
        onward = [(w, self.along_z(w, 1)) for w in everyone]
        backward = [(w, self.along_z(w, -1)) for w in everyone]
        across = [(w, self.across_x(w)) for w in everyone]
        self.rounds = [
            self.either(across, onward),
            self.either(onward, across),
            self.either(across, backward),
            self.either(backward, across),
            self.either(backward, across),
        ]

    def place(self, w):
        return w // 4, (w // 2) % 2, w % 2

    def along_z(self, w, step):
        z, x, core = self.place(w)
        z = (z + (step if x == 1 else -step)) % (self.blocks // 4)
        return (z * 2 + x) * 2 + core

    def across_x(self, w):
        z, x, core = self.place(w)
        return (z * 2 + 1 - x) * 2 + 1 - core

    def either(self, of_lead, of_other):
        return [a if lead else b for lead, a, b in zip(self.lead, of_lead, of_other)]

    def moved(self, ids, pairs):
        out = [0] * self.blocks
        for source, target in pairs:
            out[target] = ids[source]
        return out


class Slab:
    def __init__(self, array, ids, far=0):
        self.pieces = list(array) if isinstance(array, (list, tuple)) else [array]
        self.array = self.pieces[0]
        self.ids = ids
        self.far = far


def pick(step, values):
    out = values[0]
    for index, value in enumerate(values):
        if index and value != values[0]:
            out = jnp.where(step == index, value, out)
    return out


def amplitude_call(jobs, table, lines, turned, vir_rows, vir_cols, earlier):
    slabs = []
    for slab, _ in jobs:
        if slab not in slabs:
            slabs.append(slab)
    count, blocks = len(slabs), len(turned)
    cols, aux = turned[0][0].shape[0], sum(piece.shape[1] for piece in turned[0])
    held_rows = aux + TAIL
    pieces = [len(slab.pieces) for slab in slabs]
    begins = [sum(pieces[:s]) for s in range(count)]
    of_job = [slabs.index(slab) for slab, _ in jobs]
    block_of = [block for _, block in jobs]
    far_of = [slab.far for slab, _ in jobs]
    line_of = [lines[slab] for slab, _ in jobs]
    row_pieces = [len(block) for block in turned]
    chunks = aux // CHUNK
    opens = [t for t in range(len(jobs)) if t == 0 or of_job[t] != of_job[t - 1]]
    half = cols // 2

    def kernel(scalars, *refs):
        sources, refs = refs[: sum(pieces)], refs[sum(pieces) :]
        row_sources, refs = refs[: sum(row_pieces)], refs[sum(row_pieces) + len(earlier) :]
        vir_row, vir_col, out, held, rows, held_sems, row_sems = refs
        step = pl.program_id(0)

        def slab_copies(s):
            row = 0
            for index in range(pieces[s]):
                source = sources[begins[s] + index]
                for begin, size in chunks_of(source.shape[0]):
                    target = held.at[s % 2, pl.ds(row, size), :]
                    yield pltpu.make_async_copy(
                        source.at[pl.ds(begin, size)], target, held_sems.at[s % 2, row // CHUNK]
                    )
                    row += size

        def row_copies(block):
            column = 0
            for source in row_sources[sum(row_pieces[:block]) : sum(row_pieces[: block + 1])]:
                for begin, size in chunks_of(source.shape[1]):
                    target = rows.at[block, :, pl.ds(column, size)]
                    yield pltpu.make_async_copy(
                        source.at[:, pl.ds(begin, size)], target, row_sems.at[block, column // CHUNK]
                    )
                    column += size

        @pl.when(step == 0)
        def _():
            for pair in zip(slab_copies(0), row_copies(block_of[0])):
                for copy in pair:
                    copy.start()
            for copy in list(slab_copies(0))[chunks:]:
                copy.start()
            for block in list(dict.fromkeys(block_of))[1:]:
                for copy in row_copies(block):
                    copy.start()

        for s, t in enumerate(opens):

            @pl.when(step == t)
            def _(s=s):
                if s:
                    for copy in slab_copies(s):
                        copy.wait()
                if s + 1 < count:
                    for copy in slab_copies(s + 1):
                        copy.start()

        for block in list(dict.fromkeys(block_of))[1:]:

            @pl.when(step == block_of.index(block))
            def _(block=block):
                for copy in row_copies(block):
                    copy.wait()

        slot = pick(step, [s % 2 for s in of_job])
        block = pick(step, block_of)
        line = pick(step, line_of)
        @pl.when(step == 0)
        def _():
            for copy in list(slab_copies(0))[chunks:]:
                copy.wait()

        plan = held[slot, aux:, :128].astype(jnp.float32)
        lane = lax.broadcasted_iota(jnp.int32, plan.shape, 1).astype(jnp.float32)
        row = lax.broadcasted_iota(jnp.int32, plan.shape, 0)
        told = jnp.where(jnp.logical_and(row == 0, lane == scalars[line, 2]), plan, 0.0)
        weight = scalars[line, 1] + jnp.sum(told, keepdims=True)

        def finish(part, coulomb):
            denominator = (vir_row[0] + vir_col[0, :, part]) - scalars[line, 0]
            out[0, :, part] = (weight * coulomb / denominator).astype(out.dtype)

        @pl.when(step == 0)
        def _():
            coulomb = None
            for index, pair in enumerate(zip(row_copies(block_of[0]), slab_copies(0))):
                for copy in pair:
                    copy.wait()
                chunk = pl.ds(index * CHUNK, CHUNK)
                term = jnp.dot(
                    rows[block_of[0], :, chunk], held[0, chunk, :], preferred_element_type=jnp.float32
                )
                coulomb = term if coulomb is None else coulomb + term
            finish(pl.ds(0, cols), coulomb)

        @pl.when(step > 0)
        def _():
            for begin in range(0, cols, half):
                part = pl.ds(begin, half)
                finish(part, jnp.dot(rows[block], held[slot, :aux, part], preferred_element_type=jnp.float32))

    return pl.pallas_call(
        kernel,
        grid=(len(jobs),),
        in_specs=[pl.BlockSpec(memory_space=pltpu.SMEM)]
        + [pl.BlockSpec(memory_space=pl.ANY)] * (sum(pieces) + sum(row_pieces) + len(earlier))
        + [
            pl.BlockSpec((1, cols, 1), lambda t: (pick(t, block_of), 0, 0)),
            pl.BlockSpec((1, 1, cols), lambda t: (pick(t, far_of), 0, 0)),
        ],
        out_specs=pl.BlockSpec((1, cols, cols), lambda t: (t, 0, 0)),
        out_shape=jax.ShapeDtypeStruct((len(jobs), cols, cols), jnp.bfloat16),
        scratch_shapes=[
            pltpu.VMEM((2, held_rows, cols), jnp.bfloat16),
            pltpu.VMEM((blocks, cols, aux), jnp.bfloat16),
            pltpu.SemaphoreType.DMA((2, chunks + 1)),
            pltpu.SemaphoreType.DMA((blocks, chunks)),
        ],
        compiler_params=pltpu.CompilerParams(vmem_limit_bytes=VMEM),
        cost_estimate=pl.CostEstimate(
            flops=2 * len(jobs) * cols * aux * cols,
            bytes_accessed=2 * cols * (blocks * aux + count * aux + len(jobs) * cols),
            transcendentals=0,
        ),
    )(table, *[p for s in slabs for p in s.pieces], *[p for b in turned for p in b], *earlier, vir_rows, vir_cols)


def chunks_of(rows):
    return [(begin, min(CHUNK, rows - begin)) for begin in range(0, rows, CHUNK)]


def copies_in(sources, held, sems):
    row, index = 0, 0
    for source in sources:
        for begin, size in chunks_of(source.shape[0]):
            yield pltpu.make_async_copy(
                source.at[pl.ds(begin, size)], held.at[pl.ds(row + begin, size)], sems.at[index]
            )
            index += 1
        row += source.shape[0]


def copies_out(held, targets, sems):
    row, index = 0, 0
    for target in targets:
        for begin, size in chunks_of(target.shape[0]):
            yield pltpu.make_async_copy(
                held.at[pl.ds(row + begin, size)], target.at[pl.ds(begin, size)], sems.at[index]
            )
            index += 1
        row += target.shape[0]


def copy_scratch(rows, cols):
    count = len(chunks_of(rows)) + 1
    return [
        pltpu.VMEM((rows, cols), jnp.bfloat16),
        pltpu.SemaphoreType.DMA((count,)),
        pltpu.SemaphoreType.DMA((count,)),
    ]


def copy_through(sources, targets, held, in_sems, out_sems):
    if [x.shape[0] for x in sources] != [x.shape[0] for x in targets]:
        loads, stores = [list(copies_in(sources, held, in_sems))], [list(copies_out(held, targets, out_sems))]
    else:
        loads = [[copy] for copy in copies_in(sources, held, in_sems)]
        stores = [[copy] for copy in copies_out(held, targets, out_sems)]
    for copies in loads:
        for copy in copies:
            copy.start()
    for before, behind in zip(loads, stores):
        for copy in before:
            copy.wait()
        for copy in behind:
            copy.start()
    for copies in stores:
        for copy in copies:
            copy.wait()


def append_call(array, tail):
    def kernel(array_ref, tail_ref, out, held, in_sems, out_sems):
        rows = array_ref.shape[0]
        targets = [out.at[pl.ds(0, rows)], out.at[pl.ds(rows, tail_ref.shape[0])]]
        copy_through([array_ref, tail_ref], targets, held, in_sems, out_sems)

    rows, cols = array.shape[0] + tail.shape[0], array.shape[1]
    return pl.pallas_call(
        kernel,
        in_specs=[pl.BlockSpec(memory_space=pl.ANY)] * 2,
        out_specs=pl.BlockSpec(memory_space=pl.ANY),
        out_shape=jax.ShapeDtypeStruct((rows, cols), array.dtype),
        scratch_shapes=copy_scratch(rows, cols),
        compiler_params=pltpu.CompilerParams(vmem_limit_bytes=VMEM),
    )(array, tail)


def choice_call(flag, a, b, earlier, pieces=1, keep=False):
    rows, cols = a.shape
    size = rows // pieces // CHUNK * CHUNK if pieces > 1 else rows
    begins = [index * size for index in range(pieces)] + [rows]
    shapes = [(end - begin, cols) for begin, end in zip(begins, begins[1:])]
    kept = [(rows, cols)] if keep else []

    def kernel(flag_ref, a_ref, b_ref, *refs):
        refs = refs[len(earlier) :]
        outs, kept_outs, scratch = refs[:pieces], refs[pieces : pieces + len(kept)], refs[pieces + len(kept) :]
        if keep:
            held, loads, stores, other_held, other_loads, other_stores = scratch
            leads = flag_ref[0] == 1
            ours = list(copies_in([a_ref], held, loads))
            theirs = list(copies_in([b_ref], other_held, other_loads))
            kept_copies = list(copies_out(held, kept_outs, stores))
            ours_out = list(copies_out(held, outs, other_stores))
            theirs_out = list(copies_out(other_held, outs, other_stores))
            for copy in ours:
                copy.start()

            @pl.when(jnp.logical_not(leads))
            def _():
                for copy in theirs:
                    copy.start()

            for load, store, also in zip(ours, kept_copies, ours_out):
                load.wait()
                store.start()
                pl.when(leads)(also.start)

            @pl.when(jnp.logical_not(leads))
            def _():
                for load, store in zip(theirs, theirs_out):
                    load.wait()
                    store.start()

            for store, also in zip(kept_copies, ours_out):
                store.wait()
                also.wait()
        else:
            for value, source in ((1, a_ref), (0, b_ref)):

                @pl.when(flag_ref[0] == value)
                def _(source=source):
                    parts = [source.at[pl.ds(at, out.shape[0])] for at, out in zip(begins, outs)]
                    copy_through(parts, outs, *scratch)

    return pl.pallas_call(
        kernel,
        in_specs=[pl.BlockSpec(memory_space=pltpu.SMEM)]
        + [pl.BlockSpec(memory_space=pl.ANY)] * (2 + len(earlier)),
        out_specs=[pl.BlockSpec(memory_space=pl.ANY)] * (pieces + len(kept)),
        out_shape=[jax.ShapeDtypeStruct(shape, a.dtype) for shape in shapes + kept],
        scratch_shapes=copy_scratch(rows, cols) * (1 + len(kept)),
        compiler_params=pltpu.CompilerParams(vmem_limit_bytes=VMEM),
        cost_estimate=pl.CostEstimate(flops=0, bytes_accessed=2 * a.size * a.dtype.itemsize, transcendentals=0),
    )(flag, a, b, *earlier)


def join_call(earlier):
    def kernel(*refs):
        refs[-1][...] = jnp.zeros_like(refs[-1])

    return pl.pallas_call(
        kernel,
        in_specs=[pl.BlockSpec(memory_space=pl.ANY)] * len(earlier),
        out_specs=pl.BlockSpec(memory_space=pltpu.VMEM),
        out_shape=jax.ShapeDtypeStruct((8, 128), jnp.float32),
    )(*earlier)


def density_call(terms, parts, out_dtype, aux, earlier, rows=None, copied=None):
    count = len(terms)
    depth = terms[0][0].array.shape[1]
    extra = list(copied or [])
    whole = [jax.ShapeDtypeStruct((sum(x.shape[0] for x in extra), depth), jnp.bfloat16)] if extra else []
    pieces = [len(t[0].pieces) for t in terms]
    begins = [sum(pieces[:s]) for s in range(count)]
    cols = depth
    begin, length = rows or (0, aux)
    tile = 512
    while length % tile or begin % tile:
        tile //= 2
    steps = length // tile
    spans = []
    for part in parts:
        ends = np.cumsum([piece.shape[0] // tile for piece in part])
        shift = begin // tile if ends[-1] == aux // tile else 0
        spans.append([(int(end) - piece.shape[0] // tile - shift, int(end) - shift) for end, piece in zip(ends, part)])
    parts = [p for part in parts for p in part]

    def kernel(*refs):
        sources, refs = refs[: sum(pieces)], refs[sum(pieces) :]
        amps, refs = refs[:count], refs[count + len(earlier) :]
        source, refs = refs[: len(extra)], refs[len(extra) :]
        part_refs, out, refs = refs[: len(parts)], refs[len(parts)], refs[len(parts) + 1 :]
        target, refs = refs[: len(whole)], refs[len(whole) :]
        (left, right, left_sems, right_sems), scratch = refs[:4], refs[4:]
        step = pl.program_id(0)
        slot = step % 2

        def amp_copies():
            for s, (_, _, place) in enumerate(terms):
                yield pltpu.make_async_copy(
                    amps[s].at[place], right.at[:, pl.ds(s * depth, depth)], right_sems.at[s]
                )

        def slab_copies(which, start, of=range(count)):
            for s in of:
                end = 0
                for index in range(pieces[s]):
                    source = sources[begins[s] + index]
                    first = end
                    end += source.shape[0] // tile

                    def act(source=source, first=first, s=s):
                        row = pl.multiple_of((begin // tile + which - first) * tile, tile)
                        copy = pltpu.make_async_copy(
                            source.at[pl.ds(row, tile), :],
                            left.at[which % 2, :, pl.ds(s * depth, depth)],
                            left_sems.at[which % 2, s],
                        )
                        copy.start() if start else copy.wait()

                    at = begin // tile + which
                    if pieces[s] == 1:
                        act()
                    else:
                        pl.when(jnp.logical_and(at >= first, at < end))(act)

        @pl.when(step == 0)
        def _():
            for s, copy in enumerate(amp_copies()):
                copy.start()
                slab_copies(step, True, [s])
            if extra:
                for copy in copies_in(source, scratch[0], scratch[1]):
                    copy.start()

        @pl.when(step + 1 < steps)
        def _():
            slab_copies(step + 1, True)

        def finish(total):
            at = 0
            for span in spans:
                part = part_refs[at][...]
                for index in range(1, len(span)):
                    part = jnp.where(step >= span[index][0], part_refs[at + index][...], part)
                total = total + part.astype(jnp.float32)
                at += len(span)
            out[...] = total.astype(out.dtype)

        def product(a, b):
            return lax.dot_general(a, b, (((1,), (1,)), ((), ())), preferred_element_type=jnp.float32)

        @pl.when(step == 0)
        def _():
            total = None
            for s, copy in enumerate(amp_copies()):
                copy.wait()
                slab_copies(step, False, [s])
                at = pl.ds(s * depth, depth)
                term = product(left[0, :, at], right[:, at])
                total = term if total is None else total + term
            finish(total)

        @pl.when(step > 0)
        def _():
            slab_copies(step, False)
            finish(product(left[slot], right[...]))

        if extra:

            @pl.when(step == 1)
            def _():
                for copy in copies_in(source, scratch[0], scratch[1]):
                    copy.wait()
                for copy in copies_out(scratch[0], target, scratch[2]):
                    copy.start()

            @pl.when(step == steps - 1)
            def _():
                for copy in copies_out(scratch[0], target, scratch[2]):
                    copy.wait()

    def rows_of(start, end):
        return pl.BlockSpec((tile, cols), lambda i: (jnp.clip(i - start, 0, end - start - 1), 0))

    bytes_moved = 2 * count * (length * depth + cols * depth)
    bytes_moved += sum(length * cols * p.dtype.itemsize for p in parts)
    return pl.pallas_call(
        kernel,
        grid=(steps,),
        in_specs=[pl.BlockSpec(memory_space=pl.ANY)] * (sum(pieces) + count + len(earlier) + len(extra))
        + [rows_of(*ends) for span in spans for ends in span],
        out_specs=[pl.BlockSpec((tile, cols), lambda i: (i, 0))]
        + [pl.BlockSpec(memory_space=pl.ANY)] * len(whole),
        out_shape=[jax.ShapeDtypeStruct((length, cols), out_dtype)]
        + whole,
        scratch_shapes=[
            pltpu.VMEM((2, tile, count * depth), jnp.bfloat16),
            pltpu.VMEM((cols, count * depth), jnp.bfloat16),
            pltpu.SemaphoreType.DMA((2, count)),
            pltpu.SemaphoreType.DMA((count,)),
            *(copy_scratch(*whole[0].shape) if extra else []),
        ],
        compiler_params=pltpu.CompilerParams(vmem_limit_bytes=VMEM),
        cost_estimate=pl.CostEstimate(
            flops=2 * length * depth * cols * count,
            bytes_accessed=(bytes_moved + length * cols * jnp.dtype(out_dtype).itemsize),
            transcendentals=0,
        ),
    )(*[p for t in terms for p in t[0].pieces], *[t[1] for t in terms], *earlier, *extra, *parts)


def paired_plan(three_index, orbital_map, occ_energy, vir_energy, pair_kept):
    blocks = lax.axis_size("wide")
    routes = Routes(blocks)
    here = lax.axis_index("wide")
    side = lax.axis_index("narrow")
    aux, vir_count = three_index.shape[1:]

    def moved(slab, pairs):
        sent = [lax.ppermute(piece, "wide", pairs) for piece in slab.pieces]
        return Slab(sent, routes.moved(slab.ids, pairs), slab.far)

    def swapped(slab):
        return moved(slab, routes.swap)

    flag = jnp.asarray(np.array(routes.lead, np.int32))[here].reshape(1)

    def chosen(of_lead, of_other, *earlier, pieces=1):
        return Slab(
            choice_call(flag, of_lead.array, of_other.array, earlier, pieces),
            routes.either(of_lead.ids, of_other.ids),
            of_lead.far,
        )

    def sibling(array):
        return lax.ppermute(array, "narrow", [(0, 1), (1, 0)])

    plan = jnp.zeros((TAIL, vir_count), jnp.bfloat16)
    plan = plan.at[0, : ROUNDS + 1].set(pair_kept[:, 0].astype(jnp.bfloat16))
    own = Slab(append_call(three_index[0], plan), list(range(blocks)))

    r1 = moved(own, routes.rounds[0])
    split = choice_call(flag, own.array, own.array, [], pieces=2)
    own_far = Slab([sibling(piece) for piece in split], own.ids, 1)
    mate = swapped(own)

    labels = jnp.arange(occ_energy.shape[0], dtype=jnp.int32)
    picked = orbital_map[:, None] == labels[None, :]
    energy = jnp.sum(jnp.where(picked, occ_energy[None, :], 0.0), axis=1)

    def table_of(ids):
        ids = np.array(ids, np.int32).T
        places = np.arange(blocks)[:, None]
        back, forth = (places - ids) % blocks, (ids - places) % blocks
        behind = back <= ROUNDS
        known = np.stack([ids, np.where(behind, back, -1), np.where(behind, -1, forth)])
        block, mine, theirs = jnp.asarray(known.astype(np.int32))[:, here]
        places = jnp.arange(blocks, dtype=jnp.int32)[None, :]
        both = jnp.where(places == here, energy[None, :], 0.0)
        both = both + jnp.where(places == block[:, None], energy[None, :], 0.0)
        entries = jnp.arange(ROUNDS + 1, dtype=jnp.int32)[None, :]
        kept = pair_kept[:, 0].astype(jnp.float32)[None, :]
        weight = jnp.sum(jnp.where(entries == mine[:, None], kept, 0.0), axis=1)
        return jnp.stack([jnp.sum(both, axis=1), weight, theirs.astype(jnp.float32)], axis=1)

    vir = jnp.stack(
        [lax.dynamic_slice_in_dim(vir_energy, s * vir_count, vir_count) for s in (side, 1 - side)]
    )
    vir_rows, vir_cols = vir[:, :, None], vir[:, None, :]

    def moved_ids(ids_lead, ids_other, pairs):
        return routes.moved(routes.either(ids_lead, ids_other), pairs)

    def swapped_ids(ids):
        return routes.moved(ids, routes.swap)

    r2_ids = moved_ids(own.ids, r1.ids, routes.rounds[1])
    r3_ids = moved_ids(r2_ids, own.ids, routes.rounds[2])
    r4_ids = routes.moved(r3_ids, routes.rounds[3])
    r5_ids = routes.moved(own.ids, routes.rounds[4])
    all_ids = [own.ids, mate.ids]
    for ids in (r1.ids, r2_ids, r3_ids, r4_ids, r5_ids):
        all_ids += [ids, swapped_ids(ids)]
    table = table_of(all_ids)
    near, far = 0, 1
    rows_near = [own.array[:aux].T]
    stacks = {}

    def amps(jobs, turned, *earlier):
        lines = {slab: all_ids.index(slab.ids) for slab, _ in jobs}
        stack = amplitude_call(jobs, table, lines, turned, vir_rows, vir_cols, earlier)
        for place, job in enumerate(jobs):
            stacks[job] = (stack, place)
        return stack

    def density(slabs, block, parts, dtype, *earlier, rows=None, copied=None):
        terms = [(slab, *stacks[slab, block]) for slab in slabs]
        out, *copy = density_call(terms, parts, dtype, aux, earlier, rows, copied)
        return (out, *copy) if copy else out

    f32, bf16 = jnp.float32, jnp.bfloat16
    done = amps([(own, near), (mate, near)], [rows_near])

    sent, kept = choice_call(1 - flag, r1.array, own.array, [own_far.pieces[0], done], keep=True)
    r1 = Slab(kept, r1.ids)
    sent2 = Slab(sent, routes.either(own.ids, r1.ids))
    r2 = moved(sent2, routes.rounds[1])
    s1 = swapped(r1)
    done = amps([(r1, near), (s1, near)], [rows_near], sent2.array)
    part = density([own, mate, r1, s1], near, [], f32, done)

    sent, kept = choice_call(flag, r2.array, own.array, [part, *own_far.pieces], keep=True)
    r2 = Slab(kept, r2.ids)
    sent3 = Slab(sent, routes.either(r2.ids, own.ids))
    r3 = moved(sent3, routes.rounds[2])
    s2 = swapped(r2)
    mate_far = swapped(own_far)
    cut = own_far.pieces[0].shape[0]
    rows_far = [own_far.pieces[0].T, own_far.pieces[1][: aux - cut].T]
    jobs = [(r1, far), (s1, far), (r2, near), (r2, far), (s2, far), (s2, near)]
    jobs += [(own_far, near), (mate_far, near)]
    done = amps(jobs, [rows_near, rows_far], sent3.array)
    part = density([own_far, mate_far, r2, s2], near, [[part]], f32, done)

    r3 = chosen(r3, r3, part)
    r4 = moved(r3, routes.rounds[3])
    s3 = swapped(r3)
    out_part, again = density([r1, s1, r2, s2], far, [], f32, r3.array, copied=own.pieces)
    r5 = moved(Slab(again, own.ids), routes.rounds[4])
    jobs = [(r3, near), (r3, far), (s3, far), (s3, near)]
    done = amps(jobs, [rows_near, rows_far], out_part)

    done = amps([(r4, far)], [rows_near, rows_far], done)
    half = aux // 2
    slabs = [r3, s3, r4]
    sent0, again = density(
        slabs, far, [[out_part]], bf16, done, rows=(0, half), copied=own_far.pieces
    )
    r6 = moved(Slab(again, own.ids, 1), routes.rounds[4])
    sent1 = density(slabs, far, [[out_part]], bf16, sent0, rows=(half, half))
    incoming = [sibling(sent0), sibling(sent1)]
    done = amps([(r4, near)], [rows_near], sent1)
    part = density([r3, s3, r4], near, [[part]], f32, done)

    r5 = chosen(r5, r5, part, pieces=PIECES)
    s5 = swapped(r5)
    done = amps([(r5, near)], [rows_near], *r5.pieces)
    done = join_call([incoming[0], done])
    done = amps([(s5, near)], [rows_near], done)
    part = density([r5, s5], near, [[part]], f32, done)
    r6 = chosen(r6, r6, part, pieces=PIECES)
    s6 = swapped(r6)
    done = amps([(r6, near)], [rows_near], *r6.pieces)
    done = join_call([incoming[1], done])
    done = amps([(s6, near)], [rows_near], done)
    return density([r6, s6], near, [[part], incoming], f32, done)[None]


def solution(mesh):
    wide, narrow = mesh.shape["wide"], mesh.shape["narrow"]
    paired = narrow == 2 and wide % 4 == 0 and wide > 2 * ROUNDS + 1 and ROUNDS == 5

    def per_device(three_index, *rest):
        if paired and three_index.shape[0] == 1:
            return paired_plan(three_index, *rest)
        return ring_plan(three_index, *rest)

    placed = (P("wide", None, "narrow"), P(), P(), P(), P(None, "wide"))
    return jax.shard_map(
        per_device, mesh=mesh, in_specs=placed, out_specs=P("wide", None, "narrow"), check_vma=False
    )
```

```python
import jax
import jax.numpy as jnp
import numpy as np
from jax import lax
from jax.experimental import pallas as pl
from jax.experimental.pallas import tpu as pltpu
from jax.sharding import PartitionSpec as P

ROUNDS = 5
TAIL = 16
CHUNK = 512
PIECES = 3
VMEM = 24 * 1024 * 1024


def passed_along(array, axis, by):
    length = lax.axis_size(axis)
    return lax.ppermute(array, axis, [(i, (i + by) % length) for i in range(length)])


def block_energy(orbital_map, occ_energy, block_id, occ_count):
    orbits = lax.dynamic_slice_in_dim(orbital_map, block_id * occ_count, occ_count)
    labels = jnp.arange(occ_energy.shape[0], dtype=jnp.int32)
    chosen = orbits[:, None] == labels[None, :]
    return jnp.sum(jnp.where(chosen, occ_energy[None, :], 0.0), axis=1)


def amplitudes(gathered, visiting, left_energy, right_energy, vir_all, vir_local, weight):
    coulomb = jnp.einsum("ipa,jpb->ijab", gathered, visiting, preferred_element_type=jnp.float32)
    denominator = (vir_all[:, None] + vir_local[None, :])[None, None] - (
        left_energy[:, None] + right_energy[None, :]
    )[:, :, None, None]
    return (weight * coulomb / denominator).astype(jnp.bfloat16)


def ring_plan(three_index, orbital_map, occ_energy, vir_energy, pair_kept):
    occ_count = three_index.shape[0]
    vir_count = three_index.shape[2]
    blocks = lax.axis_size("wide")
    own_block = lax.axis_index("wide")
    vir_local = lax.dynamic_slice_in_dim(
        vir_energy, lax.axis_index("narrow") * vir_count, vir_count
    )
    own_energy = block_energy(orbital_map, occ_energy, own_block, occ_count)
    weights = pair_kept.astype(jnp.float32)
    gathered = lax.all_gather(three_index, "narrow", axis=2, tiled=True)
    amplitude = amplitudes(
        gathered, three_index, own_energy, own_energy, vir_energy, vir_local, weights[0, 0]
    )
    forward = jnp.einsum(
        "ijab,jpb->ipa", amplitude, three_index, preferred_element_type=jnp.float32
    )
    visiting = three_index
    stored_amps = []
    for round_index in range(1, ROUNDS + 1):
        visiting = passed_along(visiting, "wide", 1)
        partner = (own_block - round_index) % blocks
        partner_energy = block_energy(orbital_map, occ_energy, partner, occ_count)
        amplitude = amplitudes(
            gathered,
            visiting,
            own_energy,
            partner_energy,
            vir_energy,
            vir_local,
            weights[round_index, 0],
        )
        forward = forward + jnp.einsum(
            "ijab,jpb->ipa", amplitude, visiting, preferred_element_type=jnp.float32
        )
        stored_amps.append(amplitude)
    carried = None
    for round_index in range(1, ROUNDS + 1):
        backward = jnp.einsum(
            "ijab,ipa->jpb",
            stored_amps[round_index - 1],
            gathered,
            preferred_element_type=jnp.float32,
        )
        if round_index > 1:
            carried = passed_along(carried, "wide", 1) + backward
        else:
            carried = backward
    returned = passed_along(carried, "wide", -ROUNDS)
    scattered = lax.psum_scatter(forward, "narrow", scatter_dimension=2, tiled=True)
    return scattered + returned


class Routes:
    def __init__(self, blocks):
        self.blocks = blocks
        everyone = range(blocks)
        self.lead = [self.place(w)[1] == self.place(w)[2] for w in everyone]
        self.swap = [(w, w ^ 1) for w in everyone]
        onward = [(w, self.along_z(w, 1)) for w in everyone]
        backward = [(w, self.along_z(w, -1)) for w in everyone]
        across = [(w, self.across_x(w)) for w in everyone]
        self.rounds = [
            self.either(across, onward),
            self.either(onward, across),
            self.either(across, backward),
            self.either(backward, across),
            self.either(backward, across),
        ]

    def place(self, w):
        return w // 4, (w // 2) % 2, w % 2

    def along_z(self, w, step):
        z, x, core = self.place(w)
        z = (z + (step if x == 1 else -step)) % (self.blocks // 4)
        return (z * 2 + x) * 2 + core

    def across_x(self, w):
        z, x, core = self.place(w)
        return (z * 2 + 1 - x) * 2 + 1 - core

    def either(self, of_lead, of_other):
        return [a if lead else b for lead, a, b in zip(self.lead, of_lead, of_other)]

    def moved(self, ids, pairs):
        out = [0] * self.blocks
        for source, target in pairs:
            out[target] = ids[source]
        return out


class Slab:
    def __init__(self, array, ids, far=0):
        self.pieces = list(array) if isinstance(array, (list, tuple)) else [array]
        self.array = self.pieces[0]
        self.ids = ids
        self.far = far


def pick(step, values):
    out = values[0]
    for index, value in enumerate(values):
        if index and value != values[0]:
            out = jnp.where(step == index, value, out)
    return out


def amplitude_call(jobs, table, lines, turned, vir_rows, vir_cols, earlier):
    slabs = []
    for slab, _ in jobs:
        if slab not in slabs:
            slabs.append(slab)
    count, blocks = len(slabs), len(turned)
    cols, aux = turned[0][0].shape[0], sum(piece.shape[1] for piece in turned[0])
    held_rows = aux + TAIL
    pieces = [len(slab.pieces) for slab in slabs]
    begins = [sum(pieces[:s]) for s in range(count)]
    of_job = [slabs.index(slab) for slab, _ in jobs]
    block_of = [block for _, block in jobs]
    far_of = [slab.far for slab, _ in jobs]
    line_of = [lines[slab] for slab, _ in jobs]
    row_pieces = [len(block) for block in turned]
    chunks = aux // CHUNK
    opens = [t for t in range(len(jobs)) if t == 0 or of_job[t] != of_job[t - 1]]
    half = cols // 2

    def kernel(scalars, *refs):
        sources, refs = refs[: sum(pieces)], refs[sum(pieces) :]
        row_sources, refs = refs[: sum(row_pieces)], refs[sum(row_pieces) + len(earlier) :]
        vir_row, vir_col, out, held, rows, held_sems, row_sems = refs
        step = pl.program_id(0)

        def slab_copies(s):
            row = 0
            for index in range(pieces[s]):
                source = sources[begins[s] + index]
                for begin, size in chunks_of(source.shape[0]):
                    target = held.at[s % 2, pl.ds(row, size), :]
                    yield pltpu.make_async_copy(
                        source.at[pl.ds(begin, size)], target, held_sems.at[s % 2, row // CHUNK]
                    )
                    row += size

        def row_copies(block):
            column = 0
            for source in row_sources[sum(row_pieces[:block]) : sum(row_pieces[: block + 1])]:
                for begin, size in chunks_of(source.shape[1]):
                    target = rows.at[block, :, pl.ds(column, size)]
                    yield pltpu.make_async_copy(
                        source.at[:, pl.ds(begin, size)], target, row_sems.at[block, column // CHUNK]
                    )
                    column += size

        @pl.when(step == 0)
        def _():
            for pair in zip(slab_copies(0), row_copies(block_of[0])):
                for copy in pair:
                    copy.start()
            for copy in list(slab_copies(0))[chunks:]:
                copy.start()
            for block in list(dict.fromkeys(block_of))[1:]:
                for copy in row_copies(block):
                    copy.start()

        for s, t in enumerate(opens):

            @pl.when(step == t)
            def _(s=s):
                if s:
                    for copy in slab_copies(s):
                        copy.wait()
                if s + 1 < count:
                    for copy in slab_copies(s + 1):
                        copy.start()

        for block in list(dict.fromkeys(block_of))[1:]:

            @pl.when(step == block_of.index(block))
            def _(block=block):
                for copy in row_copies(block):
                    copy.wait()

        slot = pick(step, [s % 2 for s in of_job])
        block = pick(step, block_of)
        line = pick(step, line_of)
        @pl.when(step == 0)
        def _():
            for copy in list(slab_copies(0))[chunks:]:
                copy.wait()

        plan = held[slot, aux:, :128].astype(jnp.float32)
        lane = lax.broadcasted_iota(jnp.int32, plan.shape, 1).astype(jnp.float32)
        row = lax.broadcasted_iota(jnp.int32, plan.shape, 0)
        told = jnp.where(jnp.logical_and(row == 0, lane == scalars[line, 2]), plan, 0.0)
        weight = scalars[line, 1] + jnp.sum(told, keepdims=True)

        def finish(part, coulomb):
            denominator = (vir_row[0] + vir_col[0, :, part]) - scalars[line, 0]
            out[0, :, part] = (weight * coulomb / denominator).astype(out.dtype)

        @pl.when(step == 0)
        def _():
            coulomb = None
            for index, pair in enumerate(zip(row_copies(block_of[0]), slab_copies(0))):
                for copy in pair:
                    copy.wait()
                chunk = pl.ds(index * CHUNK, CHUNK)
                term = jnp.dot(
                    rows[block_of[0], :, chunk], held[0, chunk, :], preferred_element_type=jnp.float32
                )
                coulomb = term if coulomb is None else coulomb + term
            finish(pl.ds(0, cols), coulomb)

        @pl.when(step > 0)
        def _():
            for begin in range(0, cols, half):
                part = pl.ds(begin, half)
                finish(part, jnp.dot(rows[block], held[slot, :aux, part], preferred_element_type=jnp.float32))

    return pl.pallas_call(
        kernel,
        grid=(len(jobs),),
        in_specs=[pl.BlockSpec(memory_space=pltpu.SMEM)]
        + [pl.BlockSpec(memory_space=pl.ANY)] * (sum(pieces) + sum(row_pieces) + len(earlier))
        + [
            pl.BlockSpec((1, cols, 1), lambda t: (pick(t, block_of), 0, 0)),
            pl.BlockSpec((1, 1, cols), lambda t: (pick(t, far_of), 0, 0)),
        ],
        out_specs=pl.BlockSpec((1, cols, cols), lambda t: (t, 0, 0)),
        out_shape=jax.ShapeDtypeStruct((len(jobs), cols, cols), jnp.bfloat16),
        scratch_shapes=[
            pltpu.VMEM((2, held_rows, cols), jnp.bfloat16),
            pltpu.VMEM((blocks, cols, aux), jnp.bfloat16),
            pltpu.SemaphoreType.DMA((2, chunks + 1)),
            pltpu.SemaphoreType.DMA((blocks, chunks)),
        ],
        compiler_params=pltpu.CompilerParams(vmem_limit_bytes=VMEM),
        cost_estimate=pl.CostEstimate(
            flops=2 * len(jobs) * cols * aux * cols,
            bytes_accessed=2 * cols * (blocks * aux + count * aux + len(jobs) * cols),
            transcendentals=0,
        ),
    )(table, *[p for s in slabs for p in s.pieces], *[p for b in turned for p in b], *earlier, vir_rows, vir_cols)


def chunks_of(rows):
    return [(begin, min(CHUNK, rows - begin)) for begin in range(0, rows, CHUNK)]


def copies_in(sources, held, sems):
    row, index = 0, 0
    for source in sources:
        for begin, size in chunks_of(source.shape[0]):
            yield pltpu.make_async_copy(
                source.at[pl.ds(begin, size)], held.at[pl.ds(row + begin, size)], sems.at[index]
            )
            index += 1
        row += source.shape[0]


def copies_out(held, targets, sems):
    row, index = 0, 0
    for target in targets:
        for begin, size in chunks_of(target.shape[0]):
            yield pltpu.make_async_copy(
                held.at[pl.ds(row + begin, size)], target.at[pl.ds(begin, size)], sems.at[index]
            )
            index += 1
        row += target.shape[0]


def copy_scratch(rows, cols):
    count = len(chunks_of(rows)) + 1
    return [
        pltpu.VMEM((rows, cols), jnp.bfloat16),
        pltpu.SemaphoreType.DMA((count,)),
        pltpu.SemaphoreType.DMA((count,)),
    ]


def copy_through(sources, targets, held, in_sems, out_sems):
    if [x.shape[0] for x in sources] != [x.shape[0] for x in targets]:
        loads, stores = [list(copies_in(sources, held, in_sems))], [list(copies_out(held, targets, out_sems))]
    else:
        loads = [[copy] for copy in copies_in(sources, held, in_sems)]
        stores = [[copy] for copy in copies_out(held, targets, out_sems)]
    for copies in loads:
        for copy in copies:
            copy.start()
    for before, behind in zip(loads, stores):
        for copy in before:
            copy.wait()
        for copy in behind:
            copy.start()
    for copies in stores:
        for copy in copies:
            copy.wait()


def append_call(array, tail):
    def kernel(array_ref, tail_ref, out, held, in_sems, out_sems):
        rows = array_ref.shape[0]
        targets = [out.at[pl.ds(0, rows)], out.at[pl.ds(rows, tail_ref.shape[0])]]
        copy_through([array_ref, tail_ref], targets, held, in_sems, out_sems)

    rows, cols = array.shape[0] + tail.shape[0], array.shape[1]
    return pl.pallas_call(
        kernel,
        in_specs=[pl.BlockSpec(memory_space=pl.ANY)] * 2,
        out_specs=pl.BlockSpec(memory_space=pl.ANY),
        out_shape=jax.ShapeDtypeStruct((rows, cols), array.dtype),
        scratch_shapes=copy_scratch(rows, cols),
        compiler_params=pltpu.CompilerParams(vmem_limit_bytes=VMEM),
    )(array, tail)


def choice_call(flag, a, b, earlier, pieces=1, keep=False):
    rows, cols = a.shape
    size = rows // pieces // CHUNK * CHUNK if pieces > 1 else rows
    begins = [index * size for index in range(pieces)] + [rows]
    shapes = [(end - begin, cols) for begin, end in zip(begins, begins[1:])]
    kept = [(rows, cols)] if keep else []

    def kernel(flag_ref, a_ref, b_ref, *refs):
        refs = refs[len(earlier) :]
        outs, kept_outs, scratch = refs[:pieces], refs[pieces : pieces + len(kept)], refs[pieces + len(kept) :]
        if keep:
            held, loads, stores, other_held, other_loads, other_stores = scratch
            leads = flag_ref[0] == 1
            ours = list(copies_in([a_ref], held, loads))
            theirs = list(copies_in([b_ref], other_held, other_loads))
            kept_copies = list(copies_out(held, kept_outs, stores))
            ours_out = list(copies_out(held, outs, other_stores))
            theirs_out = list(copies_out(other_held, outs, other_stores))
            for copy in ours:
                copy.start()

            @pl.when(jnp.logical_not(leads))
            def _():
                for copy in theirs:
                    copy.start()

            for load, store, also in zip(ours, kept_copies, ours_out):
                load.wait()
                store.start()
                pl.when(leads)(also.start)

            @pl.when(jnp.logical_not(leads))
            def _():
                for load, store in zip(theirs, theirs_out):
                    load.wait()
                    store.start()

            for store, also in zip(kept_copies, ours_out):
                store.wait()
                also.wait()
        else:
            for value, source in ((1, a_ref), (0, b_ref)):

                @pl.when(flag_ref[0] == value)
                def _(source=source):
                    parts = [source.at[pl.ds(at, out.shape[0])] for at, out in zip(begins, outs)]
                    copy_through(parts, outs, *scratch)

    return pl.pallas_call(
        kernel,
        in_specs=[pl.BlockSpec(memory_space=pltpu.SMEM)]
        + [pl.BlockSpec(memory_space=pl.ANY)] * (2 + len(earlier)),
        out_specs=[pl.BlockSpec(memory_space=pl.ANY)] * (pieces + len(kept)),
        out_shape=[jax.ShapeDtypeStruct(shape, a.dtype) for shape in shapes + kept],
        scratch_shapes=copy_scratch(rows, cols) * (1 + len(kept)),
        compiler_params=pltpu.CompilerParams(vmem_limit_bytes=VMEM),
        cost_estimate=pl.CostEstimate(flops=0, bytes_accessed=2 * a.size * a.dtype.itemsize, transcendentals=0),
    )(flag, a, b, *earlier)


def join_call(earlier):
    def kernel(*refs):
        refs[-1][...] = jnp.zeros_like(refs[-1])

    return pl.pallas_call(
        kernel,
        in_specs=[pl.BlockSpec(memory_space=pl.ANY)] * len(earlier),
        out_specs=pl.BlockSpec(memory_space=pltpu.VMEM),
        out_shape=jax.ShapeDtypeStruct((8, 128), jnp.float32),
    )(*earlier)


def density_call(terms, parts, out_dtype, aux, earlier, rows=None, copied=None):
    count = len(terms)
    depth = terms[0][0].array.shape[1]
    extra = list(copied or [])
    whole = [jax.ShapeDtypeStruct((sum(x.shape[0] for x in extra), depth), jnp.bfloat16)] if extra else []
    pieces = [len(t[0].pieces) for t in terms]
    begins = [sum(pieces[:s]) for s in range(count)]
    cols = depth
    begin, length = rows or (0, aux)
    tile = 512
    while length % tile or begin % tile:
        tile //= 2
    steps = length // tile
    spans = []
    for part in parts:
        ends = np.cumsum([piece.shape[0] // tile for piece in part])
        shift = begin // tile if ends[-1] == aux // tile else 0
        spans.append([(int(end) - piece.shape[0] // tile - shift, int(end) - shift) for end, piece in zip(ends, part)])
    parts = [p for part in parts for p in part]

    def kernel(*refs):
        sources, refs = refs[: sum(pieces)], refs[sum(pieces) :]
        amps, refs = refs[:count], refs[count + len(earlier) :]
        source, refs = refs[: len(extra)], refs[len(extra) :]
        part_refs, out, refs = refs[: len(parts)], refs[len(parts)], refs[len(parts) + 1 :]
        target, refs = refs[: len(whole)], refs[len(whole) :]
        (left, right, left_sems, right_sems), scratch = refs[:4], refs[4:]
        step = pl.program_id(0)
        slot = step % 2

        def amp_copies():
            for s, (_, _, place) in enumerate(terms):
                yield pltpu.make_async_copy(
                    amps[s].at[place], right.at[:, pl.ds(s * depth, depth)], right_sems.at[s]
                )

        def slab_copies(which, start, of=range(count)):
            for s in of:
                end = 0
                for index in range(pieces[s]):
                    source = sources[begins[s] + index]
                    first = end
                    end += source.shape[0] // tile

                    def act(source=source, first=first, s=s):
                        row = pl.multiple_of((begin // tile + which - first) * tile, tile)
                        copy = pltpu.make_async_copy(
                            source.at[pl.ds(row, tile), :],
                            left.at[which % 2, :, pl.ds(s * depth, depth)],
                            left_sems.at[which % 2, s],
                        )
                        copy.start() if start else copy.wait()

                    at = begin // tile + which
                    if pieces[s] == 1:
                        act()
                    else:
                        pl.when(jnp.logical_and(at >= first, at < end))(act)

        @pl.when(step == 0)
        def _():
            for s, copy in enumerate(amp_copies()):
                copy.start()
                slab_copies(step, True, [s])
            if extra:
                for copy in copies_in(source, scratch[0], scratch[1]):
                    copy.start()

        @pl.when(step + 1 < steps)
        def _():
            slab_copies(step + 1, True)

        def finish(total):
            at = 0
            for span in spans:
                part = part_refs[at][...]
                for index in range(1, len(span)):
                    part = jnp.where(step >= span[index][0], part_refs[at + index][...], part)
                total = total + part.astype(jnp.float32)
                at += len(span)
            out[...] = total.astype(out.dtype)

        def product(a, b):
            return lax.dot_general(a, b, (((1,), (1,)), ((), ())), preferred_element_type=jnp.float32)

        @pl.when(step == 0)
        def _():
            total = None
            for s, copy in enumerate(amp_copies()):
                copy.wait()
                slab_copies(step, False, [s])
                at = pl.ds(s * depth, depth)
                term = product(left[0, :, at], right[:, at])
                total = term if total is None else total + term
            finish(total)

        @pl.when(step > 0)
        def _():
            slab_copies(step, False)
            finish(product(left[slot], right[...]))

        if extra:

            @pl.when(step == 1)
            def _():
                for copy in copies_in(source, scratch[0], scratch[1]):
                    copy.wait()
                for copy in copies_out(scratch[0], target, scratch[2]):
                    copy.start()

            @pl.when(step == steps - 1)
            def _():
                for copy in copies_out(scratch[0], target, scratch[2]):
                    copy.wait()

    def rows_of(start, end):
        return pl.BlockSpec((tile, cols), lambda i: (jnp.clip(i - start, 0, end - start - 1), 0))

    bytes_moved = 2 * count * (length * depth + cols * depth)
    bytes_moved += sum(length * cols * p.dtype.itemsize for p in parts)
    return pl.pallas_call(
        kernel,
        grid=(steps,),
        in_specs=[pl.BlockSpec(memory_space=pl.ANY)] * (sum(pieces) + count + len(earlier) + len(extra))
        + [rows_of(*ends) for span in spans for ends in span],
        out_specs=[pl.BlockSpec((tile, cols), lambda i: (i, 0))]
        + [pl.BlockSpec(memory_space=pl.ANY)] * len(whole),
        out_shape=[jax.ShapeDtypeStruct((length, cols), out_dtype)]
        + whole,
        scratch_shapes=[
            pltpu.VMEM((2, tile, count * depth), jnp.bfloat16),
            pltpu.VMEM((cols, count * depth), jnp.bfloat16),
            pltpu.SemaphoreType.DMA((2, count)),
            pltpu.SemaphoreType.DMA((count,)),
            *(copy_scratch(*whole[0].shape) if extra else []),
        ],
        compiler_params=pltpu.CompilerParams(vmem_limit_bytes=VMEM),
        cost_estimate=pl.CostEstimate(
            flops=2 * length * depth * cols * count,
            bytes_accessed=(bytes_moved + length * cols * jnp.dtype(out_dtype).itemsize),
            transcendentals=0,
        ),
    )(*[p for t in terms for p in t[0].pieces], *[t[1] for t in terms], *earlier, *extra, *parts)


def paired_plan(three_index, orbital_map, occ_energy, vir_energy, pair_kept):
    blocks = lax.axis_size("wide")
    routes = Routes(blocks)
    here = lax.axis_index("wide")
    side = lax.axis_index("narrow")
    aux, vir_count = three_index.shape[1:]

    def moved(slab, pairs):
        sent = [lax.ppermute(piece, "wide", pairs) for piece in slab.pieces]
        return Slab(sent, routes.moved(slab.ids, pairs), slab.far)

    def swapped(slab):
        return moved(slab, routes.swap)

    flag = jnp.asarray(np.array(routes.lead, np.int32))[here].reshape(1)

    def chosen(of_lead, of_other, *earlier, pieces=1):
        return Slab(
            choice_call(flag, of_lead.array, of_other.array, earlier, pieces),
            routes.either(of_lead.ids, of_other.ids),
            of_lead.far,
        )

    def sibling(array):
        return lax.ppermute(array, "narrow", [(0, 1), (1, 0)])

    plan = jnp.zeros((TAIL, vir_count), jnp.bfloat16)
    plan = plan.at[0, : ROUNDS + 1].set(pair_kept[:, 0].astype(jnp.bfloat16))
    own = Slab(append_call(three_index[0], plan), list(range(blocks)))

    r1 = moved(own, routes.rounds[0])
    split = choice_call(flag, own.array, own.array, [], pieces=2)
    own_far = Slab([sibling(piece) for piece in split], own.ids, 1)
    mate = swapped(own)

    labels = jnp.arange(occ_energy.shape[0], dtype=jnp.int32)
    picked = orbital_map[:, None] == labels[None, :]
    energy = jnp.sum(jnp.where(picked, occ_energy[None, :], 0.0), axis=1)

    def table_of(ids):
        ids = np.array(ids, np.int32).T
        places = np.arange(blocks)[:, None]
        back, forth = (places - ids) % blocks, (ids - places) % blocks
        behind = back <= ROUNDS
        known = np.stack([ids, np.where(behind, back, -1), np.where(behind, -1, forth)])
        block, mine, theirs = jnp.asarray(known.astype(np.int32))[:, here]
        places = jnp.arange(blocks, dtype=jnp.int32)[None, :]
        both = jnp.where(places == here, energy[None, :], 0.0)
        both = both + jnp.where(places == block[:, None], energy[None, :], 0.0)
        entries = jnp.arange(ROUNDS + 1, dtype=jnp.int32)[None, :]
        kept = pair_kept[:, 0].astype(jnp.float32)[None, :]
        weight = jnp.sum(jnp.where(entries == mine[:, None], kept, 0.0), axis=1)
        return jnp.stack([jnp.sum(both, axis=1), weight, theirs.astype(jnp.float32)], axis=1)

    vir = jnp.stack(
        [lax.dynamic_slice_in_dim(vir_energy, s * vir_count, vir_count) for s in (side, 1 - side)]
    )
    vir_rows, vir_cols = vir[:, :, None], vir[:, None, :]

    def moved_ids(ids_lead, ids_other, pairs):
        return routes.moved(routes.either(ids_lead, ids_other), pairs)

    def swapped_ids(ids):
        return routes.moved(ids, routes.swap)

    r2_ids = moved_ids(own.ids, r1.ids, routes.rounds[1])
    r3_ids = moved_ids(r2_ids, own.ids, routes.rounds[2])
    r4_ids = routes.moved(r3_ids, routes.rounds[3])
    r5_ids = routes.moved(own.ids, routes.rounds[4])
    all_ids = [own.ids, mate.ids]
    for ids in (r1.ids, r2_ids, r3_ids, r4_ids, r5_ids):
        all_ids += [ids, swapped_ids(ids)]
    table = table_of(all_ids)
    near, far = 0, 1
    rows_near = [own.array[:aux].T]
    stacks = {}

    def amps(jobs, turned, *earlier):
        lines = {slab: all_ids.index(slab.ids) for slab, _ in jobs}
        stack = amplitude_call(jobs, table, lines, turned, vir_rows, vir_cols, earlier)
        for place, job in enumerate(jobs):
            stacks[job] = (stack, place)
        return stack

    def density(slabs, block, parts, dtype, *earlier, rows=None, copied=None):
        terms = [(slab, *stacks[slab, block]) for slab in slabs]
        out, *copy = density_call(terms, parts, dtype, aux, earlier, rows, copied)
        return (out, *copy) if copy else out

    f32, bf16 = jnp.float32, jnp.bfloat16
    done = amps([(own, near), (mate, near)], [rows_near])

    sent, kept = choice_call(1 - flag, r1.array, own.array, [own_far.pieces[0], done], keep=True)
    r1 = Slab(kept, r1.ids)
    sent2 = Slab(sent, routes.either(own.ids, r1.ids))
    r2 = moved(sent2, routes.rounds[1])
    s1 = swapped(r1)
    done = amps([(r1, near), (s1, near)], [rows_near], sent2.array)
    part = density([own, mate, r1, s1], near, [], f32, done)

    sent, kept = choice_call(flag, r2.array, own.array, [part, *own_far.pieces], keep=True)
    r2 = Slab(kept, r2.ids)
    sent3 = Slab(sent, routes.either(r2.ids, own.ids))
    r3 = moved(sent3, routes.rounds[2])
    s2 = swapped(r2)
    mate_far = swapped(own_far)
    cut = own_far.pieces[0].shape[0]
    rows_far = [own_far.pieces[0].T, own_far.pieces[1][: aux - cut].T]
    jobs = [(r1, far), (s1, far), (r2, near), (r2, far), (s2, far), (s2, near)]
    jobs += [(own_far, near), (mate_far, near)]
    done = amps(jobs, [rows_near, rows_far], sent3.array)
    part = density([own_far, mate_far, r2, s2], near, [[part]], f32, done)

    r3 = chosen(r3, r3, part)
    r4 = moved(r3, routes.rounds[3])
    s3 = swapped(r3)
    out_part, again = density([r1, s1, r2, s2], far, [], f32, r3.array, copied=own.pieces)
    r5 = moved(Slab(again, own.ids), routes.rounds[4])
    jobs = [(r3, near), (r3, far), (s3, far), (s3, near)]
    done = amps(jobs, [rows_near, rows_far], out_part)

    done = amps([(r4, far)], [rows_near, rows_far], done)
    half = aux // 2
    slabs = [r3, s3, r4]
    sent0, again = density(
        slabs, far, [[out_part]], bf16, done, rows=(0, half), copied=own_far.pieces
    )
    r6 = moved(Slab(again, own.ids, 1), routes.rounds[4])
    sent1 = density(slabs, far, [[out_part]], bf16, sent0, rows=(half, half))
    incoming = [sibling(sent0), sibling(sent1)]
    done = amps([(r4, near)], [rows_near], sent1)
    part = density([r3, s3, r4], near, [[part]], f32, done)

    r5 = chosen(r5, r5, part, pieces=PIECES)
    s5 = swapped(r5)
    done = amps([(r5, near)], [rows_near], *r5.pieces)
    done = join_call([incoming[0], done])
    done = amps([(s5, near)], [rows_near], done)
    part = density([r5, s5], near, [[part]], f32, done)
    r6 = chosen(r6, r6, part, pieces=PIECES)
    s6 = swapped(r6)
    done = amps([(r6, near)], [rows_near], *r6.pieces)
    done = join_call([incoming[1], done])
    done = amps([(s6, near)], [rows_near], done)
    return density([r6, s6], near, [[part], incoming], f32, done)[None]


def solution(mesh):
    wide, narrow = mesh.shape["wide"], mesh.shape["narrow"]
    paired = narrow == 2 and wide % 4 == 0 and wide > 2 * ROUNDS + 1 and ROUNDS == 5

    def per_device(three_index, *rest):
        if paired and three_index.shape[0] == 1:
            return paired_plan(three_index, *rest)
        return ring_plan(three_index, *rest)

    placed = (P("wide", None, "narrow"), P(), P(), P(), P(None, "wide"))
    return jax.shard_map(
        per_device, mesh=mesh, in_specs=placed, out_specs=P("wide", None, "narrow"), check_vma=False
    )
```

```python
import jax
import jax.numpy as jnp
import numpy as np
from jax import lax
from jax.experimental import pallas as pl
from jax.experimental.pallas import tpu as pltpu
from jax.sharding import PartitionSpec as P

ROUNDS = 5
TAIL = 16
CHUNK = 512
VMEM = 24 * 1024 * 1024


def passed_along(array, axis, by):
    length = lax.axis_size(axis)
    return lax.ppermute(array, axis, [(i, (i + by) % length) for i in range(length)])


def block_energy(orbital_map, occ_energy, block_id, occ_count):
    orbits = lax.dynamic_slice_in_dim(orbital_map, block_id * occ_count, occ_count)
    labels = jnp.arange(occ_energy.shape[0], dtype=jnp.int32)
    chosen = orbits[:, None] == labels[None, :]
    return jnp.sum(jnp.where(chosen, occ_energy[None, :], 0.0), axis=1)


def amplitudes(gathered, visiting, left_energy, right_energy, vir_all, vir_local, weight):
    coulomb = jnp.einsum("ipa,jpb->ijab", gathered, visiting, preferred_element_type=jnp.float32)
    denominator = (vir_all[:, None] + vir_local[None, :])[None, None] - (
        left_energy[:, None] + right_energy[None, :]
    )[:, :, None, None]
    return (weight * coulomb / denominator).astype(jnp.bfloat16)


def ring_plan(three_index, orbital_map, occ_energy, vir_energy, pair_kept):
    occ_count = three_index.shape[0]
    vir_count = three_index.shape[2]
    blocks = lax.axis_size("wide")
    own_block = lax.axis_index("wide")
    vir_local = lax.dynamic_slice_in_dim(
        vir_energy, lax.axis_index("narrow") * vir_count, vir_count
    )
    own_energy = block_energy(orbital_map, occ_energy, own_block, occ_count)
    weights = pair_kept.astype(jnp.float32)
    gathered = lax.all_gather(three_index, "narrow", axis=2, tiled=True)
    amplitude = amplitudes(
        gathered, three_index, own_energy, own_energy, vir_energy, vir_local, weights[0, 0]
    )
    forward = jnp.einsum(
        "ijab,jpb->ipa", amplitude, three_index, preferred_element_type=jnp.float32
    )
    visiting = three_index
    stored_amps = []
    for round_index in range(1, ROUNDS + 1):
        visiting = passed_along(visiting, "wide", 1)
        partner = (own_block - round_index) % blocks
        partner_energy = block_energy(orbital_map, occ_energy, partner, occ_count)
        amplitude = amplitudes(
            gathered,
            visiting,
            own_energy,
            partner_energy,
            vir_energy,
            vir_local,
            weights[round_index, 0],
        )
        forward = forward + jnp.einsum(
            "ijab,jpb->ipa", amplitude, visiting, preferred_element_type=jnp.float32
        )
        stored_amps.append(amplitude)
    carried = None
    for round_index in range(1, ROUNDS + 1):
        backward = jnp.einsum(
            "ijab,ipa->jpb",
            stored_amps[round_index - 1],
            gathered,
            preferred_element_type=jnp.float32,
        )
        if round_index > 1:
            carried = passed_along(carried, "wide", 1) + backward
        else:
            carried = backward
    returned = passed_along(carried, "wide", -ROUNDS)
    scattered = lax.psum_scatter(forward, "narrow", scatter_dimension=2, tiled=True)
    return scattered + returned


class Routes:
    def __init__(self, blocks):
        self.blocks = blocks
        everyone = range(blocks)
        self.lead = [self.place(w)[1] == self.place(w)[2] for w in everyone]
        self.swap = [(w, w ^ 1) for w in everyone]
        onward = [(w, self.along_z(w, 1)) for w in everyone]
        backward = [(w, self.along_z(w, -1)) for w in everyone]
        across = [(w, self.across_x(w)) for w in everyone]
        self.rounds = [
            self.either(across, onward),
            self.either(onward, across),
            self.either(across, backward),
            self.either(backward, across),
            self.either(backward, across),
        ]

    def place(self, w):
        return w // 4, (w // 2) % 2, w % 2

    def along_z(self, w, step):
        z, x, core = self.place(w)
        z = (z + (step if x == 1 else -step)) % (self.blocks // 4)
        return (z * 2 + x) * 2 + core

    def across_x(self, w):
        z, x, core = self.place(w)
        return (z * 2 + 1 - x) * 2 + 1 - core

    def either(self, of_lead, of_other):
        return [a if lead else b for lead, a, b in zip(self.lead, of_lead, of_other)]

    def moved(self, ids, pairs):
        out = [0] * self.blocks
        for source, target in pairs:
            out[target] = ids[source]
        return out


class Slab:
    def __init__(self, array, ids, far=0):
        self.pieces = list(array) if isinstance(array, (list, tuple)) else [array]
        self.array = self.pieces[0]
        self.ids = ids
        self.far = far


def pick(step, values):
    out = values[0]
    for index, value in enumerate(values):
        if index and value != values[0]:
            out = jnp.where(step == index, value, out)
    return out


def amplitude_call(jobs, table, lines, turned, vir_rows, vir_cols, earlier):
    slabs = []
    for slab, _ in jobs:
        if slab not in slabs:
            slabs.append(slab)
    count, blocks = len(slabs), len(turned)
    cols, aux = turned[0][0].shape[0], sum(piece.shape[1] for piece in turned[0])
    held_rows = aux + TAIL
    pieces = [len(slab.pieces) for slab in slabs]
    begins = [sum(pieces[:s]) for s in range(count)]
    of_job = [slabs.index(slab) for slab, _ in jobs]
    block_of = [block for _, block in jobs]
    far_of = [slab.far for slab, _ in jobs]
    line_of = [lines[slab] for slab, _ in jobs]
    row_pieces = [len(block) for block in turned]
    chunks = aux // CHUNK
    opens = [t for t in range(len(jobs)) if t == 0 or of_job[t] != of_job[t - 1]]
    half = cols // 2

    def kernel(scalars, *refs):
        sources, refs = refs[: sum(pieces)], refs[sum(pieces) :]
        row_sources, refs = refs[: sum(row_pieces)], refs[sum(row_pieces) + len(earlier) :]
        vir_row, vir_col, out, held, rows, held_sems, row_sems = refs
        step = pl.program_id(0)

        def slab_copies(s):
            row = 0
            for index in range(pieces[s]):
                source = sources[begins[s] + index]
                for begin, size in chunks_of(source.shape[0]):
                    target = held.at[s % 2, pl.ds(row, size), :]
                    yield pltpu.make_async_copy(
                        source.at[pl.ds(begin, size)], target, held_sems.at[s % 2, row // CHUNK]
                    )
                    row += size

        def row_copies(block):
            column = 0
            for source in row_sources[sum(row_pieces[:block]) : sum(row_pieces[: block + 1])]:
                for begin, size in chunks_of(source.shape[1]):
                    target = rows.at[block, :, pl.ds(column, size)]
                    yield pltpu.make_async_copy(
                        source.at[:, pl.ds(begin, size)], target, row_sems.at[block, column // CHUNK]
                    )
                    column += size

        @pl.when(step == 0)
        def _():
            for pair in zip(slab_copies(0), row_copies(block_of[0])):
                for copy in pair:
                    copy.start()
            for copy in list(slab_copies(0))[chunks:]:
                copy.start()
            for block in list(dict.fromkeys(block_of))[1:]:
                for copy in row_copies(block):
                    copy.start()

        for s, t in enumerate(opens):

            @pl.when(step == t)
            def _(s=s):
                if s:
                    for copy in slab_copies(s):
                        copy.wait()
                if s + 1 < count:
                    for copy in slab_copies(s + 1):
                        copy.start()

        for block in list(dict.fromkeys(block_of))[1:]:

            @pl.when(step == block_of.index(block))
            def _(block=block):
                for copy in row_copies(block):
                    copy.wait()

        slot = pick(step, [s % 2 for s in of_job])
        block = pick(step, block_of)
        line = pick(step, line_of)
        @pl.when(step == 0)
        def _():
            for copy in list(slab_copies(0))[chunks:]:
                copy.wait()

        plan = held[slot, aux:, :128].astype(jnp.float32)
        lane = lax.broadcasted_iota(jnp.int32, plan.shape, 1).astype(jnp.float32)
        row = lax.broadcasted_iota(jnp.int32, plan.shape, 0)
        told = jnp.where(jnp.logical_and(row == 0, lane == scalars[line, 2]), plan, 0.0)
        weight = scalars[line, 1] + jnp.sum(told, keepdims=True)

        def finish(part, coulomb):
            denominator = (vir_row[0] + vir_col[0, :, part]) - scalars[line, 0]
            out[0, :, part] = (weight * coulomb / denominator).astype(out.dtype)

        @pl.when(step == 0)
        def _():
            coulomb = None
            for index, pair in enumerate(zip(row_copies(block_of[0]), slab_copies(0))):
                for copy in pair:
                    copy.wait()
                chunk = pl.ds(index * CHUNK, CHUNK)
                term = jnp.dot(
                    rows[block_of[0], :, chunk], held[0, chunk, :], preferred_element_type=jnp.float32
                )
                coulomb = term if coulomb is None else coulomb + term
            finish(pl.ds(0, cols), coulomb)

        @pl.when(step > 0)
        def _():
            for begin in range(0, cols, half):
                part = pl.ds(begin, half)
                finish(part, jnp.dot(rows[block], held[slot, :aux, part], preferred_element_type=jnp.float32))

    return pl.pallas_call(
        kernel,
        grid=(len(jobs),),
        in_specs=[pl.BlockSpec(memory_space=pltpu.SMEM)]
        + [pl.BlockSpec(memory_space=pl.ANY)] * (sum(pieces) + sum(row_pieces) + len(earlier))
        + [
            pl.BlockSpec((1, cols, 1), lambda t: (pick(t, block_of), 0, 0)),
            pl.BlockSpec((1, 1, cols), lambda t: (pick(t, far_of), 0, 0)),
        ],
        out_specs=pl.BlockSpec((1, cols, cols), lambda t: (t, 0, 0)),
        out_shape=jax.ShapeDtypeStruct((len(jobs), cols, cols), jnp.bfloat16),
        scratch_shapes=[
            pltpu.VMEM((2, held_rows, cols), jnp.bfloat16),
            pltpu.VMEM((blocks, cols, aux), jnp.bfloat16),
            pltpu.SemaphoreType.DMA((2, chunks + 1)),
            pltpu.SemaphoreType.DMA((blocks, chunks)),
        ],
        compiler_params=pltpu.CompilerParams(vmem_limit_bytes=VMEM),
        cost_estimate=pl.CostEstimate(
            flops=2 * len(jobs) * cols * aux * cols,
            bytes_accessed=2 * cols * (blocks * aux + count * aux + len(jobs) * cols),
            transcendentals=0,
        ),
    )(table, *[p for s in slabs for p in s.pieces], *[p for b in turned for p in b], *earlier, vir_rows, vir_cols)


def chunks_of(rows):
    return [(begin, min(CHUNK, rows - begin)) for begin in range(0, rows, CHUNK)]


def copies_in(sources, held, sems):
    row, index = 0, 0
    for source in sources:
        for begin, size in chunks_of(source.shape[0]):
            yield pltpu.make_async_copy(
                source.at[pl.ds(begin, size)], held.at[pl.ds(row + begin, size)], sems.at[index]
            )
            index += 1
        row += source.shape[0]


def copies_out(held, targets, sems):
    row, index = 0, 0
    for target in targets:
        for begin, size in chunks_of(target.shape[0]):
            yield pltpu.make_async_copy(
                held.at[pl.ds(row + begin, size)], target.at[pl.ds(begin, size)], sems.at[index]
            )
            index += 1
        row += target.shape[0]


def copy_scratch(rows, cols):
    count = len(chunks_of(rows)) + 1
    return [
        pltpu.VMEM((rows, cols), jnp.bfloat16),
        pltpu.SemaphoreType.DMA((count,)),
        pltpu.SemaphoreType.DMA((count,)),
    ]


def copy_through(sources, targets, held, in_sems, out_sems):
    if [x.shape[0] for x in sources] != [x.shape[0] for x in targets]:
        loads, stores = [list(copies_in(sources, held, in_sems))], [list(copies_out(held, targets, out_sems))]
    else:
        loads = [[copy] for copy in copies_in(sources, held, in_sems)]
        stores = [[copy] for copy in copies_out(held, targets, out_sems)]
    for copies in loads:
        for copy in copies:
            copy.start()
    for before, behind in zip(loads, stores):
        for copy in before:
            copy.wait()
        for copy in behind:
            copy.start()
    for copies in stores:
        for copy in copies:
            copy.wait()


def append_call(array, tail, cuts):
    rows, cols = array.shape[0] + tail.shape[0], array.shape[1]
    begins = [0, *cuts, rows]
    sizes = [end - begin for begin, end in zip(begins, begins[1:])]

    def kernel(array_ref, tail_ref, out, *refs):
        pieces, (held, in_sems, out_sems, piece_sems) = refs[: len(sizes)], refs[len(sizes) :]
        loads = list(copies_in([array_ref, tail_ref], held, in_sems))
        stores = list(copies_out(held, [out], out_sems))
        piece_stores = list(copies_out(held, pieces, piece_sems))
        for copy in loads:
            copy.start()
        for load, *behind in zip(loads, stores, piece_stores):
            load.wait()
            for copy in behind:
                copy.start()
        for copy in stores + piece_stores:
            copy.wait()

    scratch = copy_scratch(rows, cols)
    return pl.pallas_call(
        kernel,
        in_specs=[pl.BlockSpec(memory_space=pl.ANY)] * 2,
        out_specs=[pl.BlockSpec(memory_space=pl.ANY)] * (1 + len(sizes)),
        out_shape=[jax.ShapeDtypeStruct((size, cols), array.dtype) for size in (rows, *sizes)],
        scratch_shapes=scratch + scratch[-1:],
        compiler_params=pltpu.CompilerParams(vmem_limit_bytes=VMEM),
    )(array, tail)


def choice_call(flag, a, b, earlier, cuts=(), keep=False):
    rows, cols = a.shape
    begins = [0, *cuts, rows]
    pieces = len(cuts) + 1
    shapes = [(end - begin, cols) for begin, end in zip(begins, begins[1:])]
    kept = [(rows, cols)] if keep else []

    def kernel(flag_ref, a_ref, b_ref, *refs):
        refs = refs[len(earlier) :]
        outs, kept_outs, scratch = refs[:pieces], refs[pieces : pieces + len(kept)], refs[pieces + len(kept) :]
        if keep:
            held, loads, stores, other_held, other_loads, other_stores = scratch
            leads = flag_ref[0] == 1
            ours = list(copies_in([a_ref], held, loads))
            theirs = list(copies_in([b_ref], other_held, other_loads))
            kept_copies = list(copies_out(held, kept_outs, stores))
            ours_out = list(copies_out(held, outs, other_stores))
            theirs_out = list(copies_out(other_held, outs, other_stores))
            for copy in ours:
                copy.start()

            @pl.when(jnp.logical_not(leads))
            def _():
                for copy in theirs:
                    copy.start()

            for load, store, also in zip(ours, kept_copies, ours_out):
                load.wait()
                store.start()
                pl.when(leads)(also.start)

            @pl.when(jnp.logical_not(leads))
            def _():
                for load, store in zip(theirs, theirs_out):
                    load.wait()
                    store.start()

            for store, also in zip(kept_copies, ours_out):
                store.wait()
                also.wait()
        else:
            for value, source in ((1, a_ref), (0, b_ref)):

                @pl.when(flag_ref[0] == value)
                def _(source=source):
                    parts = [source.at[pl.ds(at, out.shape[0])] for at, out in zip(begins, outs)]
                    copy_through(parts, outs, *scratch)

    return pl.pallas_call(
        kernel,
        in_specs=[pl.BlockSpec(memory_space=pltpu.SMEM)]
        + [pl.BlockSpec(memory_space=pl.ANY)] * (2 + len(earlier)),
        out_specs=[pl.BlockSpec(memory_space=pl.ANY)] * (pieces + len(kept)),
        out_shape=[jax.ShapeDtypeStruct(shape, a.dtype) for shape in shapes + kept],
        scratch_shapes=copy_scratch(rows, cols) * (1 + len(kept)),
        compiler_params=pltpu.CompilerParams(vmem_limit_bytes=VMEM),
        cost_estimate=pl.CostEstimate(flops=0, bytes_accessed=2 * a.size * a.dtype.itemsize, transcendentals=0),
    )(flag, a, b, *earlier)


def turn_call(array, rows, earlier):
    cols = array.shape[1]

    def kernel(array_ref, *refs):
        refs[-1][...] = array_ref[...].T

    return pl.pallas_call(
        kernel,
        grid=(rows // CHUNK,),
        in_specs=[pl.BlockSpec((CHUNK, cols), lambda i: (i, 0))]
        + [pl.BlockSpec(memory_space=pl.ANY)] * len(earlier),
        out_specs=pl.BlockSpec((cols, CHUNK), lambda i: (0, i)),
        out_shape=jax.ShapeDtypeStruct((cols, rows), array.dtype),
        compiler_params=pltpu.CompilerParams(vmem_limit_bytes=VMEM),
    )(array, *earlier)


def join_call(earlier):
    def kernel(*refs):
        refs[-1][...] = jnp.zeros_like(refs[-1])

    return pl.pallas_call(
        kernel,
        in_specs=[pl.BlockSpec(memory_space=pl.ANY)] * len(earlier),
        out_specs=pl.BlockSpec(memory_space=pltpu.VMEM),
        out_shape=jax.ShapeDtypeStruct((8, 128), jnp.float32),
    )(*earlier)


def density_call(terms, parts, out_dtype, aux, earlier, rows=None, copied=None, cuts=()):
    count = len(terms)
    depth = terms[0][0].array.shape[1]
    extra = list(copied or [])
    total_rows = sum(x.shape[0] for x in extra)
    ends = [0, *cuts, total_rows]
    whole = [jax.ShapeDtypeStruct((b - a, depth), jnp.bfloat16) for a, b in zip(ends, ends[1:]) if extra]
    pieces = [len(t[0].pieces) for t in terms]
    begins = [sum(pieces[:s]) for s in range(count)]
    cols = depth
    begin, length = rows or (0, aux)
    tile = 512
    while length % tile or begin % tile:
        tile //= 2
    steps = length // tile
    spans = []
    for part in parts:
        ends = np.cumsum([piece.shape[0] // tile for piece in part])
        shift = begin // tile if ends[-1] == aux // tile else 0
        spans.append([(int(end) - piece.shape[0] // tile - shift, int(end) - shift) for end, piece in zip(ends, part)])
    parts = [p for part in parts for p in part]

    def kernel(*refs):
        sources, refs = refs[: sum(pieces)], refs[sum(pieces) :]
        amps, refs = refs[:count], refs[count + len(earlier) :]
        source, refs = refs[: len(extra)], refs[len(extra) :]
        part_refs, out, refs = refs[: len(parts)], refs[len(parts)], refs[len(parts) + 1 :]
        target, refs = refs[: len(whole)], refs[len(whole) :]
        (left, right, left_sems, right_sems), scratch = refs[:4], refs[4:]
        step = pl.program_id(0)
        slot = step % 2

        def amp_copies():
            for s, (_, _, place) in enumerate(terms):
                yield pltpu.make_async_copy(
                    amps[s].at[place], right.at[:, pl.ds(s * depth, depth)], right_sems.at[s]
                )

        def slab_copies(which, start, of=range(count)):
            for s in of:
                end = 0
                for index in range(pieces[s]):
                    source = sources[begins[s] + index]
                    first = end
                    end += source.shape[0] // tile

                    def act(source=source, first=first, s=s):
                        row = pl.multiple_of((begin // tile + which - first) * tile, tile)
                        copy = pltpu.make_async_copy(
                            source.at[pl.ds(row, tile), :],
                            left.at[which % 2, :, pl.ds(s * depth, depth)],
                            left_sems.at[which % 2, s],
                        )
                        copy.start() if start else copy.wait()

                    at = begin // tile + which
                    if pieces[s] == 1:
                        act()
                    else:
                        pl.when(jnp.logical_and(at >= first, at < end))(act)

        @pl.when(step == 0)
        def _():
            for s, copy in enumerate(amp_copies()):
                copy.start()
                slab_copies(step, True, [s])
            if extra:
                for copy in copies_in(source, scratch[0], scratch[1]):
                    copy.start()

        @pl.when(step + 1 < steps)
        def _():
            slab_copies(step + 1, True)

        def finish(total):
            at = 0
            for span in spans:
                part = part_refs[at][...]
                for index in range(1, len(span)):
                    part = jnp.where(step >= span[index][0], part_refs[at + index][...], part)
                total = total + part.astype(jnp.float32)
                at += len(span)
            out[...] = total.astype(out.dtype)

        def product(a, b):
            return lax.dot_general(a, b, (((1,), (1,)), ((), ())), preferred_element_type=jnp.float32)

        @pl.when(step == 0)
        def _():
            total = None
            for s, copy in enumerate(amp_copies()):
                copy.wait()
                slab_copies(step, False, [s])
                at = pl.ds(s * depth, depth)
                term = product(left[0, :, at], right[:, at])
                total = term if total is None else total + term
            finish(total)

        @pl.when(step > 0)
        def _():
            slab_copies(step, False)
            finish(product(left[slot], right[...]))

        if extra:

            @pl.when(step == 1)
            def _():
                for copy in copies_in(source, scratch[0], scratch[1]):
                    copy.wait()
                for copy in copies_out(scratch[0], target, scratch[2]):
                    copy.start()

            @pl.when(step == steps - 1)
            def _():
                for copy in copies_out(scratch[0], target, scratch[2]):
                    copy.wait()

    def rows_of(start, end):
        return pl.BlockSpec((tile, cols), lambda i: (jnp.clip(i - start, 0, end - start - 1), 0))

    bytes_moved = 2 * count * (length * depth + cols * depth)
    bytes_moved += sum(length * cols * p.dtype.itemsize for p in parts)
    return pl.pallas_call(
        kernel,
        grid=(steps,),
        in_specs=[pl.BlockSpec(memory_space=pl.ANY)] * (sum(pieces) + count + len(earlier) + len(extra))
        + [rows_of(*ends) for span in spans for ends in span],
        out_specs=[pl.BlockSpec((tile, cols), lambda i: (i, 0))]
        + [pl.BlockSpec(memory_space=pl.ANY)] * len(whole),
        out_shape=[jax.ShapeDtypeStruct((length, cols), out_dtype)]
        + whole,
        scratch_shapes=[
            pltpu.VMEM((2, tile, count * depth), jnp.bfloat16),
            pltpu.VMEM((cols, count * depth), jnp.bfloat16),
            pltpu.SemaphoreType.DMA((2, count)),
            pltpu.SemaphoreType.DMA((count,)),
            *(copy_scratch(total_rows, depth) if extra else []),
        ],
        compiler_params=pltpu.CompilerParams(vmem_limit_bytes=VMEM),
        cost_estimate=pl.CostEstimate(
            flops=2 * length * depth * cols * count,
            bytes_accessed=(bytes_moved + length * cols * jnp.dtype(out_dtype).itemsize),
            transcendentals=0,
        ),
    )(*[p for t in terms for p in t[0].pieces], *[t[1] for t in terms], *earlier, *extra, *parts)


def paired_plan(three_index, orbital_map, occ_energy, vir_energy, pair_kept):
    blocks = lax.axis_size("wide")
    routes = Routes(blocks)
    here = lax.axis_index("wide")
    side = lax.axis_index("narrow")
    aux, vir_count = three_index.shape[1:]

    def moved(slab, pairs):
        sent = [lax.ppermute(piece, "wide", pairs) for piece in slab.pieces]
        return Slab(sent, routes.moved(slab.ids, pairs), slab.far)

    def swapped(slab):
        return moved(slab, routes.swap)

    flag = jnp.asarray(np.array(routes.lead, np.int32))[here].reshape(1)

    def copied(array, *earlier, cuts=()):
        return choice_call(flag, array, array, earlier, cuts)

    def sibling(array):
        return lax.ppermute(array, "narrow", [(0, 1), (1, 0)])

    plan = jnp.zeros((TAIL, vir_count), jnp.bfloat16)
    plan = plan.at[0, : ROUNDS + 1].set(pair_kept[:, 0].astype(jnp.bfloat16))
    whole, *split = append_call(three_index[0], plan, [aux // 2])
    own = Slab(whole, list(range(blocks)))

    r1 = moved(own, routes.rounds[0])
    own_far = Slab([sibling(piece) for piece in split], own.ids, 1)
    mate = swapped(own)

    labels = jnp.arange(occ_energy.shape[0], dtype=jnp.int32)
    picked = orbital_map[:, None] == labels[None, :]
    energy = jnp.sum(jnp.where(picked, occ_energy[None, :], 0.0), axis=1)

    def table_of(ids):
        ids = np.array(ids, np.int32).T
        places = np.arange(blocks)[:, None]
        back, forth = (places - ids) % blocks, (ids - places) % blocks
        behind = back <= ROUNDS
        known = np.stack([ids, np.where(behind, back, -1), np.where(behind, -1, forth)])
        block, mine, theirs = jnp.asarray(known.astype(np.int32))[:, here]
        places = jnp.arange(blocks, dtype=jnp.int32)[None, :]
        both = jnp.where(places == here, energy[None, :], 0.0)
        both = both + jnp.where(places == block[:, None], energy[None, :], 0.0)
        entries = jnp.arange(ROUNDS + 1, dtype=jnp.int32)[None, :]
        kept = pair_kept[:, 0].astype(jnp.float32)[None, :]
        weight = jnp.sum(jnp.where(entries == mine[:, None], kept, 0.0), axis=1)
        return jnp.stack([jnp.sum(both, axis=1), weight, theirs.astype(jnp.float32)], axis=1)

    vir = jnp.stack(
        [lax.dynamic_slice_in_dim(vir_energy, s * vir_count, vir_count) for s in (side, 1 - side)]
    )
    vir_rows, vir_cols = vir[:, :, None], vir[:, None, :]

    def moved_ids(ids_lead, ids_other, pairs):
        return routes.moved(routes.either(ids_lead, ids_other), pairs)

    def swapped_ids(ids):
        return routes.moved(ids, routes.swap)

    r2_ids = moved_ids(own.ids, r1.ids, routes.rounds[1])
    r3_ids = moved_ids(r2_ids, own.ids, routes.rounds[2])
    r4_ids = routes.moved(r3_ids, routes.rounds[3])
    r5_ids = routes.moved(own.ids, routes.rounds[4])
    all_ids = [own.ids, mate.ids]
    for ids in (r1.ids, r2_ids, r3_ids, r4_ids, r5_ids):
        all_ids += [ids, swapped_ids(ids)]
    table = table_of(all_ids)
    near, far = 0, 1
    rows_near = [own.array[:aux].T]
    stacks = {}

    def amps(jobs, turned, *earlier):
        lines = {slab: all_ids.index(slab.ids) for slab, _ in jobs}
        stack = amplitude_call(jobs, table, lines, turned, vir_rows, vir_cols, earlier)
        for place, job in enumerate(jobs):
            stacks[job] = (stack, place)
        return stack

    def density(slabs, block, parts, dtype, *earlier, rows=None, copied=None, cuts=()):
        terms = [(slab, *stacks[slab, block]) for slab in slabs]
        out, *copy = density_call(terms, parts, dtype, aux, earlier, rows, copied, cuts)
        return (out, *copy) if copy else out

    f32, bf16 = jnp.float32, jnp.bfloat16
    done = amps([(own, near), (mate, near)], [rows_near])

    parts = own_far.pieces
    sent, kept = choice_call(1 - flag, r1.array, own.array, [parts[0], done], keep=True)
    r1 = Slab(kept, r1.ids)
    sent2 = Slab(sent, routes.either(own.ids, r1.ids))
    r2 = moved(sent2, routes.rounds[1])
    s1 = swapped(r1)
    done = amps([(r1, near), (s1, near)], [rows_near], sent2.array)
    part = density([own, mate, r1, s1], near, [], f32, done)
    cut = parts[0].shape[0]
    rows_far = [turn_call(parts[0], cut, [part])]

    sent, kept = choice_call(flag, r2.array, own.array, [parts[1], *rows_far], keep=True)
    r2 = Slab(kept, r2.ids)
    sent3 = Slab(sent, routes.either(r2.ids, own.ids))
    r3 = moved(sent3, routes.rounds[2])
    s2 = swapped(r2)
    mate_far = swapped(own_far)
    rows_far.append(turn_call(parts[1], aux - cut, [sent3.array]))
    jobs = [(r2, near), (r2, far), (s2, far), (s2, near), (r1, far), (s1, far)]
    jobs += [(own_far, near), (mate_far, near)]
    done = amps(jobs, [rows_near, rows_far])
    part = density([own_far, mate_far, r2, s2], near, [[part]], f32, done)

    r3 = Slab(copied(r3.array, part), r3.ids)
    r4 = moved(r3, routes.rounds[3])
    s3 = swapped(r3)
    out_part, again = density([r1, s1, r2, s2], far, [], f32, r3.array, copied=own.pieces)
    r5 = moved(Slab(again, own.ids), routes.rounds[4])
    jobs = [(r3, near), (r3, far), (s3, far), (s3, near)]
    done = amps(jobs, [rows_near, rows_far], out_part)

    done = amps([(r4, far)], [rows_near, rows_far], done)
    half = aux // 2
    slabs = [r3, s3, r4]
    sent0, again = density(
        slabs, far, [[out_part]], bf16, done, rows=(0, half), copied=own_far.pieces
    )
    r6 = moved(Slab(again, own.ids, 1), routes.rounds[4])
    sent1 = density(slabs, far, [[out_part]], bf16, sent0, rows=(half, half))
    incoming = [sibling(sent0), sibling(sent1)]
    done = amps([(r4, near)], [rows_near], sent1)
    part = density([r3, s3, r4], near, [[part]], f32, done)

    thirds = [aux // 3, aux // 3 * 2]
    r5 = Slab(copied(r5.array, part, cuts=thirds), r5.ids)
    s5 = swapped(r5)
    done = amps([(r5, near)], [rows_near], *r5.pieces)
    done = join_call([incoming[0], done])
    done = amps([(s5, near)], [rows_near], done)
    part = density([r5, s5], near, [[part]], f32, done)
    r6 = Slab(copied(r6.array, part, cuts=thirds), r6.ids, 1)
    s6 = swapped(r6)
    done = amps([(r6, near)], [rows_near], *r6.pieces)
    done = join_call([incoming[1], done])
    done = amps([(s6, near)], [rows_near], done)
    return density([r6, s6], near, [[part], incoming], f32, done)[None]


def solution(mesh):
    wide, narrow = mesh.shape["wide"], mesh.shape["narrow"]
    paired = narrow == 2 and wide % 4 == 0 and wide > 2 * ROUNDS + 1 and ROUNDS == 5

    def per_device(three_index, *rest):
        if paired and three_index.shape[0] == 1:
            return paired_plan(three_index, *rest)
        return ring_plan(three_index, *rest)

    placed = (P("wide", None, "narrow"), P(), P(), P(), P(None, "wide"))
    return jax.shard_map(
        per_device, mesh=mesh, in_specs=placed, out_specs=P("wide", None, "narrow"), check_vma=False
    )
```

```python
import jax
import jax.numpy as jnp
import numpy as np
from jax import lax
from jax.experimental import pallas as pl
from jax.experimental.pallas import tpu as pltpu
from jax.sharding import PartitionSpec as P

ROUNDS = 5
TAIL = 16
CHUNK = 512
VMEM = 48 * 1024 * 1024


def passed_along(array, axis, by):
    length = lax.axis_size(axis)
    return lax.ppermute(array, axis, [(i, (i + by) % length) for i in range(length)])


def block_energy(orbital_map, occ_energy, block_id, occ_count):
    orbits = lax.dynamic_slice_in_dim(orbital_map, block_id * occ_count, occ_count)
    labels = jnp.arange(occ_energy.shape[0], dtype=jnp.int32)
    chosen = orbits[:, None] == labels[None, :]
    return jnp.sum(jnp.where(chosen, occ_energy[None, :], 0.0), axis=1)


def amplitudes(gathered, visiting, left_energy, right_energy, vir_all, vir_local, weight):
    coulomb = jnp.einsum("ipa,jpb->ijab", gathered, visiting, preferred_element_type=jnp.float32)
    denominator = (vir_all[:, None] + vir_local[None, :])[None, None] - (
        left_energy[:, None] + right_energy[None, :]
    )[:, :, None, None]
    return (weight * coulomb / denominator).astype(jnp.bfloat16)


def ring_plan(three_index, orbital_map, occ_energy, vir_energy, pair_kept):
    occ_count = three_index.shape[0]
    vir_count = three_index.shape[2]
    blocks = lax.axis_size("wide")
    own_block = lax.axis_index("wide")
    vir_local = lax.dynamic_slice_in_dim(
        vir_energy, lax.axis_index("narrow") * vir_count, vir_count
    )
    own_energy = block_energy(orbital_map, occ_energy, own_block, occ_count)
    weights = pair_kept.astype(jnp.float32)
    gathered = lax.all_gather(three_index, "narrow", axis=2, tiled=True)
    amplitude = amplitudes(
        gathered, three_index, own_energy, own_energy, vir_energy, vir_local, weights[0, 0]
    )
    forward = jnp.einsum(
        "ijab,jpb->ipa", amplitude, three_index, preferred_element_type=jnp.float32
    )
    visiting = three_index
    stored_amps = []
    for round_index in range(1, ROUNDS + 1):
        visiting = passed_along(visiting, "wide", 1)
        partner = (own_block - round_index) % blocks
        partner_energy = block_energy(orbital_map, occ_energy, partner, occ_count)
        amplitude = amplitudes(
            gathered,
            visiting,
            own_energy,
            partner_energy,
            vir_energy,
            vir_local,
            weights[round_index, 0],
        )
        forward = forward + jnp.einsum(
            "ijab,jpb->ipa", amplitude, visiting, preferred_element_type=jnp.float32
        )
        stored_amps.append(amplitude)
    carried = None
    for round_index in range(1, ROUNDS + 1):
        backward = jnp.einsum(
            "ijab,ipa->jpb",
            stored_amps[round_index - 1],
            gathered,
            preferred_element_type=jnp.float32,
        )
        if round_index > 1:
            carried = passed_along(carried, "wide", 1) + backward
        else:
            carried = backward
    returned = passed_along(carried, "wide", -ROUNDS)
    scattered = lax.psum_scatter(forward, "narrow", scatter_dimension=2, tiled=True)
    return scattered + returned


class Routes:
    def __init__(self, blocks):
        self.blocks = blocks
        everyone = range(blocks)
        self.lead = [self.place(w)[1] == self.place(w)[2] for w in everyone]
        self.swap = [(w, w ^ 1) for w in everyone]
        onward = [(w, self.along_z(w, 1)) for w in everyone]
        backward = [(w, self.along_z(w, -1)) for w in everyone]
        across = [(w, self.across_x(w)) for w in everyone]
        self.rounds = [
            self.either(across, onward),
            self.either(onward, across),
            self.either(across, backward),
            self.either(backward, across),
            self.either(backward, across),
        ]

    def place(self, w):
        return w // 4, (w // 2) % 2, w % 2

    def along_z(self, w, step):
        z, x, core = self.place(w)
        z = (z + (step if x == 1 else -step)) % (self.blocks // 4)
        return (z * 2 + x) * 2 + core

    def across_x(self, w):
        z, x, core = self.place(w)
        return (z * 2 + 1 - x) * 2 + 1 - core

    def either(self, of_lead, of_other):
        return [a if lead else b for lead, a, b in zip(self.lead, of_lead, of_other)]

    def moved(self, ids, pairs):
        out = [0] * self.blocks
        for source, target in pairs:
            out[target] = ids[source]
        return out


class Slab:
    def __init__(self, array, ids, far=0):
        self.pieces = list(array) if isinstance(array, (list, tuple)) else [array]
        self.array = self.pieces[0]
        self.ids = ids
        self.far = far


def pick(step, values):
    out = values[0]
    for index, value in enumerate(values):
        if index and value != values[0]:
            out = jnp.where(step == index, value, out)
    return out


def amplitude_call(jobs, table, lines, turned, vir_rows, vir_cols, earlier):
    slabs = []
    for slab, _ in jobs:
        if slab not in slabs:
            slabs.append(slab)
    count, blocks = len(slabs), len(turned)
    cols, aux = turned[0][0].shape[0], sum(piece.shape[1] for piece in turned[0])
    held_rows = aux + TAIL
    pieces = [len(slab.pieces) for slab in slabs]
    begins = [sum(pieces[:s]) for s in range(count)]
    of_job = [slabs.index(slab) for slab, _ in jobs]
    block_of = [block for _, block in jobs]
    far_of = [slab.far for slab, _ in jobs]
    line_of = [lines[slab] for slab, _ in jobs]
    row_pieces = [len(block) for block in turned]
    chunks = aux // CHUNK
    opens = [t for t in range(len(jobs)) if t == 0 or of_job[t] != of_job[t - 1]]
    half = cols // 2

    def kernel(scalars, *refs):
        sources, refs = refs[: sum(pieces)], refs[sum(pieces) :]
        row_sources, refs = refs[: sum(row_pieces)], refs[sum(row_pieces) + len(earlier) :]
        vir_row, vir_col, out, held, rows, held_sems, row_sems = refs
        step = pl.program_id(0)

        def slab_copies(s):
            row = 0
            for index in range(pieces[s]):
                source = sources[begins[s] + index]
                for begin, size in chunks_of(source.shape[0]):
                    target = held.at[s % 2, pl.ds(row, size), :]
                    yield pltpu.make_async_copy(
                        source.at[pl.ds(begin, size)], target, held_sems.at[s % 2, row // CHUNK]
                    )
                    row += size

        def row_copies(block):
            column = 0
            for source in row_sources[sum(row_pieces[:block]) : sum(row_pieces[: block + 1])]:
                for begin, size in chunks_of(source.shape[1]):
                    target = rows.at[block, :, pl.ds(column, size)]
                    yield pltpu.make_async_copy(
                        source.at[:, pl.ds(begin, size)], target, row_sems.at[block, column // CHUNK]
                    )
                    column += size

        @pl.when(step == 0)
        def _():
            for pair in zip(slab_copies(0), row_copies(block_of[0])):
                for copy in pair:
                    copy.start()
            for copy in list(slab_copies(0))[chunks:]:
                copy.start()
            for block in list(dict.fromkeys(block_of))[1:]:
                for copy in row_copies(block):
                    copy.start()

        for s, t in enumerate(opens):

            @pl.when(step == t)
            def _(s=s):
                if s:
                    for copy in slab_copies(s):
                        copy.wait()
                if s + 1 < count:
                    for copy in slab_copies(s + 1):
                        copy.start()

        for block in list(dict.fromkeys(block_of))[1:]:

            @pl.when(step == block_of.index(block))
            def _(block=block):
                for copy in row_copies(block):
                    copy.wait()

        slot = pick(step, [s % 2 for s in of_job])
        block = pick(step, block_of)
        line = pick(step, line_of)
        @pl.when(step == 0)
        def _():
            for copy in list(slab_copies(0))[chunks:]:
                copy.wait()

        plan = held[slot, aux:, :128].astype(jnp.float32)
        lane = lax.broadcasted_iota(jnp.int32, plan.shape, 1).astype(jnp.float32)
        row = lax.broadcasted_iota(jnp.int32, plan.shape, 0)
        told = jnp.where(jnp.logical_and(row == 0, lane == scalars[line, 2]), plan, 0.0)
        weight = scalars[line, 1] + jnp.sum(told, keepdims=True)

        def finish(part, coulomb):
            denominator = (vir_row[0] + vir_col[0, :, part]) - scalars[line, 0]
            out[0, :, part] = (weight * coulomb / denominator).astype(out.dtype)

        @pl.when(step == 0)
        def _():
            coulomb = None
            for index, pair in enumerate(zip(row_copies(block_of[0]), slab_copies(0))):
                for copy in pair:
                    copy.wait()
                chunk = pl.ds(index * CHUNK, CHUNK)
                term = jnp.dot(
                    rows[block_of[0], :, chunk], held[0, chunk, :], preferred_element_type=jnp.float32
                )
                coulomb = term if coulomb is None else coulomb + term
            finish(pl.ds(0, cols), coulomb)

        @pl.when(step > 0)
        def _():
            for begin in range(0, cols, half):
                part = pl.ds(begin, half)
                finish(part, jnp.dot(rows[block], held[slot, :aux, part], preferred_element_type=jnp.float32))

    return pl.pallas_call(
        kernel,
        grid=(len(jobs),),
        in_specs=[pl.BlockSpec(memory_space=pltpu.SMEM)]
        + [pl.BlockSpec(memory_space=pl.ANY)] * (sum(pieces) + sum(row_pieces) + len(earlier))
        + [
            pl.BlockSpec((1, cols, 1), lambda t: (pick(t, block_of), 0, 0)),
            pl.BlockSpec((1, 1, cols), lambda t: (pick(t, far_of), 0, 0)),
        ],
        out_specs=pl.BlockSpec((1, cols, cols), lambda t: (t, 0, 0)),
        out_shape=jax.ShapeDtypeStruct((len(jobs), cols, cols), jnp.bfloat16),
        scratch_shapes=[
            pltpu.VMEM((2, held_rows, cols), jnp.bfloat16),
            pltpu.VMEM((blocks, cols, aux), jnp.bfloat16),
            pltpu.SemaphoreType.DMA((2, chunks + 1)),
            pltpu.SemaphoreType.DMA((blocks, chunks)),
        ],
        compiler_params=pltpu.CompilerParams(vmem_limit_bytes=VMEM),
        cost_estimate=pl.CostEstimate(
            flops=2 * len(jobs) * cols * aux * cols,
            bytes_accessed=2 * cols * (blocks * aux + count * aux + len(jobs) * cols),
            transcendentals=0,
        ),
    )(table, *[p for s in slabs for p in s.pieces], *[p for b in turned for p in b], *earlier, vir_rows, vir_cols)


def chunks_of(rows):
    return [(begin, min(CHUNK, rows - begin)) for begin in range(0, rows, CHUNK)]


def copies_in(sources, held, sems):
    row, index = 0, 0
    for source in sources:
        for begin, size in chunks_of(source.shape[0]):
            yield pltpu.make_async_copy(
                source.at[pl.ds(begin, size)], held.at[pl.ds(row + begin, size)], sems.at[index]
            )
            index += 1
        row += source.shape[0]


def copies_out(held, targets, sems):
    row, index = 0, 0
    for target in targets:
        for begin, size in chunks_of(target.shape[0]):
            yield pltpu.make_async_copy(
                held.at[pl.ds(row + begin, size)], target.at[pl.ds(begin, size)], sems.at[index]
            )
            index += 1
        row += target.shape[0]


def copy_scratch(rows, cols):
    count = len(chunks_of(rows)) + 1
    return [
        pltpu.VMEM((rows, cols), jnp.bfloat16),
        pltpu.SemaphoreType.DMA((count,)),
        pltpu.SemaphoreType.DMA((count,)),
    ]


def copy_through(sources, targets, held, in_sems, out_sems):
    if [x.shape[0] for x in sources] != [x.shape[0] for x in targets]:
        loads, stores = [list(copies_in(sources, held, in_sems))], [list(copies_out(held, targets, out_sems))]
    else:
        loads = [[copy] for copy in copies_in(sources, held, in_sems)]
        stores = [[copy] for copy in copies_out(held, targets, out_sems)]
    for copies in loads:
        for copy in copies:
            copy.start()
    for before, behind in zip(loads, stores):
        for copy in before:
            copy.wait()
        for copy in behind:
            copy.start()
    for copies in stores:
        for copy in copies:
            copy.wait()


def append_call(array, tail, cuts):
    rows, cols = array.shape[0] + tail.shape[0], array.shape[1]
    begins = [0, *cuts, rows]
    sizes = [end - begin for begin, end in zip(begins, begins[1:])]

    def kernel(array_ref, tail_ref, out, *refs):
        pieces, (held, in_sems, out_sems, piece_sems) = refs[: len(sizes)], refs[len(sizes) :]
        loads = list(copies_in([array_ref, tail_ref], held, in_sems))
        stores = list(copies_out(held, [out], out_sems))
        piece_stores = list(copies_out(held, pieces, piece_sems))
        for copy in loads:
            copy.start()
        for load, *behind in zip(loads, stores, piece_stores):
            load.wait()
            for copy in behind:
                copy.start()
        for copy in stores + piece_stores:
            copy.wait()

    scratch = copy_scratch(rows, cols)
    return pl.pallas_call(
        kernel,
        in_specs=[pl.BlockSpec(memory_space=pl.ANY)] * 2,
        out_specs=[pl.BlockSpec(memory_space=pl.ANY)] * (1 + len(sizes)),
        out_shape=[jax.ShapeDtypeStruct((size, cols), array.dtype) for size in (rows, *sizes)],
        scratch_shapes=scratch + scratch[-1:],
        compiler_params=pltpu.CompilerParams(vmem_limit_bytes=VMEM),
    )(array, tail)


def choice_call(flag, a, b, earlier, cuts=(), keep=False):
    rows, cols = a.shape
    begins = [0, *cuts, rows]
    pieces = len(cuts) + 1
    shapes = [(end - begin, cols) for begin, end in zip(begins, begins[1:])]
    kept = [(rows, cols)] if keep else []

    def kernel(flag_ref, a_ref, b_ref, *refs):
        refs = refs[len(earlier) :]
        outs, kept_outs, scratch = refs[:pieces], refs[pieces : pieces + len(kept)], refs[pieces + len(kept) :]
        if keep:
            held, loads, stores, other_held, other_loads, other_stores = scratch
            leads = flag_ref[0] == 1
            ours = list(copies_in([a_ref], held, loads))
            theirs = list(copies_in([b_ref], other_held, other_loads))
            kept_copies = list(copies_out(held, kept_outs, stores))
            ours_out = list(copies_out(held, outs, other_stores))
            theirs_out = list(copies_out(other_held, outs, other_stores))
            for copy in ours:
                copy.start()

            @pl.when(jnp.logical_not(leads))
            def _():
                for copy in theirs:
                    copy.start()

            for load, store, also in zip(ours, kept_copies, ours_out):
                load.wait()
                store.start()
                pl.when(leads)(also.start)

            @pl.when(jnp.logical_not(leads))
            def _():
                for load, store in zip(theirs, theirs_out):
                    load.wait()
                    store.start()

            for store, also in zip(kept_copies, ours_out):
                store.wait()
                also.wait()
        else:
            for value, source in ((1, a_ref), (0, b_ref)):

                @pl.when(flag_ref[0] == value)
                def _(source=source):
                    parts = [source.at[pl.ds(at, out.shape[0])] for at, out in zip(begins, outs)]
                    copy_through(parts, outs, *scratch)

    return pl.pallas_call(
        kernel,
        in_specs=[pl.BlockSpec(memory_space=pltpu.SMEM)]
        + [pl.BlockSpec(memory_space=pl.ANY)] * (2 + len(earlier)),
        out_specs=[pl.BlockSpec(memory_space=pl.ANY)] * (pieces + len(kept)),
        out_shape=[jax.ShapeDtypeStruct(shape, a.dtype) for shape in shapes + kept],
        scratch_shapes=copy_scratch(rows, cols) * (1 + len(kept)),
        compiler_params=pltpu.CompilerParams(vmem_limit_bytes=VMEM),
        cost_estimate=pl.CostEstimate(flops=0, bytes_accessed=2 * a.size * a.dtype.itemsize, transcendentals=0),
    )(flag, a, b, *earlier)


def turn_call(array, rows, earlier):
    cols = array.shape[1]

    def kernel(array_ref, *refs):
        refs[-1][...] = array_ref[...].T

    return pl.pallas_call(
        kernel,
        grid=(rows // CHUNK,),
        in_specs=[pl.BlockSpec((CHUNK, cols), lambda i: (i, 0))]
        + [pl.BlockSpec(memory_space=pl.ANY)] * len(earlier),
        out_specs=pl.BlockSpec((cols, CHUNK), lambda i: (0, i)),
        out_shape=jax.ShapeDtypeStruct((cols, rows), array.dtype),
        compiler_params=pltpu.CompilerParams(vmem_limit_bytes=VMEM),
    )(array, *earlier)


def join_call(earlier):
    def kernel(*refs):
        refs[-1][...] = jnp.zeros_like(refs[-1])

    return pl.pallas_call(
        kernel,
        in_specs=[pl.BlockSpec(memory_space=pl.ANY)] * len(earlier),
        out_specs=pl.BlockSpec(memory_space=pltpu.VMEM),
        out_shape=jax.ShapeDtypeStruct((8, 128), jnp.float32),
    )(*earlier)


def density_call(terms, parts, out_dtype, aux, earlier, rows=None, copied=None, cuts=()):
    count = len(terms)
    depth = terms[0][0].array.shape[1]
    extra = list(copied or [])
    total_rows = sum(x.shape[0] for x in extra)
    ends = [0, *cuts, total_rows]
    whole = [jax.ShapeDtypeStruct((b - a, depth), jnp.bfloat16) for a, b in zip(ends, ends[1:]) if extra]
    pieces = [len(t[0].pieces) for t in terms]
    begins = [sum(pieces[:s]) for s in range(count)]
    cols = depth
    begin, length = rows or (0, aux)
    tile = 512
    while length % tile or begin % tile:
        tile //= 2
    steps = length // tile
    spans = []
    for part in parts:
        ends = np.cumsum([piece.shape[0] // tile for piece in part])
        shift = begin // tile if ends[-1] == aux // tile else 0
        spans.append([(int(end) - piece.shape[0] // tile - shift, int(end) - shift) for end, piece in zip(ends, part)])
    parts = [p for part in parts for p in part]

    def kernel(*refs):
        sources, refs = refs[: sum(pieces)], refs[sum(pieces) :]
        amps, refs = refs[:count], refs[count + len(earlier) :]
        source, refs = refs[: len(extra)], refs[len(extra) :]
        part_refs, out, refs = refs[: len(parts)], refs[len(parts)], refs[len(parts) + 1 :]
        target, refs = refs[: len(whole)], refs[len(whole) :]
        (left, right, left_sems, right_sems), scratch = refs[:4], refs[4:]
        step = pl.program_id(0)
        slot = step % 2

        def amp_copies():
            for s, (_, _, place) in enumerate(terms):
                yield pltpu.make_async_copy(
                    amps[s].at[place], right.at[:, pl.ds(s * depth, depth)], right_sems.at[s]
                )

        def slab_copies(which, start, of=range(count)):
            for s in of:
                end = 0
                for index in range(pieces[s]):
                    source = sources[begins[s] + index]
                    first = end
                    end += source.shape[0] // tile

                    def act(source=source, first=first, s=s):
                        row = pl.multiple_of((begin // tile + which - first) * tile, tile)
                        copy = pltpu.make_async_copy(
                            source.at[pl.ds(row, tile), :],
                            left.at[which % 2, :, pl.ds(s * depth, depth)],
                            left_sems.at[which % 2, s],
                        )
                        copy.start() if start else copy.wait()

                    at = begin // tile + which
                    if pieces[s] == 1:
                        act()
                    else:
                        pl.when(jnp.logical_and(at >= first, at < end))(act)

        @pl.when(step == 0)
        def _():
            for s, copy in enumerate(amp_copies()):
                copy.start()
                slab_copies(step, True, [s])
            if extra:
                for copy in copies_in(source, scratch[0], scratch[1]):
                    copy.start()

        @pl.when(step + 1 < steps)
        def _():
            slab_copies(step + 1, True)

        def finish(total):
            at = 0
            for span in spans:
                part = part_refs[at][...]
                for index in range(1, len(span)):
                    part = jnp.where(step >= span[index][0], part_refs[at + index][...], part)
                total = total + part.astype(jnp.float32)
                at += len(span)
            out[...] = total.astype(out.dtype)

        def product(a, b):
            return lax.dot_general(a, b, (((1,), (1,)), ((), ())), preferred_element_type=jnp.float32)

        @pl.when(step == 0)
        def _():
            total = None
            for s, copy in enumerate(amp_copies()):
                copy.wait()
                slab_copies(step, False, [s])
                at = pl.ds(s * depth, depth)
                term = product(left[0, :, at], right[:, at])
                total = term if total is None else total + term
            finish(total)

        @pl.when(step > 0)
        def _():
            slab_copies(step, False)
            finish(product(left[slot], right[...]))

        if extra:

            @pl.when(step == 1)
            def _():
                for copy in copies_in(source, scratch[0], scratch[1]):
                    copy.wait()
                for copy in copies_out(scratch[0], target, scratch[2]):
                    copy.start()

            @pl.when(step == steps - 1)
            def _():
                for copy in copies_out(scratch[0], target, scratch[2]):
                    copy.wait()

    def rows_of(start, end):
        return pl.BlockSpec((tile, cols), lambda i: (jnp.clip(i - start, 0, end - start - 1), 0))

    bytes_moved = 2 * count * (length * depth + cols * depth)
    bytes_moved += sum(length * cols * p.dtype.itemsize for p in parts)
    return pl.pallas_call(
        kernel,
        grid=(steps,),
        in_specs=[pl.BlockSpec(memory_space=pl.ANY)] * (sum(pieces) + count + len(earlier) + len(extra))
        + [rows_of(*ends) for span in spans for ends in span],
        out_specs=[pl.BlockSpec((tile, cols), lambda i: (i, 0))]
        + [pl.BlockSpec(memory_space=pl.ANY)] * len(whole),
        out_shape=[jax.ShapeDtypeStruct((length, cols), out_dtype)]
        + whole,
        scratch_shapes=[
            pltpu.VMEM((2, tile, count * depth), jnp.bfloat16),
            pltpu.VMEM((cols, count * depth), jnp.bfloat16),
            pltpu.SemaphoreType.DMA((2, count)),
            pltpu.SemaphoreType.DMA((count,)),
            *(copy_scratch(total_rows, depth) if extra else []),
        ],
        compiler_params=pltpu.CompilerParams(vmem_limit_bytes=VMEM),
        cost_estimate=pl.CostEstimate(
            flops=2 * length * depth * cols * count,
            bytes_accessed=(bytes_moved + length * cols * jnp.dtype(out_dtype).itemsize),
            transcendentals=0,
        ),
    )(*[p for t in terms for p in t[0].pieces], *[t[1] for t in terms], *earlier, *extra, *parts)


def paired_plan(three_index, orbital_map, occ_energy, vir_energy, pair_kept):
    blocks = lax.axis_size("wide")
    routes = Routes(blocks)
    here = lax.axis_index("wide")
    side = lax.axis_index("narrow")
    aux, vir_count = three_index.shape[1:]

    def moved(slab, pairs):
        sent = [lax.ppermute(piece, "wide", pairs) for piece in slab.pieces]
        return Slab(sent, routes.moved(slab.ids, pairs), slab.far)

    def swapped(slab):
        return moved(slab, routes.swap)

    flag = jnp.asarray(np.array(routes.lead, np.int32))[here].reshape(1)

    def copied(array, *earlier, cuts=()):
        return choice_call(flag, array, array, earlier, cuts)

    def sibling(array):
        return lax.ppermute(array, "narrow", [(0, 1), (1, 0)])

    plan = jnp.zeros((TAIL, vir_count), jnp.bfloat16)
    plan = plan.at[0, : ROUNDS + 1].set(pair_kept[:, 0].astype(jnp.bfloat16))
    whole, *split = append_call(three_index[0], plan, [aux // 2])
    own = Slab(whole, list(range(blocks)))

    r1 = moved(own, routes.rounds[0])
    own_far = Slab([sibling(piece) for piece in split], own.ids, 1)
    mate = swapped(own)

    labels = jnp.arange(occ_energy.shape[0], dtype=jnp.int32)
    picked = orbital_map[:, None] == labels[None, :]
    energy = jnp.sum(jnp.where(picked, occ_energy[None, :], 0.0), axis=1)

    def table_of(ids):
        ids = np.array(ids, np.int32).T
        places = np.arange(blocks)[:, None]
        back, forth = (places - ids) % blocks, (ids - places) % blocks
        behind = back <= ROUNDS
        known = np.stack([ids, np.where(behind, back, -1), np.where(behind, -1, forth)])
        block, mine, theirs = jnp.asarray(known.astype(np.int32))[:, here]
        places = jnp.arange(blocks, dtype=jnp.int32)[None, :]
        both = jnp.where(places == here, energy[None, :], 0.0)
        both = both + jnp.where(places == block[:, None], energy[None, :], 0.0)
        entries = jnp.arange(ROUNDS + 1, dtype=jnp.int32)[None, :]
        kept = pair_kept[:, 0].astype(jnp.float32)[None, :]
        weight = jnp.sum(jnp.where(entries == mine[:, None], kept, 0.0), axis=1)
        return jnp.stack([jnp.sum(both, axis=1), weight, theirs.astype(jnp.float32)], axis=1)

    vir = jnp.stack(
        [lax.dynamic_slice_in_dim(vir_energy, s * vir_count, vir_count) for s in (side, 1 - side)]
    )
    vir_rows, vir_cols = vir[:, :, None], vir[:, None, :]

    def moved_ids(ids_lead, ids_other, pairs):
        return routes.moved(routes.either(ids_lead, ids_other), pairs)

    def swapped_ids(ids):
        return routes.moved(ids, routes.swap)

    r2_ids = moved_ids(own.ids, r1.ids, routes.rounds[1])
    r3_ids = moved_ids(r2_ids, own.ids, routes.rounds[2])
    r4_ids = routes.moved(r3_ids, routes.rounds[3])
    r5_ids = routes.moved(own.ids, routes.rounds[4])
    all_ids = [own.ids, mate.ids]
    for ids in (r1.ids, r2_ids, r3_ids, r4_ids, r5_ids):
        all_ids += [ids, swapped_ids(ids)]
    table = table_of(all_ids)
    near, far = 0, 1
    rows_near = [own.array[:aux].T]
    stacks = {}

    def amps(jobs, turned, *earlier):
        lines = {slab: all_ids.index(slab.ids) for slab, _ in jobs}
        stack = amplitude_call(jobs, table, lines, turned, vir_rows, vir_cols, earlier)
        for place, job in enumerate(jobs):
            stacks[job] = (stack, place)
        return stack

    def density(slabs, block, parts, dtype, *earlier, rows=None, copied=None, cuts=()):
        terms = [(slab, *stacks[slab, block]) for slab in slabs]
        out, *copy = density_call(terms, parts, dtype, aux, earlier, rows, copied, cuts)
        return (out, *copy) if copy else out

    f32, bf16 = jnp.float32, jnp.bfloat16
    done = amps([(own, near), (mate, near)], [rows_near])

    parts = own_far.pieces
    sent, kept = choice_call(1 - flag, r1.array, own.array, [parts[0], done], keep=True)
    r1 = Slab(kept, r1.ids)
    sent2 = Slab(sent, routes.either(own.ids, r1.ids))
    r2 = moved(sent2, routes.rounds[1])
    s1 = swapped(r1)
    done = amps([(r1, near), (s1, near)], [rows_near], sent2.array)
    part = density([own, mate, r1, s1], near, [], f32, done)
    cut = parts[0].shape[0]
    rows_far = [turn_call(parts[0], cut, [part])]

    sent, kept = choice_call(flag, r2.array, own.array, [parts[1], *rows_far], keep=True)
    r2 = Slab(kept, r2.ids)
    sent3 = Slab(sent, routes.either(r2.ids, own.ids))
    r3 = moved(sent3, routes.rounds[2])
    s2 = swapped(r2)
    mate_far = swapped(own_far)
    rows_far.append(turn_call(parts[1], aux - cut, [sent3.array]))
    jobs = [(r2, near), (r2, far), (s2, far), (s2, near), (r1, far), (s1, far)]
    jobs += [(own_far, near)]
    done = amps(jobs, [rows_near, rows_far])
    part = density([own_far, r2, s2], near, [[part]], f32, done)

    r3 = Slab(copied(r3.array, part), r3.ids)
    r4 = moved(r3, routes.rounds[3])
    s3 = swapped(r3)
    out_part, again = density([r1, s1, r2, s2], far, [], f32, r3.array, copied=own.pieces)
    r5 = moved(Slab(again, own.ids), routes.rounds[4])
    jobs = [(mate_far, near), (r3, near), (r3, far), (s3, far), (s3, near)]
    done = amps(jobs, [rows_near, rows_far], out_part)

    done = amps([(r4, far)], [rows_near, rows_far], done)
    half = aux // 2
    slabs = [r3, s3, r4]
    sent0, again = density(
        slabs, far, [[out_part]], bf16, done, rows=(0, half), copied=own_far.pieces
    )
    r6 = moved(Slab(again, own.ids, 1), routes.rounds[4])
    sent1 = density(slabs, far, [[out_part]], bf16, sent0, rows=(half, half))
    incoming = [sibling(sent0), sibling(sent1)]
    done = amps([(r4, near)], [rows_near], sent1)
    part = density([mate_far, r3, s3, r4], near, [[part]], f32, done)

    thirds = [aux // 3, aux // 3 * 2]
    r5 = Slab(copied(r5.array, part, cuts=thirds), r5.ids)
    s5 = swapped(r5)
    done = amps([(r5, near)], [rows_near], *r5.pieces)
    done = join_call([incoming[0], done])
    done = amps([(s5, near)], [rows_near], done)
    part = density([r5, s5], near, [[part]], f32, done)
    r6 = Slab(copied(r6.array, part, cuts=thirds), r6.ids, 1)
    s6 = swapped(r6)
    done = amps([(r6, near)], [rows_near], *r6.pieces)
    done = join_call([incoming[1], done])
    done = amps([(s6, near)], [rows_near], done)
    return density([r6, s6], near, [[part], incoming], f32, done)[None]


def solution(mesh):
    wide, narrow = mesh.shape["wide"], mesh.shape["narrow"]
    paired = narrow == 2 and wide % 4 == 0 and wide > 2 * ROUNDS + 1 and ROUNDS == 5

    def per_device(three_index, *rest):
        if paired and three_index.shape[0] == 1:
            return paired_plan(three_index, *rest)
        return ring_plan(three_index, *rest)

    placed = (P("wide", None, "narrow"), P(), P(), P(), P(None, "wide"))
    return jax.shard_map(
        per_device, mesh=mesh, in_specs=placed, out_specs=P("wide", None, "narrow"), check_vma=False
    )
```

```python
import jax
import jax.numpy as jnp
import numpy as np
from jax import lax
from jax.experimental import pallas as pl
from jax.experimental.pallas import tpu as pltpu
from jax.sharding import PartitionSpec as P

ROUNDS = 5
TAIL = 16
CHUNK = 512
VMEM = 48 * 1024 * 1024


def passed_along(array, axis, by):
    length = lax.axis_size(axis)
    return lax.ppermute(array, axis, [(i, (i + by) % length) for i in range(length)])


def block_energy(orbital_map, occ_energy, block_id, occ_count):
    orbits = lax.dynamic_slice_in_dim(orbital_map, block_id * occ_count, occ_count)
    labels = jnp.arange(occ_energy.shape[0], dtype=jnp.int32)
    chosen = orbits[:, None] == labels[None, :]
    return jnp.sum(jnp.where(chosen, occ_energy[None, :], 0.0), axis=1)


def amplitudes(gathered, visiting, left_energy, right_energy, vir_all, vir_local, weight):
    coulomb = jnp.einsum("ipa,jpb->ijab", gathered, visiting, preferred_element_type=jnp.float32)
    denominator = (vir_all[:, None] + vir_local[None, :])[None, None] - (
        left_energy[:, None] + right_energy[None, :]
    )[:, :, None, None]
    return (weight * coulomb / denominator).astype(jnp.bfloat16)


def ring_plan(three_index, orbital_map, occ_energy, vir_energy, pair_kept):
    occ_count = three_index.shape[0]
    vir_count = three_index.shape[2]
    blocks = lax.axis_size("wide")
    own_block = lax.axis_index("wide")
    vir_local = lax.dynamic_slice_in_dim(
        vir_energy, lax.axis_index("narrow") * vir_count, vir_count
    )
    own_energy = block_energy(orbital_map, occ_energy, own_block, occ_count)
    weights = pair_kept.astype(jnp.float32)
    gathered = lax.all_gather(three_index, "narrow", axis=2, tiled=True)
    amplitude = amplitudes(
        gathered, three_index, own_energy, own_energy, vir_energy, vir_local, weights[0, 0]
    )
    forward = jnp.einsum(
        "ijab,jpb->ipa", amplitude, three_index, preferred_element_type=jnp.float32
    )
    visiting = three_index
    stored_amps = []
    for round_index in range(1, ROUNDS + 1):
        visiting = passed_along(visiting, "wide", 1)
        partner = (own_block - round_index) % blocks
        partner_energy = block_energy(orbital_map, occ_energy, partner, occ_count)
        amplitude = amplitudes(
            gathered,
            visiting,
            own_energy,
            partner_energy,
            vir_energy,
            vir_local,
            weights[round_index, 0],
        )
        forward = forward + jnp.einsum(
            "ijab,jpb->ipa", amplitude, visiting, preferred_element_type=jnp.float32
        )
        stored_amps.append(amplitude)
    carried = None
    for round_index in range(1, ROUNDS + 1):
        backward = jnp.einsum(
            "ijab,ipa->jpb",
            stored_amps[round_index - 1],
            gathered,
            preferred_element_type=jnp.float32,
        )
        if round_index > 1:
            carried = passed_along(carried, "wide", 1) + backward
        else:
            carried = backward
    returned = passed_along(carried, "wide", -ROUNDS)
    scattered = lax.psum_scatter(forward, "narrow", scatter_dimension=2, tiled=True)
    return scattered + returned


class Routes:
    def __init__(self, blocks):
        self.blocks = blocks
        everyone = range(blocks)
        self.lead = [self.place(w)[1] == self.place(w)[2] for w in everyone]
        self.swap = [(w, w ^ 1) for w in everyone]
        onward = [(w, self.along_z(w, 1)) for w in everyone]
        backward = [(w, self.along_z(w, -1)) for w in everyone]
        across = [(w, self.across_x(w)) for w in everyone]
        self.rounds = [
            self.either(across, onward),
            self.either(onward, across),
            self.either(across, backward),
            self.either(backward, across),
            self.either(backward, across),
        ]

    def place(self, w):
        return w // 4, (w // 2) % 2, w % 2

    def along_z(self, w, step):
        z, x, core = self.place(w)
        z = (z + (step if x == 1 else -step)) % (self.blocks // 4)
        return (z * 2 + x) * 2 + core

    def across_x(self, w):
        z, x, core = self.place(w)
        return (z * 2 + 1 - x) * 2 + 1 - core

    def either(self, of_lead, of_other):
        return [a if lead else b for lead, a, b in zip(self.lead, of_lead, of_other)]

    def moved(self, ids, pairs):
        out = [0] * self.blocks
        for source, target in pairs:
            out[target] = ids[source]
        return out


class Slab:
    def __init__(self, array, ids, far=0):
        self.pieces = list(array) if isinstance(array, (list, tuple)) else [array]
        self.array = self.pieces[0]
        self.ids = ids
        self.far = far


def pick(step, values):
    out = values[0]
    for index, value in enumerate(values):
        if index and value != values[0]:
            out = jnp.where(step == index, value, out)
    return out


def amplitude_call(jobs, table, lines, turned, vir_rows, vir_cols, earlier):
    slabs = []
    for slab, _ in jobs:
        if slab not in slabs:
            slabs.append(slab)
    count, blocks = len(slabs), len(turned)
    cols, aux = turned[0][0].shape[0], sum(piece.shape[1] for piece in turned[0])
    held_rows = aux + TAIL
    pieces = [len(slab.pieces) for slab in slabs]
    begins = [sum(pieces[:s]) for s in range(count)]
    of_job = [slabs.index(slab) for slab, _ in jobs]
    block_of = [block for _, block in jobs]
    far_of = [slab.far for slab, _ in jobs]
    line_of = [lines[slab] for slab, _ in jobs]
    row_pieces = [len(block) for block in turned]
    chunks = aux // CHUNK
    opens = [t for t in range(len(jobs)) if t == 0 or of_job[t] != of_job[t - 1]]
    half = cols // 2

    def kernel(scalars, *refs):
        sources, refs = refs[: sum(pieces)], refs[sum(pieces) :]
        row_sources, refs = refs[: sum(row_pieces)], refs[sum(row_pieces) + len(earlier) :]
        vir_row, vir_col, out, held, rows, held_sems, row_sems = refs
        step = pl.program_id(0)

        def slab_copies(s):
            row = 0
            for index in range(pieces[s]):
                source = sources[begins[s] + index]
                for begin, size in chunks_of(source.shape[0]):
                    target = held.at[s % 2, pl.ds(row, size), :]
                    yield pltpu.make_async_copy(
                        source.at[pl.ds(begin, size)], target, held_sems.at[s % 2, row // CHUNK]
                    )
                    row += size

        def row_copies(block):
            column = 0
            for source in row_sources[sum(row_pieces[:block]) : sum(row_pieces[: block + 1])]:
                for begin, size in chunks_of(source.shape[1]):
                    target = rows.at[block, :, pl.ds(column, size)]
                    yield pltpu.make_async_copy(
                        source.at[:, pl.ds(begin, size)], target, row_sems.at[block, column // CHUNK]
                    )
                    column += size

        @pl.when(step == 0)
        def _():
            for pair in zip(slab_copies(0), row_copies(block_of[0])):
                for copy in pair:
                    copy.start()
            for copy in list(slab_copies(0))[chunks:]:
                copy.start()
            for block in list(dict.fromkeys(block_of))[1:]:
                for copy in row_copies(block):
                    copy.start()

        for s, t in enumerate(opens):

            @pl.when(step == t)
            def _(s=s):
                if s:
                    for copy in slab_copies(s):
                        copy.wait()
                if s + 1 < count:
                    for copy in slab_copies(s + 1):
                        copy.start()

        for block in list(dict.fromkeys(block_of))[1:]:

            @pl.when(step == block_of.index(block))
            def _(block=block):
                for copy in row_copies(block):
                    copy.wait()

        slot = pick(step, [s % 2 for s in of_job])
        block = pick(step, block_of)
        line = pick(step, line_of)
        @pl.when(step == 0)
        def _():
            for copy in list(slab_copies(0))[chunks:]:
                copy.wait()

        plan = held[slot, aux:, :128].astype(jnp.float32)
        lane = lax.broadcasted_iota(jnp.int32, plan.shape, 1).astype(jnp.float32)
        row = lax.broadcasted_iota(jnp.int32, plan.shape, 0)
        told = jnp.where(jnp.logical_and(row == 0, lane == scalars[line, 2]), plan, 0.0)
        weight = scalars[line, 1] + jnp.sum(told, keepdims=True)

        def finish(part, coulomb):
            denominator = (vir_row[0] + vir_col[0, :, part]) - scalars[line, 0]
            out[0, :, part] = (weight * coulomb / denominator).astype(out.dtype)

        @pl.when(step == 0)
        def _():
            coulomb = None
            for index, pair in enumerate(zip(row_copies(block_of[0]), slab_copies(0))):
                for copy in pair:
                    copy.wait()
                chunk = pl.ds(index * CHUNK, CHUNK)
                term = jnp.dot(
                    rows[block_of[0], :, chunk], held[0, chunk, :], preferred_element_type=jnp.float32
                )
                coulomb = term if coulomb is None else coulomb + term
            finish(pl.ds(0, cols), coulomb)

        @pl.when(step > 0)
        def _():
            for begin in range(0, cols, half):
                part = pl.ds(begin, half)
                finish(part, jnp.dot(rows[block], held[slot, :aux, part], preferred_element_type=jnp.float32))

    return pl.pallas_call(
        kernel,
        grid=(len(jobs),),
        in_specs=[pl.BlockSpec(memory_space=pltpu.SMEM)]
        + [pl.BlockSpec(memory_space=pl.ANY)] * (sum(pieces) + sum(row_pieces) + len(earlier))
        + [
            pl.BlockSpec((1, cols, 1), lambda t: (pick(t, block_of), 0, 0)),
            pl.BlockSpec((1, 1, cols), lambda t: (pick(t, far_of), 0, 0)),
        ],
        out_specs=pl.BlockSpec((1, cols, cols), lambda t: (t, 0, 0)),
        out_shape=jax.ShapeDtypeStruct((len(jobs), cols, cols), jnp.bfloat16),
        scratch_shapes=[
            pltpu.VMEM((2, held_rows, cols), jnp.bfloat16),
            pltpu.VMEM((blocks, cols, aux), jnp.bfloat16),
            pltpu.SemaphoreType.DMA((2, chunks + 1)),
            pltpu.SemaphoreType.DMA((blocks, chunks)),
        ],
        compiler_params=pltpu.CompilerParams(vmem_limit_bytes=VMEM),
        cost_estimate=pl.CostEstimate(
            flops=2 * len(jobs) * cols * aux * cols,
            bytes_accessed=2 * cols * (blocks * aux + count * aux + len(jobs) * cols),
            transcendentals=0,
        ),
    )(table, *[p for s in slabs for p in s.pieces], *[p for b in turned for p in b], *earlier, vir_rows, vir_cols)


def chunks_of(rows):
    return [(begin, min(CHUNK, rows - begin)) for begin in range(0, rows, CHUNK)]


def copies_in(sources, held, sems):
    row, index = 0, 0
    for source in sources:
        for begin, size in chunks_of(source.shape[0]):
            yield pltpu.make_async_copy(
                source.at[pl.ds(begin, size)], held.at[pl.ds(row + begin, size)], sems.at[index]
            )
            index += 1
        row += source.shape[0]


def copies_out(held, targets, sems):
    row, index = 0, 0
    for target in targets:
        for begin, size in chunks_of(target.shape[0]):
            yield pltpu.make_async_copy(
                held.at[pl.ds(row + begin, size)], target.at[pl.ds(begin, size)], sems.at[index]
            )
            index += 1
        row += target.shape[0]


def copy_scratch(rows, cols):
    count = len(chunks_of(rows)) + 1
    return [
        pltpu.VMEM((rows, cols), jnp.bfloat16),
        pltpu.SemaphoreType.DMA((count,)),
        pltpu.SemaphoreType.DMA((count,)),
    ]


def copy_through(sources, targets, held, in_sems, out_sems):
    if [x.shape[0] for x in sources] != [x.shape[0] for x in targets]:
        loads, stores = [list(copies_in(sources, held, in_sems))], [list(copies_out(held, targets, out_sems))]
    else:
        loads = [[copy] for copy in copies_in(sources, held, in_sems)]
        stores = [[copy] for copy in copies_out(held, targets, out_sems)]
    for copies in loads:
        for copy in copies:
            copy.start()
    for before, behind in zip(loads, stores):
        for copy in before:
            copy.wait()
        for copy in behind:
            copy.start()
    for copies in stores:
        for copy in copies:
            copy.wait()


def append_call(array, tail, cuts):
    rows, cols = array.shape[0] + tail.shape[0], array.shape[1]
    begins = [0, *cuts, rows]
    sizes = [end - begin for begin, end in zip(begins, begins[1:])]

    def kernel(array_ref, tail_ref, out, *refs):
        pieces, (held, in_sems, out_sems, piece_sems) = refs[: len(sizes)], refs[len(sizes) :]
        loads = list(copies_in([array_ref, tail_ref], held, in_sems))
        stores = list(copies_out(held, [out], out_sems))
        piece_stores = list(copies_out(held, pieces, piece_sems))
        for copy in loads:
            copy.start()
        for load, *behind in zip(loads, stores, piece_stores):
            load.wait()
            for copy in behind:
                copy.start()
        for copy in stores + piece_stores:
            copy.wait()

    scratch = copy_scratch(rows, cols)
    return pl.pallas_call(
        kernel,
        in_specs=[pl.BlockSpec(memory_space=pl.ANY)] * 2,
        out_specs=[pl.BlockSpec(memory_space=pl.ANY)] * (1 + len(sizes)),
        out_shape=[jax.ShapeDtypeStruct((size, cols), array.dtype) for size in (rows, *sizes)],
        scratch_shapes=scratch + scratch[-1:],
        compiler_params=pltpu.CompilerParams(vmem_limit_bytes=VMEM),
    )(array, tail)


def choice_call(flag, a, b, earlier, cuts=(), keep=False):
    rows, cols = a.shape
    begins = [0, *cuts, rows]
    pieces = len(cuts) + 1
    shapes = [(end - begin, cols) for begin, end in zip(begins, begins[1:])]
    kept = [(rows, cols)] if keep else []

    def kernel(flag_ref, a_ref, b_ref, *refs):
        refs = refs[len(earlier) :]
        outs, kept_outs, scratch = refs[:pieces], refs[pieces : pieces + len(kept)], refs[pieces + len(kept) :]
        if keep:
            held, loads, stores, other_held, other_loads, other_stores = scratch
            leads = flag_ref[0] == 1
            ours = list(copies_in([a_ref], held, loads))
            theirs = list(copies_in([b_ref], other_held, other_loads))
            kept_copies = list(copies_out(held, kept_outs, stores))
            ours_out = list(copies_out(held, outs, other_stores))
            theirs_out = list(copies_out(other_held, outs, other_stores))
            for copy in ours:
                copy.start()

            @pl.when(jnp.logical_not(leads))
            def _():
                for copy in theirs:
                    copy.start()

            for load, store, also in zip(ours, kept_copies, ours_out):
                load.wait()
                store.start()
                pl.when(leads)(also.start)

            @pl.when(jnp.logical_not(leads))
            def _():
                for load, store in zip(theirs, theirs_out):
                    load.wait()
                    store.start()

            for store, also in zip(kept_copies, ours_out):
                store.wait()
                also.wait()
        else:
            for value, source in ((1, a_ref), (0, b_ref)):

                @pl.when(flag_ref[0] == value)
                def _(source=source):
                    parts = [source.at[pl.ds(at, out.shape[0])] for at, out in zip(begins, outs)]
                    copy_through(parts, outs, *scratch)

    return pl.pallas_call(
        kernel,
        in_specs=[pl.BlockSpec(memory_space=pltpu.SMEM)]
        + [pl.BlockSpec(memory_space=pl.ANY)] * (2 + len(earlier)),
        out_specs=[pl.BlockSpec(memory_space=pl.ANY)] * (pieces + len(kept)),
        out_shape=[jax.ShapeDtypeStruct(shape, a.dtype) for shape in shapes + kept],
        scratch_shapes=copy_scratch(rows, cols) * (1 + len(kept)),
        compiler_params=pltpu.CompilerParams(vmem_limit_bytes=VMEM),
        cost_estimate=pl.CostEstimate(flops=0, bytes_accessed=2 * a.size * a.dtype.itemsize, transcendentals=0),
    )(flag, a, b, *earlier)


def turn_call(array, rows, earlier):
    cols = array.shape[1]

    def kernel(array_ref, *refs):
        refs[-1][...] = array_ref[...].T

    return pl.pallas_call(
        kernel,
        grid=(rows // CHUNK,),
        in_specs=[pl.BlockSpec((CHUNK, cols), lambda i: (i, 0))]
        + [pl.BlockSpec(memory_space=pl.ANY)] * len(earlier),
        out_specs=pl.BlockSpec((cols, CHUNK), lambda i: (0, i)),
        out_shape=jax.ShapeDtypeStruct((cols, rows), array.dtype),
        compiler_params=pltpu.CompilerParams(vmem_limit_bytes=VMEM),
    )(array, *earlier)


def join_call(earlier):
    def kernel(*refs):
        refs[-1][...] = jnp.zeros_like(refs[-1])

    return pl.pallas_call(
        kernel,
        in_specs=[pl.BlockSpec(memory_space=pl.ANY)] * len(earlier),
        out_specs=pl.BlockSpec(memory_space=pltpu.VMEM),
        out_shape=jax.ShapeDtypeStruct((8, 128), jnp.float32),
    )(*earlier)


def density_call(terms, parts, out_dtype, aux, earlier, rows=None, copied=None, cuts=()):
    count = len(terms)
    depth = terms[0][0].array.shape[1]
    extra = list(copied or [])
    total_rows = sum(x.shape[0] for x in extra)
    ends = [0, *cuts, total_rows]
    whole = [jax.ShapeDtypeStruct((b - a, depth), jnp.bfloat16) for a, b in zip(ends, ends[1:]) if extra]
    pieces = [len(t[0].pieces) for t in terms]
    begins = [sum(pieces[:s]) for s in range(count)]
    cols = depth
    begin, length = rows or (0, aux)
    tile = 512
    while length % tile or begin % tile:
        tile //= 2
    steps = length // tile
    spans = []
    for part in parts:
        ends = np.cumsum([piece.shape[0] // tile for piece in part])
        shift = begin // tile if ends[-1] == aux // tile else 0
        spans.append([(int(end) - piece.shape[0] // tile - shift, int(end) - shift) for end, piece in zip(ends, part)])
    parts = [p for part in parts for p in part]

    def kernel(*refs):
        sources, refs = refs[: sum(pieces)], refs[sum(pieces) :]
        amps, refs = refs[:count], refs[count + len(earlier) :]
        source, refs = refs[: len(extra)], refs[len(extra) :]
        part_refs, out, refs = refs[: len(parts)], refs[len(parts)], refs[len(parts) + 1 :]
        target, refs = refs[: len(whole)], refs[len(whole) :]
        (left, right, left_sems, right_sems), scratch = refs[:4], refs[4:]
        step = pl.program_id(0)
        slot = step % 2

        def amp_copies():
            for s, (_, _, place) in enumerate(terms):
                yield pltpu.make_async_copy(
                    amps[s].at[place], right.at[:, pl.ds(s * depth, depth)], right_sems.at[s]
                )

        def slab_copies(which, start, of=range(count)):
            for s in of:
                end = 0
                for index in range(pieces[s]):
                    source = sources[begins[s] + index]
                    first = end
                    end += source.shape[0] // tile

                    def act(source=source, first=first, s=s):
                        row = pl.multiple_of((begin // tile + which - first) * tile, tile)
                        copy = pltpu.make_async_copy(
                            source.at[pl.ds(row, tile), :],
                            left.at[which % 2, :, pl.ds(s * depth, depth)],
                            left_sems.at[which % 2, s],
                        )
                        copy.start() if start else copy.wait()

                    at = begin // tile + which
                    if pieces[s] == 1:
                        act()
                    else:
                        pl.when(jnp.logical_and(at >= first, at < end))(act)

        @pl.when(step == 0)
        def _():
            for s, copy in enumerate(amp_copies()):
                copy.start()
                slab_copies(step, True, [s])
            if extra:
                for copy in copies_in(source, scratch[0], scratch[1]):
                    copy.start()

        @pl.when(step + 1 < steps)
        def _():
            slab_copies(step + 1, True)

        def finish(total):
            at = 0
            for span in spans:
                part = part_refs[at][...]
                for index in range(1, len(span)):
                    part = jnp.where(step >= span[index][0], part_refs[at + index][...], part)
                total = total + part.astype(jnp.float32)
                at += len(span)
            out[...] = total.astype(out.dtype)

        def product(a, b):
            return lax.dot_general(a, b, (((1,), (1,)), ((), ())), preferred_element_type=jnp.float32)

        @pl.when(step == 0)
        def _():
            total = None
            for s, copy in enumerate(amp_copies()):
                copy.wait()
                slab_copies(step, False, [s])
                at = pl.ds(s * depth, depth)
                term = product(left[0, :, at], right[:, at])
                total = term if total is None else total + term
            finish(total)

        @pl.when(step > 0)
        def _():
            slab_copies(step, False)
            finish(product(left[slot], right[...]))

        if extra:

            @pl.when(step == 1)
            def _():
                for copy in copies_in(source, scratch[0], scratch[1]):
                    copy.wait()
                for copy in copies_out(scratch[0], target, scratch[2]):
                    copy.start()

            @pl.when(step == steps - 1)
            def _():
                for copy in copies_out(scratch[0], target, scratch[2]):
                    copy.wait()

    def rows_of(start, end):
        return pl.BlockSpec((tile, cols), lambda i: (jnp.clip(i - start, 0, end - start - 1), 0))

    bytes_moved = 2 * count * (length * depth + cols * depth)
    bytes_moved += sum(length * cols * p.dtype.itemsize for p in parts)
    return pl.pallas_call(
        kernel,
        grid=(steps,),
        in_specs=[pl.BlockSpec(memory_space=pl.ANY)] * (sum(pieces) + count + len(earlier) + len(extra))
        + [rows_of(*ends) for span in spans for ends in span],
        out_specs=[pl.BlockSpec((tile, cols), lambda i: (i, 0))]
        + [pl.BlockSpec(memory_space=pl.ANY)] * len(whole),
        out_shape=[jax.ShapeDtypeStruct((length, cols), out_dtype)]
        + whole,
        scratch_shapes=[
            pltpu.VMEM((2, tile, count * depth), jnp.bfloat16),
            pltpu.VMEM((cols, count * depth), jnp.bfloat16),
            pltpu.SemaphoreType.DMA((2, count)),
            pltpu.SemaphoreType.DMA((count,)),
            *(copy_scratch(total_rows, depth) if extra else []),
        ],
        compiler_params=pltpu.CompilerParams(vmem_limit_bytes=VMEM),
        cost_estimate=pl.CostEstimate(
            flops=2 * length * depth * cols * count,
            bytes_accessed=(bytes_moved + length * cols * jnp.dtype(out_dtype).itemsize),
            transcendentals=0,
        ),
    )(*[p for t in terms for p in t[0].pieces], *[t[1] for t in terms], *earlier, *extra, *parts)


def paired_plan(three_index, orbital_map, occ_energy, vir_energy, pair_kept):
    blocks = lax.axis_size("wide")
    routes = Routes(blocks)
    here = lax.axis_index("wide")
    side = lax.axis_index("narrow")
    aux, vir_count = three_index.shape[1:]

    def moved(slab, pairs):
        sent = [lax.ppermute(piece, "wide", pairs) for piece in slab.pieces]
        return Slab(sent, routes.moved(slab.ids, pairs), slab.far)

    def swapped(slab):
        return moved(slab, routes.swap)

    flag = jnp.asarray(np.array(routes.lead, np.int32))[here].reshape(1)

    def copied(array, *earlier, cuts=()):
        return choice_call(flag, array, array, earlier, cuts)

    def sibling(array):
        return lax.ppermute(array, "narrow", [(0, 1), (1, 0)])

    plan = jnp.zeros((TAIL, vir_count), jnp.bfloat16)
    plan = plan.at[0, : ROUNDS + 1].set(pair_kept[:, 0].astype(jnp.bfloat16))
    whole, *split = append_call(three_index[0], plan, [aux // 2])
    own = Slab(whole, list(range(blocks)))

    r1 = moved(own, routes.rounds[0])
    own_far = Slab([sibling(piece) for piece in split], own.ids, 1)
    mate = swapped(own)

    labels = jnp.arange(occ_energy.shape[0], dtype=jnp.int32)
    picked = orbital_map[:, None] == labels[None, :]
    energy = jnp.sum(jnp.where(picked, occ_energy[None, :], 0.0), axis=1)

    def table_of(ids):
        ids = np.array(ids, np.int32).T
        places = np.arange(blocks)[:, None]
        back, forth = (places - ids) % blocks, (ids - places) % blocks
        behind = back <= ROUNDS
        known = np.stack([ids, np.where(behind, back, -1), np.where(behind, -1, forth)])
        block, mine, theirs = jnp.asarray(known.astype(np.int32))[:, here]
        places = jnp.arange(blocks, dtype=jnp.int32)[None, :]
        both = jnp.where(places == here, energy[None, :], 0.0)
        both = both + jnp.where(places == block[:, None], energy[None, :], 0.0)
        entries = jnp.arange(ROUNDS + 1, dtype=jnp.int32)[None, :]
        kept = pair_kept[:, 0].astype(jnp.float32)[None, :]
        weight = jnp.sum(jnp.where(entries == mine[:, None], kept, 0.0), axis=1)
        return jnp.stack([jnp.sum(both, axis=1), weight, theirs.astype(jnp.float32)], axis=1)

    vir = jnp.stack(
        [lax.dynamic_slice_in_dim(vir_energy, s * vir_count, vir_count) for s in (side, 1 - side)]
    )
    vir_rows, vir_cols = vir[:, :, None], vir[:, None, :]

    def moved_ids(ids_lead, ids_other, pairs):
        return routes.moved(routes.either(ids_lead, ids_other), pairs)

    def swapped_ids(ids):
        return routes.moved(ids, routes.swap)

    r2_ids = moved_ids(own.ids, r1.ids, routes.rounds[1])
    r3_ids = moved_ids(r2_ids, own.ids, routes.rounds[2])
    r4_ids = routes.moved(r3_ids, routes.rounds[3])
    r5_ids = routes.moved(own.ids, routes.rounds[4])
    all_ids = [own.ids, mate.ids]
    for ids in (r1.ids, r2_ids, r3_ids, r4_ids, r5_ids):
        all_ids += [ids, swapped_ids(ids)]
    table = table_of(all_ids)
    near, far = 0, 1
    rows_near = [own.array[:aux].T]
    stacks = {}

    def amps(jobs, turned, *earlier):
        lines = {slab: all_ids.index(slab.ids) for slab, _ in jobs}
        stack = amplitude_call(jobs, table, lines, turned, vir_rows, vir_cols, earlier)
        for place, job in enumerate(jobs):
            stacks[job] = (stack, place)
        return stack

    def density(slabs, block, parts, dtype, *earlier, rows=None, copied=None, cuts=()):
        terms = [(slab, *stacks[slab, block]) for slab in slabs]
        out, *copy = density_call(terms, parts, dtype, aux, earlier, rows, copied, cuts)
        return (out, *copy) if copy else out

    f32, bf16 = jnp.float32, jnp.bfloat16
    done = amps([(own, near), (mate, near)], [rows_near])

    parts = own_far.pieces
    sent, kept = choice_call(1 - flag, r1.array, own.array, [parts[0], done], keep=True)
    r1 = Slab(kept, r1.ids)
    sent2 = Slab(sent, routes.either(own.ids, r1.ids))
    r2 = moved(sent2, routes.rounds[1])
    s1 = swapped(r1)
    done = amps([(r1, near), (s1, near)], [rows_near], sent2.array)
    part = density([own, mate, r1, s1], near, [], f32, done)
    cut = parts[0].shape[0]
    rows_far = [turn_call(parts[0], cut, [part])]

    sent, kept = choice_call(flag, r2.array, own.array, [parts[1], *rows_far], keep=True)
    r2 = Slab(kept, r2.ids)
    sent3 = Slab(sent, routes.either(r2.ids, own.ids))
    r3 = moved(sent3, routes.rounds[2])
    s2 = swapped(r2)
    mate_far = swapped(own_far)
    rows_far.append(turn_call(parts[1], aux - cut, [sent3.array]))
    jobs = [(r2, near), (r2, far), (s2, far), (s2, near), (r1, far), (s1, far)]
    done = amps(jobs, [rows_near, rows_far])
    part = density([r2, s2], near, [[part]], f32, done)

    r3 = Slab(copied(r3.array, part), r3.ids)
    r4 = moved(r3, routes.rounds[3])
    s3 = swapped(r3)
    out_part, again = density([r1, s1, r2, s2], far, [], f32, r3.array, copied=own.pieces)
    r5 = moved(Slab(again, own.ids), routes.rounds[4])
    jobs = [(own_far, near), (mate_far, near), (r3, near), (r3, far), (s3, far), (s3, near)]
    done = amps(jobs, [rows_near, rows_far], out_part)

    done = amps([(r4, far)], [rows_near, rows_far], done)
    half = aux // 2
    slabs = [r3, s3, r4]
    sent0, again = density(
        slabs, far, [[out_part]], bf16, done, rows=(0, half), copied=own_far.pieces
    )
    r6 = moved(Slab(again, own.ids, 1), routes.rounds[4])
    sent1 = density(slabs, far, [[out_part]], bf16, sent0, rows=(half, half))
    incoming = [sibling(sent0), sibling(sent1)]
    done = amps([(r4, near)], [rows_near], sent1)

    thirds = [aux // 3, aux // 3 * 2]
    r5 = Slab(copied(r5.array, done, cuts=thirds), r5.ids)
    s5 = swapped(r5)
    done = amps([(r5, near)], [rows_near], *r5.pieces)
    done = join_call([incoming[0], done])
    done = amps([(s5, near)], [rows_near], done)
    part = density([own_far, mate_far, r3, s3, r4, r5, s5], near, [[part]], f32, done)
    r6 = Slab(copied(r6.array, part, cuts=thirds), r6.ids, 1)
    s6 = swapped(r6)
    done = amps([(r6, near)], [rows_near], *r6.pieces)
    done = amps([(s6, near)], [rows_near], done)
    return density([r6, s6], near, [[part], incoming], f32, done)[None]


def solution(mesh):
    wide, narrow = mesh.shape["wide"], mesh.shape["narrow"]
    paired = narrow == 2 and wide % 4 == 0 and wide > 2 * ROUNDS + 1 and ROUNDS == 5

    def per_device(three_index, *rest):
        if paired and three_index.shape[0] == 1:
            return paired_plan(three_index, *rest)
        return ring_plan(three_index, *rest)

    placed = (P("wide", None, "narrow"), P(), P(), P(), P(None, "wide"))
    return jax.shard_map(
        per_device, mesh=mesh, in_specs=placed, out_specs=P("wide", None, "narrow"), check_vma=False
    )
```

```python
import jax
import jax.numpy as jnp
import numpy as np
from jax import lax
from jax.experimental import pallas as pl
from jax.experimental.pallas import tpu as pltpu
from jax.sharding import PartitionSpec as P

ROUNDS = 5
TAIL = 16
CHUNK = 512
VMEM = 48 * 1024 * 1024


def passed_along(array, axis, by):
    length = lax.axis_size(axis)
    return lax.ppermute(array, axis, [(i, (i + by) % length) for i in range(length)])


def block_energy(orbital_map, occ_energy, block_id, occ_count):
    orbits = lax.dynamic_slice_in_dim(orbital_map, block_id * occ_count, occ_count)
    labels = jnp.arange(occ_energy.shape[0], dtype=jnp.int32)
    chosen = orbits[:, None] == labels[None, :]
    return jnp.sum(jnp.where(chosen, occ_energy[None, :], 0.0), axis=1)


def amplitudes(gathered, visiting, left_energy, right_energy, vir_all, vir_local, weight):
    coulomb = jnp.einsum("ipa,jpb->ijab", gathered, visiting, preferred_element_type=jnp.float32)
    denominator = (vir_all[:, None] + vir_local[None, :])[None, None] - (
        left_energy[:, None] + right_energy[None, :]
    )[:, :, None, None]
    return (weight * coulomb / denominator).astype(jnp.bfloat16)


def ring_plan(three_index, orbital_map, occ_energy, vir_energy, pair_kept):
    occ_count = three_index.shape[0]
    vir_count = three_index.shape[2]
    blocks = lax.axis_size("wide")
    own_block = lax.axis_index("wide")
    vir_local = lax.dynamic_slice_in_dim(
        vir_energy, lax.axis_index("narrow") * vir_count, vir_count
    )
    own_energy = block_energy(orbital_map, occ_energy, own_block, occ_count)
    weights = pair_kept.astype(jnp.float32)
    gathered = lax.all_gather(three_index, "narrow", axis=2, tiled=True)
    amplitude = amplitudes(
        gathered, three_index, own_energy, own_energy, vir_energy, vir_local, weights[0, 0]
    )
    forward = jnp.einsum(
        "ijab,jpb->ipa", amplitude, three_index, preferred_element_type=jnp.float32
    )
    visiting = three_index
    stored_amps = []
    for round_index in range(1, ROUNDS + 1):
        visiting = passed_along(visiting, "wide", 1)
        partner = (own_block - round_index) % blocks
        partner_energy = block_energy(orbital_map, occ_energy, partner, occ_count)
        amplitude = amplitudes(
            gathered,
            visiting,
            own_energy,
            partner_energy,
            vir_energy,
            vir_local,
            weights[round_index, 0],
        )
        forward = forward + jnp.einsum(
            "ijab,jpb->ipa", amplitude, visiting, preferred_element_type=jnp.float32
        )
        stored_amps.append(amplitude)
    carried = None
    for round_index in range(1, ROUNDS + 1):
        backward = jnp.einsum(
            "ijab,ipa->jpb",
            stored_amps[round_index - 1],
            gathered,
            preferred_element_type=jnp.float32,
        )
        if round_index > 1:
            carried = passed_along(carried, "wide", 1) + backward
        else:
            carried = backward
    returned = passed_along(carried, "wide", -ROUNDS)
    scattered = lax.psum_scatter(forward, "narrow", scatter_dimension=2, tiled=True)
    return scattered + returned


class Routes:
    def __init__(self, blocks):
        self.blocks = blocks
        everyone = range(blocks)
        self.lead = [self.place(w)[1] == self.place(w)[2] for w in everyone]
        self.swap = [(w, w ^ 1) for w in everyone]
        onward = [(w, self.along_z(w, 1)) for w in everyone]
        backward = [(w, self.along_z(w, -1)) for w in everyone]
        across = [(w, self.across_x(w)) for w in everyone]
        self.rounds = [
            self.either(across, onward),
            self.either(onward, across),
            self.either(across, backward),
            self.either(backward, across),
            self.either(backward, across),
        ]

    def place(self, w):
        return w // 4, (w // 2) % 2, w % 2

    def along_z(self, w, step):
        z, x, core = self.place(w)
        z = (z + (step if x == 1 else -step)) % (self.blocks // 4)
        return (z * 2 + x) * 2 + core

    def across_x(self, w):
        z, x, core = self.place(w)
        return (z * 2 + 1 - x) * 2 + 1 - core

    def either(self, of_lead, of_other):
        return [a if lead else b for lead, a, b in zip(self.lead, of_lead, of_other)]

    def moved(self, ids, pairs):
        out = [0] * self.blocks
        for source, target in pairs:
            out[target] = ids[source]
        return out


class Slab:
    def __init__(self, array, ids, far=0):
        self.pieces = list(array) if isinstance(array, (list, tuple)) else [array]
        self.array = self.pieces[0]
        self.ids = ids
        self.far = far


def pick(step, values):
    out = values[0]
    for index, value in enumerate(values):
        if index and value != values[0]:
            out = jnp.where(step == index, value, out)
    return out


def amplitude_call(jobs, table, lines, turned, vir_rows, vir_cols, earlier):
    slabs = []
    for slab, _ in jobs:
        if slab not in slabs:
            slabs.append(slab)
    count, blocks = len(slabs), len(turned)
    cols, aux = turned[0][0].shape[0], sum(piece.shape[1] for piece in turned[0])
    held_rows = aux + TAIL
    pieces = [len(slab.pieces) for slab in slabs]
    begins = [sum(pieces[:s]) for s in range(count)]
    of_job = [slabs.index(slab) for slab, _ in jobs]
    block_of = [block for _, block in jobs]
    far_of = [slab.far for slab, _ in jobs]
    line_of = [lines[slab] for slab, _ in jobs]
    row_pieces = [len(block) for block in turned]
    chunks = aux // CHUNK
    opens = [t for t in range(len(jobs)) if t == 0 or of_job[t] != of_job[t - 1]]
    half = cols // 2

    def kernel(scalars, *refs):
        sources, refs = refs[: sum(pieces)], refs[sum(pieces) :]
        row_sources, refs = refs[: sum(row_pieces)], refs[sum(row_pieces) + len(earlier) :]
        vir_row, vir_col, out, held, rows, held_sems, row_sems = refs
        step = pl.program_id(0)

        def slab_copies(s):
            row = 0
            for index in range(pieces[s]):
                source = sources[begins[s] + index]
                for begin, size in chunks_of(source.shape[0]):
                    target = held.at[s % 2, pl.ds(row, size), :]
                    yield pltpu.make_async_copy(
                        source.at[pl.ds(begin, size)], target, held_sems.at[s % 2, row // CHUNK]
                    )
                    row += size

        def row_copies(block):
            column = 0
            for source in row_sources[sum(row_pieces[:block]) : sum(row_pieces[: block + 1])]:
                for begin, size in chunks_of(source.shape[1]):
                    target = rows.at[block, :, pl.ds(column, size)]
                    yield pltpu.make_async_copy(
                        source.at[:, pl.ds(begin, size)], target, row_sems.at[block, column // CHUNK]
                    )
                    column += size

        @pl.when(step == 0)
        def _():
            for pair in zip(slab_copies(0), row_copies(block_of[0])):
                for copy in pair:
                    copy.start()
            for copy in list(slab_copies(0))[chunks:]:
                copy.start()
            for block in list(dict.fromkeys(block_of))[1:]:
                for copy in row_copies(block):
                    copy.start()

        for s, t in enumerate(opens):

            @pl.when(step == t)
            def _(s=s):
                if s:
                    for copy in slab_copies(s):
                        copy.wait()
                if s + 1 < count:
                    for copy in slab_copies(s + 1):
                        copy.start()

        for block in list(dict.fromkeys(block_of))[1:]:

            @pl.when(step == block_of.index(block))
            def _(block=block):
                for copy in row_copies(block):
                    copy.wait()

        slot = pick(step, [s % 2 for s in of_job])
        block = pick(step, block_of)
        line = pick(step, line_of)
        @pl.when(step == 0)
        def _():
            for copy in list(slab_copies(0))[chunks:]:
                copy.wait()

        plan = held[slot, aux:, :128].astype(jnp.float32)
        lane = lax.broadcasted_iota(jnp.int32, plan.shape, 1).astype(jnp.float32)
        row = lax.broadcasted_iota(jnp.int32, plan.shape, 0)
        told = jnp.where(jnp.logical_and(row == 0, lane == scalars[line, 2]), plan, 0.0)
        weight = scalars[line, 1] + jnp.sum(told, keepdims=True)

        def finish(part, coulomb):
            denominator = (vir_row[0] + vir_col[0, :, part]) - scalars[line, 0]
            out[0, :, part] = (weight * coulomb / denominator).astype(out.dtype)

        @pl.when(step == 0)
        def _():
            coulomb = None
            for index, pair in enumerate(zip(row_copies(block_of[0]), slab_copies(0))):
                for copy in pair:
                    copy.wait()
                chunk = pl.ds(index * CHUNK, CHUNK)
                term = jnp.dot(
                    rows[block_of[0], :, chunk], held[0, chunk, :], preferred_element_type=jnp.float32
                )
                coulomb = term if coulomb is None else coulomb + term
            finish(pl.ds(0, cols), coulomb)

        @pl.when(step > 0)
        def _():
            for begin in range(0, cols, half):
                part = pl.ds(begin, half)
                finish(part, jnp.dot(rows[block], held[slot, :aux, part], preferred_element_type=jnp.float32))

    return pl.pallas_call(
        kernel,
        grid=(len(jobs),),
        in_specs=[pl.BlockSpec(memory_space=pltpu.SMEM)]
        + [pl.BlockSpec(memory_space=pl.ANY)] * (sum(pieces) + sum(row_pieces) + len(earlier))
        + [
            pl.BlockSpec((1, cols, 1), lambda t: (pick(t, block_of), 0, 0)),
            pl.BlockSpec((1, 1, cols), lambda t: (pick(t, far_of), 0, 0)),
        ],
        out_specs=pl.BlockSpec((1, cols, cols), lambda t: (t, 0, 0)),
        out_shape=jax.ShapeDtypeStruct((len(jobs), cols, cols), jnp.bfloat16),
        scratch_shapes=[
            pltpu.VMEM((2, held_rows, cols), jnp.bfloat16),
            pltpu.VMEM((blocks, cols, aux), jnp.bfloat16),
            pltpu.SemaphoreType.DMA((2, chunks + 1)),
            pltpu.SemaphoreType.DMA((blocks, chunks)),
        ],
        compiler_params=pltpu.CompilerParams(vmem_limit_bytes=VMEM),
        cost_estimate=pl.CostEstimate(
            flops=2 * len(jobs) * cols * aux * cols,
            bytes_accessed=2 * cols * (blocks * aux + count * aux + len(jobs) * cols),
            transcendentals=0,
        ),
    )(table, *[p for s in slabs for p in s.pieces], *[p for b in turned for p in b], *earlier, vir_rows, vir_cols)


def chunks_of(rows):
    return [(begin, min(CHUNK, rows - begin)) for begin in range(0, rows, CHUNK)]


def copies_in(sources, held, sems):
    row, index = 0, 0
    for source in sources:
        for begin, size in chunks_of(source.shape[0]):
            yield pltpu.make_async_copy(
                source.at[pl.ds(begin, size)], held.at[pl.ds(row + begin, size)], sems.at[index]
            )
            index += 1
        row += source.shape[0]


def copies_out(held, targets, sems):
    row, index = 0, 0
    for target in targets:
        for begin, size in chunks_of(target.shape[0]):
            yield pltpu.make_async_copy(
                held.at[pl.ds(row + begin, size)], target.at[pl.ds(begin, size)], sems.at[index]
            )
            index += 1
        row += target.shape[0]


def copy_scratch(rows, cols):
    count = len(chunks_of(rows)) + 1
    return [
        pltpu.VMEM((rows, cols), jnp.bfloat16),
        pltpu.SemaphoreType.DMA((count,)),
        pltpu.SemaphoreType.DMA((count,)),
    ]


def copy_through(sources, targets, held, in_sems, out_sems):
    if [x.shape[0] for x in sources] != [x.shape[0] for x in targets]:
        loads, stores = [list(copies_in(sources, held, in_sems))], [list(copies_out(held, targets, out_sems))]
    else:
        loads = [[copy] for copy in copies_in(sources, held, in_sems)]
        stores = [[copy] for copy in copies_out(held, targets, out_sems)]
    for copies in loads:
        for copy in copies:
            copy.start()
    for before, behind in zip(loads, stores):
        for copy in before:
            copy.wait()
        for copy in behind:
            copy.start()
    for copies in stores:
        for copy in copies:
            copy.wait()


def append_call(array, tail, cuts):
    rows, cols = array.shape[0] + tail.shape[0], array.shape[1]
    begins = [0, *cuts, rows]
    sizes = [end - begin for begin, end in zip(begins, begins[1:])]

    def kernel(array_ref, tail_ref, out, *refs):
        pieces, (held, in_sems, out_sems, piece_sems) = refs[: len(sizes)], refs[len(sizes) :]
        loads = list(copies_in([array_ref, tail_ref], held, in_sems))
        stores = list(copies_out(held, [out], out_sems))
        piece_stores = list(copies_out(held, pieces, piece_sems))
        for copy in loads:
            copy.start()
        for load, *behind in zip(loads, stores, piece_stores):
            load.wait()
            for copy in behind:
                copy.start()
        for copy in stores + piece_stores:
            copy.wait()

    scratch = copy_scratch(rows, cols)
    return pl.pallas_call(
        kernel,
        in_specs=[pl.BlockSpec(memory_space=pl.ANY)] * 2,
        out_specs=[pl.BlockSpec(memory_space=pl.ANY)] * (1 + len(sizes)),
        out_shape=[jax.ShapeDtypeStruct((size, cols), array.dtype) for size in (rows, *sizes)],
        scratch_shapes=scratch + scratch[-1:],
        compiler_params=pltpu.CompilerParams(vmem_limit_bytes=VMEM),
    )(array, tail)


def choice_call(flag, a, b, earlier, cuts=(), keep=False):
    rows, cols = a.shape
    begins = [0, *cuts, rows]
    pieces = len(cuts) + 1
    shapes = [(end - begin, cols) for begin, end in zip(begins, begins[1:])]
    kept = [(rows, cols)] if keep else []

    def kernel(flag_ref, a_ref, b_ref, *refs):
        refs = refs[len(earlier) :]
        outs, kept_outs, scratch = refs[:pieces], refs[pieces : pieces + len(kept)], refs[pieces + len(kept) :]
        if keep:
            held, loads, stores, other_held, other_loads, other_stores = scratch
            leads = flag_ref[0] == 1
            ours = list(copies_in([a_ref], held, loads))
            theirs = list(copies_in([b_ref], other_held, other_loads))
            kept_copies = list(copies_out(held, kept_outs, stores))
            ours_out = list(copies_out(held, outs, other_stores))
            theirs_out = list(copies_out(other_held, outs, other_stores))
            for copy in ours:
                copy.start()

            @pl.when(jnp.logical_not(leads))
            def _():
                for copy in theirs:
                    copy.start()

            for load, store, also in zip(ours, kept_copies, ours_out):
                load.wait()
                store.start()
                pl.when(leads)(also.start)

            @pl.when(jnp.logical_not(leads))
            def _():
                for load, store in zip(theirs, theirs_out):
                    load.wait()
                    store.start()

            for store, also in zip(kept_copies, ours_out):
                store.wait()
                also.wait()
        else:
            for value, source in ((1, a_ref), (0, b_ref)):

                @pl.when(flag_ref[0] == value)
                def _(source=source):
                    parts = [source.at[pl.ds(at, out.shape[0])] for at, out in zip(begins, outs)]
                    copy_through(parts, outs, *scratch)

    return pl.pallas_call(
        kernel,
        in_specs=[pl.BlockSpec(memory_space=pltpu.SMEM)]
        + [pl.BlockSpec(memory_space=pl.ANY)] * (2 + len(earlier)),
        out_specs=[pl.BlockSpec(memory_space=pl.ANY)] * (pieces + len(kept)),
        out_shape=[jax.ShapeDtypeStruct(shape, a.dtype) for shape in shapes + kept],
        scratch_shapes=copy_scratch(rows, cols) * (1 + len(kept)),
        compiler_params=pltpu.CompilerParams(vmem_limit_bytes=VMEM),
        cost_estimate=pl.CostEstimate(flops=0, bytes_accessed=2 * a.size * a.dtype.itemsize, transcendentals=0),
    )(flag, a, b, *earlier)


def turn_call(array, rows, earlier):
    cols = array.shape[1]

    def kernel(array_ref, *refs):
        refs[-1][...] = array_ref[...].T

    return pl.pallas_call(
        kernel,
        grid=(rows // CHUNK,),
        in_specs=[pl.BlockSpec((CHUNK, cols), lambda i: (i, 0))]
        + [pl.BlockSpec(memory_space=pl.ANY)] * len(earlier),
        out_specs=pl.BlockSpec((cols, CHUNK), lambda i: (0, i)),
        out_shape=jax.ShapeDtypeStruct((cols, rows), array.dtype),
        compiler_params=pltpu.CompilerParams(vmem_limit_bytes=VMEM),
    )(array, *earlier)


def join_call(earlier):
    def kernel(*refs):
        refs[-1][...] = jnp.zeros_like(refs[-1])

    return pl.pallas_call(
        kernel,
        in_specs=[pl.BlockSpec(memory_space=pl.ANY)] * len(earlier),
        out_specs=pl.BlockSpec(memory_space=pltpu.VMEM),
        out_shape=jax.ShapeDtypeStruct((8, 128), jnp.float32),
    )(*earlier)


def density_call(terms, parts, out_dtype, aux, earlier, rows=None, copied=None, cuts=()):
    count = len(terms)
    depth = terms[0][0].array.shape[1]
    extra = list(copied or [])
    total_rows = sum(x.shape[0] for x in extra)
    ends = [0, *cuts, total_rows]
    whole = [jax.ShapeDtypeStruct((b - a, depth), jnp.bfloat16) for a, b in zip(ends, ends[1:]) if extra]
    pieces = [len(t[0].pieces) for t in terms]
    begins = [sum(pieces[:s]) for s in range(count)]
    cols = depth
    begin, length = rows or (0, aux)
    tile = 512
    while length % tile or begin % tile:
        tile //= 2
    steps = length // tile
    spans = []
    for part in parts:
        ends = np.cumsum([piece.shape[0] // tile for piece in part])
        shift = begin // tile if ends[-1] == aux // tile else 0
        spans.append([(int(end) - piece.shape[0] // tile - shift, int(end) - shift) for end, piece in zip(ends, part)])
    parts = [p for part in parts for p in part]

    def kernel(*refs):
        sources, refs = refs[: sum(pieces)], refs[sum(pieces) :]
        amps, refs = refs[:count], refs[count + len(earlier) :]
        source, refs = refs[: len(extra)], refs[len(extra) :]
        part_refs, out, refs = refs[: len(parts)], refs[len(parts)], refs[len(parts) + 1 :]
        target, refs = refs[: len(whole)], refs[len(whole) :]
        (left, right, left_sems, right_sems), scratch = refs[:4], refs[4:]
        step = pl.program_id(0)
        slot = step % 2

        def amp_copies():
            for s, (_, _, place) in enumerate(terms):
                yield pltpu.make_async_copy(
                    amps[s].at[place], right.at[:, pl.ds(s * depth, depth)], right_sems.at[s]
                )

        def slab_copies(which, start, of=range(count)):
            for s in of:
                end = 0
                for index in range(pieces[s]):
                    source = sources[begins[s] + index]
                    first = end
                    end += source.shape[0] // tile

                    def act(source=source, first=first, s=s):
                        row = pl.multiple_of((begin // tile + which - first) * tile, tile)
                        copy = pltpu.make_async_copy(
                            source.at[pl.ds(row, tile), :],
                            left.at[which % 2, :, pl.ds(s * depth, depth)],
                            left_sems.at[which % 2, s],
                        )
                        copy.start() if start else copy.wait()

                    at = begin // tile + which
                    if pieces[s] == 1:
                        act()
                    else:
                        pl.when(jnp.logical_and(at >= first, at < end))(act)

        @pl.when(step == 0)
        def _():
            for s, copy in enumerate(amp_copies()):
                copy.start()
                slab_copies(step, True, [s])
            if extra:
                for copy in copies_in(source, scratch[0], scratch[1]):
                    copy.start()

        @pl.when(step + 1 < steps)
        def _():
            slab_copies(step + 1, True)

        def finish(total):
            at = 0
            for span in spans:
                part = part_refs[at][...]
                for index in range(1, len(span)):
                    part = jnp.where(step >= span[index][0], part_refs[at + index][...], part)
                total = total + part.astype(jnp.float32)
                at += len(span)
            out[...] = total.astype(out.dtype)

        def product(a, b):
            return lax.dot_general(a, b, (((1,), (1,)), ((), ())), preferred_element_type=jnp.float32)

        @pl.when(step == 0)
        def _():
            total = None
            for s, copy in enumerate(amp_copies()):
                copy.wait()
                slab_copies(step, False, [s])
                at = pl.ds(s * depth, depth)
                term = product(left[0, :, at], right[:, at])
                total = term if total is None else total + term
            finish(total)

        @pl.when(step > 0)
        def _():
            slab_copies(step, False)
            finish(product(left[slot], right[...]))

        if extra:

            @pl.when(step == 1)
            def _():
                for copy in copies_in(source, scratch[0], scratch[1]):
                    copy.wait()
                for copy in copies_out(scratch[0], target, scratch[2]):
                    copy.start()

            @pl.when(step == steps - 1)
            def _():
                for copy in copies_out(scratch[0], target, scratch[2]):
                    copy.wait()

    def rows_of(start, end):
        return pl.BlockSpec((tile, cols), lambda i: (jnp.clip(i - start, 0, end - start - 1), 0))

    bytes_moved = 2 * count * (length * depth + cols * depth)
    bytes_moved += sum(length * cols * p.dtype.itemsize for p in parts)
    return pl.pallas_call(
        kernel,
        grid=(steps,),
        in_specs=[pl.BlockSpec(memory_space=pl.ANY)] * (sum(pieces) + count + len(earlier) + len(extra))
        + [rows_of(*ends) for span in spans for ends in span],
        out_specs=[pl.BlockSpec((tile, cols), lambda i: (i, 0))]
        + [pl.BlockSpec(memory_space=pl.ANY)] * len(whole),
        out_shape=[jax.ShapeDtypeStruct((length, cols), out_dtype)]
        + whole,
        scratch_shapes=[
            pltpu.VMEM((2, tile, count * depth), jnp.bfloat16),
            pltpu.VMEM((cols, count * depth), jnp.bfloat16),
            pltpu.SemaphoreType.DMA((2, count)),
            pltpu.SemaphoreType.DMA((count,)),
            *(copy_scratch(total_rows, depth) if extra else []),
        ],
        compiler_params=pltpu.CompilerParams(vmem_limit_bytes=VMEM),
        cost_estimate=pl.CostEstimate(
            flops=2 * length * depth * cols * count,
            bytes_accessed=(bytes_moved + length * cols * jnp.dtype(out_dtype).itemsize),
            transcendentals=0,
        ),
    )(*[p for t in terms for p in t[0].pieces], *[t[1] for t in terms], *earlier, *extra, *parts)


def paired_plan(three_index, orbital_map, occ_energy, vir_energy, pair_kept):
    blocks = lax.axis_size("wide")
    routes = Routes(blocks)
    here = lax.axis_index("wide")
    side = lax.axis_index("narrow")
    aux, vir_count = three_index.shape[1:]

    def moved(slab, pairs):
        sent = [lax.ppermute(piece, "wide", pairs) for piece in slab.pieces]
        return Slab(sent, routes.moved(slab.ids, pairs), slab.far)

    def swapped(slab):
        return moved(slab, routes.swap)

    flag = jnp.asarray(np.array(routes.lead, np.int32))[here].reshape(1)

    def copied(array, *earlier, cuts=()):
        return choice_call(flag, array, array, earlier, cuts)

    def sibling(array):
        return lax.ppermute(array, "narrow", [(0, 1), (1, 0)])

    plan = jnp.zeros((TAIL, vir_count), jnp.bfloat16)
    plan = plan.at[0, : ROUNDS + 1].set(pair_kept[:, 0].astype(jnp.bfloat16))
    whole, *split = append_call(three_index[0], plan, [aux // 2])
    own = Slab(whole, list(range(blocks)))

    r1 = moved(own, routes.rounds[0])
    own_far = Slab([sibling(piece) for piece in split], own.ids, 1)
    mate = swapped(own)

    labels = jnp.arange(occ_energy.shape[0], dtype=jnp.int32)
    picked = orbital_map[:, None] == labels[None, :]
    energy = jnp.sum(jnp.where(picked, occ_energy[None, :], 0.0), axis=1)

    def table_of(ids):
        ids = np.array(ids, np.int32).T
        places = np.arange(blocks)[:, None]
        back, forth = (places - ids) % blocks, (ids - places) % blocks
        behind = back <= ROUNDS
        known = np.stack([ids, np.where(behind, back, -1), np.where(behind, -1, forth)])
        block, mine, theirs = jnp.asarray(known.astype(np.int32))[:, here]
        places = jnp.arange(blocks, dtype=jnp.int32)[None, :]
        both = jnp.where(places == here, energy[None, :], 0.0)
        both = both + jnp.where(places == block[:, None], energy[None, :], 0.0)
        entries = jnp.arange(ROUNDS + 1, dtype=jnp.int32)[None, :]
        kept = pair_kept[:, 0].astype(jnp.float32)[None, :]
        weight = jnp.sum(jnp.where(entries == mine[:, None], kept, 0.0), axis=1)
        return jnp.stack([jnp.sum(both, axis=1), weight, theirs.astype(jnp.float32)], axis=1)

    vir = jnp.stack(
        [lax.dynamic_slice_in_dim(vir_energy, s * vir_count, vir_count) for s in (side, 1 - side)]
    )
    vir_rows, vir_cols = vir[:, :, None], vir[:, None, :]

    def moved_ids(ids_lead, ids_other, pairs):
        return routes.moved(routes.either(ids_lead, ids_other), pairs)

    def swapped_ids(ids):
        return routes.moved(ids, routes.swap)

    r2_ids = moved_ids(own.ids, r1.ids, routes.rounds[1])
    r3_ids = moved_ids(r2_ids, own.ids, routes.rounds[2])
    r4_ids = routes.moved(r3_ids, routes.rounds[3])
    r5_ids = routes.moved(own.ids, routes.rounds[4])
    all_ids = [own.ids, mate.ids]
    for ids in (r1.ids, r2_ids, r3_ids, r4_ids, r5_ids):
        all_ids += [ids, swapped_ids(ids)]
    table = table_of(all_ids)
    near, far = 0, 1
    rows_near = [own.array[:aux].T]
    stacks = {}

    def amps(jobs, turned, *earlier):
        lines = {slab: all_ids.index(slab.ids) for slab, _ in jobs}
        stack = amplitude_call(jobs, table, lines, turned, vir_rows, vir_cols, earlier)
        for place, job in enumerate(jobs):
            stacks[job] = (stack, place)
        return stack

    def density(slabs, block, parts, dtype, *earlier, rows=None, copied=None, cuts=()):
        terms = [(slab, *stacks[slab, block]) for slab in slabs]
        out, *copy = density_call(terms, parts, dtype, aux, earlier, rows, copied, cuts)
        return (out, *copy) if copy else out

    f32, bf16 = jnp.float32, jnp.bfloat16
    done = amps([(own, near), (mate, near)], [rows_near])

    parts = own_far.pieces
    sent, kept = choice_call(1 - flag, r1.array, own.array, [parts[0], done], keep=True)
    r1 = Slab(kept, r1.ids)
    sent2 = Slab(sent, routes.either(own.ids, r1.ids))
    r2 = moved(sent2, routes.rounds[1])
    s1 = swapped(r1)
    done = amps([(r1, near), (s1, near)], [rows_near], sent2.array)
    part = density([own, mate, r1, s1], near, [], f32, done)
    cut = parts[0].shape[0]
    rows_far = [turn_call(parts[0], cut, [part])]

    sent, kept = choice_call(flag, r2.array, own.array, [parts[1], *rows_far], keep=True)
    r2 = Slab(kept, r2.ids)
    sent3 = Slab(sent, routes.either(r2.ids, own.ids))
    r3 = moved(sent3, routes.rounds[2])
    s2 = swapped(r2)
    mate_far = swapped(own_far)
    rows_far.append(turn_call(parts[1], aux - cut, [sent3.array]))
    jobs = [(r2, near), (r2, far), (s2, far), (s2, near), (r1, far), (s1, far)]
    done = amps(jobs, [rows_near, rows_far])
    part = density([r2, s2], near, [[part]], f32, done)

    r3 = Slab(copied(r3.array, part), r3.ids)
    r4 = moved(r3, routes.rounds[3])
    s3 = swapped(r3)
    out_part, again = density([r1, s1, r2, s2], far, [], f32, r3.array, copied=own.pieces)
    r5 = moved(Slab(again, own.ids), routes.rounds[4])
    jobs = [(own_far, near), (mate_far, near), (r3, near), (r3, far), (s3, far), (s3, near)]
    done = amps(jobs, [rows_near, rows_far], out_part)

    done = amps([(r4, far)], [rows_near, rows_far], done)
    half = aux // 2
    slabs = [r3, s3, r4]
    sent0, again = density(
        slabs, far, [[out_part]], bf16, done, rows=(0, half), copied=own_far.pieces
    )
    r6 = moved(Slab(again, own.ids, 1), routes.rounds[4])
    sent1 = density(slabs, far, [[out_part]], bf16, sent0, rows=(half, half))
    incoming = [sibling(sent0), sibling(sent1)]
    done = amps([(r4, near)], [rows_near], sent1)
    part = density([own_far, mate_far, r3, s3, r4], near, [[part]], f32, done)

    thirds = [aux // 3, aux // 3 * 2]
    r5 = Slab(copied(r5.array, part, cuts=thirds), r5.ids)
    s5 = swapped(r5)
    done = amps([(r5, near)], [rows_near], *r5.pieces)
    done = join_call([incoming[0], done])
    done = amps([(s5, near)], [rows_near], done)
    part = density([r5, s5], near, [[part]], f32, done)
    r6 = Slab(copied(r6.array, part, cuts=thirds), r6.ids, 1)
    s6 = swapped(r6)
    done = amps([(r6, near)], [rows_near], *r6.pieces)
    done = amps([(s6, near)], [rows_near], done)
    return density([r6, s6], near, [[part], incoming], f32, done)[None]


def solution(mesh):
    wide, narrow = mesh.shape["wide"], mesh.shape["narrow"]
    paired = narrow == 2 and wide % 4 == 0 and wide > 2 * ROUNDS + 1 and ROUNDS == 5

    def per_device(three_index, *rest):
        if paired and three_index.shape[0] == 1:
            return paired_plan(three_index, *rest)
        return ring_plan(three_index, *rest)

    placed = (P("wide", None, "narrow"), P(), P(), P(), P(None, "wide"))
    return jax.shard_map(
        per_device, mesh=mesh, in_specs=placed, out_specs=P("wide", None, "narrow"), check_vma=False
    )
```

```python
import jax
import jax.numpy as jnp
import numpy as np
from jax import lax
from jax.experimental import pallas as pl
from jax.experimental.pallas import tpu as pltpu
from jax.sharding import PartitionSpec as P

ROUNDS = 5
TAIL = 16
CHUNK = 512
VMEM = 48 * 1024 * 1024


def passed_along(array, axis, by):
    length = lax.axis_size(axis)
    return lax.ppermute(array, axis, [(i, (i + by) % length) for i in range(length)])


def block_energy(orbital_map, occ_energy, block_id, occ_count):
    orbits = lax.dynamic_slice_in_dim(orbital_map, block_id * occ_count, occ_count)
    labels = jnp.arange(occ_energy.shape[0], dtype=jnp.int32)
    chosen = orbits[:, None] == labels[None, :]
    return jnp.sum(jnp.where(chosen, occ_energy[None, :], 0.0), axis=1)


def amplitudes(gathered, visiting, left_energy, right_energy, vir_all, vir_local, weight):
    coulomb = jnp.einsum("ipa,jpb->ijab", gathered, visiting, preferred_element_type=jnp.float32)
    denominator = (vir_all[:, None] + vir_local[None, :])[None, None] - (
        left_energy[:, None] + right_energy[None, :]
    )[:, :, None, None]
    return (weight * coulomb / denominator).astype(jnp.bfloat16)


def ring_plan(three_index, orbital_map, occ_energy, vir_energy, pair_kept):
    occ_count = three_index.shape[0]
    vir_count = three_index.shape[2]
    blocks = lax.axis_size("wide")
    own_block = lax.axis_index("wide")
    vir_local = lax.dynamic_slice_in_dim(
        vir_energy, lax.axis_index("narrow") * vir_count, vir_count
    )
    own_energy = block_energy(orbital_map, occ_energy, own_block, occ_count)
    weights = pair_kept.astype(jnp.float32)
    gathered = lax.all_gather(three_index, "narrow", axis=2, tiled=True)
    amplitude = amplitudes(
        gathered, three_index, own_energy, own_energy, vir_energy, vir_local, weights[0, 0]
    )
    forward = jnp.einsum(
        "ijab,jpb->ipa", amplitude, three_index, preferred_element_type=jnp.float32
    )
    visiting = three_index
    stored_amps = []
    for round_index in range(1, ROUNDS + 1):
        visiting = passed_along(visiting, "wide", 1)
        partner = (own_block - round_index) % blocks
        partner_energy = block_energy(orbital_map, occ_energy, partner, occ_count)
        amplitude = amplitudes(
            gathered,
            visiting,
            own_energy,
            partner_energy,
            vir_energy,
            vir_local,
            weights[round_index, 0],
        )
        forward = forward + jnp.einsum(
            "ijab,jpb->ipa", amplitude, visiting, preferred_element_type=jnp.float32
        )
        stored_amps.append(amplitude)
    carried = None
    for round_index in range(1, ROUNDS + 1):
        backward = jnp.einsum(
            "ijab,ipa->jpb",
            stored_amps[round_index - 1],
            gathered,
            preferred_element_type=jnp.float32,
        )
        if round_index > 1:
            carried = passed_along(carried, "wide", 1) + backward
        else:
            carried = backward
    returned = passed_along(carried, "wide", -ROUNDS)
    scattered = lax.psum_scatter(forward, "narrow", scatter_dimension=2, tiled=True)
    return scattered + returned


class Routes:
    def __init__(self, blocks):
        self.blocks = blocks
        everyone = range(blocks)
        self.lead = [self.place(w)[1] == self.place(w)[2] for w in everyone]
        self.swap = [(w, w ^ 1) for w in everyone]
        onward = [(w, self.along_z(w, 1)) for w in everyone]
        backward = [(w, self.along_z(w, -1)) for w in everyone]
        across = [(w, self.across_x(w)) for w in everyone]
        self.rounds = [
            self.either(across, onward),
            self.either(onward, across),
            self.either(across, backward),
            self.either(backward, across),
            self.either(backward, across),
        ]

    def place(self, w):
        return w // 4, (w // 2) % 2, w % 2

    def along_z(self, w, step):
        z, x, core = self.place(w)
        z = (z + (step if x == 1 else -step)) % (self.blocks // 4)
        return (z * 2 + x) * 2 + core

    def across_x(self, w):
        z, x, core = self.place(w)
        return (z * 2 + 1 - x) * 2 + 1 - core

    def either(self, of_lead, of_other):
        return [a if lead else b for lead, a, b in zip(self.lead, of_lead, of_other)]

    def moved(self, ids, pairs):
        out = [0] * self.blocks
        for source, target in pairs:
            out[target] = ids[source]
        return out


class Slab:
    def __init__(self, array, ids, far=0):
        self.pieces = list(array) if isinstance(array, (list, tuple)) else [array]
        self.array = self.pieces[0]
        self.ids = ids
        self.far = far


def pick(step, values):
    out = values[0]
    for index, value in enumerate(values):
        if index and value != values[0]:
            out = jnp.where(step == index, value, out)
    return out


def amplitude_call(jobs, table, lines, turned, vir_rows, vir_cols, earlier):
    slabs = []
    for slab, _ in jobs:
        if slab not in slabs:
            slabs.append(slab)
    count, blocks = len(slabs), len(turned)
    cols, aux = turned[0][0].shape[0], sum(piece.shape[1] for piece in turned[0])
    held_rows = aux + TAIL
    pieces = [len(slab.pieces) for slab in slabs]
    begins = [sum(pieces[:s]) for s in range(count)]
    of_job = [slabs.index(slab) for slab, _ in jobs]
    block_of = [block for _, block in jobs]
    far_of = [slab.far for slab, _ in jobs]
    line_of = [lines[slab] for slab, _ in jobs]
    row_pieces = [len(block) for block in turned]
    chunks = aux // CHUNK
    opens = [t for t in range(len(jobs)) if t == 0 or of_job[t] != of_job[t - 1]]
    half = cols // 2

    def kernel(scalars, *refs):
        sources, refs = refs[: sum(pieces)], refs[sum(pieces) :]
        row_sources, refs = refs[: sum(row_pieces)], refs[sum(row_pieces) + len(earlier) :]
        vir_row, vir_col, out, held, rows, held_sems, row_sems = refs
        step = pl.program_id(0)

        def slab_copies(s):
            row = 0
            for index in range(pieces[s]):
                source = sources[begins[s] + index]
                for begin, size in chunks_of(source.shape[0]):
                    target = held.at[s % 2, pl.ds(row, size), :]
                    yield pltpu.make_async_copy(
                        source.at[pl.ds(begin, size)], target, held_sems.at[s % 2, row // CHUNK]
                    )
                    row += size

        def row_copies(block):
            column = 0
            for source in row_sources[sum(row_pieces[:block]) : sum(row_pieces[: block + 1])]:
                for begin, size in chunks_of(source.shape[1]):
                    target = rows.at[block, :, pl.ds(column, size)]
                    yield pltpu.make_async_copy(
                        source.at[:, pl.ds(begin, size)], target, row_sems.at[block, column // CHUNK]
                    )
                    column += size

        @pl.when(step == 0)
        def _():
            for pair in zip(slab_copies(0), row_copies(block_of[0])):
                for copy in pair:
                    copy.start()
            for copy in list(slab_copies(0))[chunks:]:
                copy.start()
            for block in list(dict.fromkeys(block_of))[1:]:
                for copy in row_copies(block):
                    copy.start()

        for s, t in enumerate(opens):

            @pl.when(step == t)
            def _(s=s):
                if s:
                    for copy in slab_copies(s):
                        copy.wait()
                if s + 1 < count:
                    for copy in slab_copies(s + 1):
                        copy.start()

        for block in list(dict.fromkeys(block_of))[1:]:

            @pl.when(step == block_of.index(block))
            def _(block=block):
                for copy in row_copies(block):
                    copy.wait()

        slot = pick(step, [s % 2 for s in of_job])
        block = pick(step, block_of)
        line = pick(step, line_of)
        @pl.when(step == 0)
        def _():
            for copy in list(slab_copies(0))[chunks:]:
                copy.wait()

        plan = held[slot, aux:, :128].astype(jnp.float32)
        lane = lax.broadcasted_iota(jnp.int32, plan.shape, 1).astype(jnp.float32)
        row = lax.broadcasted_iota(jnp.int32, plan.shape, 0)
        told = jnp.where(jnp.logical_and(row == 0, lane == scalars[line, 2]), plan, 0.0)
        weight = scalars[line, 1] + jnp.sum(told, keepdims=True)

        def finish(part, coulomb):
            denominator = (vir_row[0] + vir_col[0, :, part]) - scalars[line, 0]
            out[0, :, part] = (weight * coulomb / denominator).astype(out.dtype)

        @pl.when(step == 0)
        def _():
            coulomb = None
            for index, pair in enumerate(zip(row_copies(block_of[0]), slab_copies(0))):
                for copy in pair:
                    copy.wait()
                chunk = pl.ds(index * CHUNK, CHUNK)
                term = jnp.dot(
                    rows[block_of[0], :, chunk], held[0, chunk, :], preferred_element_type=jnp.float32
                )
                coulomb = term if coulomb is None else coulomb + term
            finish(pl.ds(0, cols), coulomb)

        @pl.when(step > 0)
        def _():
            for begin in range(0, cols, half):
                part = pl.ds(begin, half)
                finish(part, jnp.dot(rows[block], held[slot, :aux, part], preferred_element_type=jnp.float32))

    return pl.pallas_call(
        kernel,
        grid=(len(jobs),),
        in_specs=[pl.BlockSpec(memory_space=pltpu.SMEM)]
        + [pl.BlockSpec(memory_space=pl.ANY)] * (sum(pieces) + sum(row_pieces) + len(earlier))
        + [
            pl.BlockSpec((1, cols, 1), lambda t: (pick(t, block_of), 0, 0)),
            pl.BlockSpec((1, 1, cols), lambda t: (pick(t, far_of), 0, 0)),
        ],
        out_specs=pl.BlockSpec((1, cols, cols), lambda t: (t, 0, 0)),
        out_shape=jax.ShapeDtypeStruct((len(jobs), cols, cols), jnp.bfloat16),
        scratch_shapes=[
            pltpu.VMEM((2, held_rows, cols), jnp.bfloat16),
            pltpu.VMEM((blocks, cols, aux), jnp.bfloat16),
            pltpu.SemaphoreType.DMA((2, chunks + 1)),
            pltpu.SemaphoreType.DMA((blocks, chunks)),
        ],
        compiler_params=pltpu.CompilerParams(vmem_limit_bytes=VMEM),
        cost_estimate=pl.CostEstimate(
            flops=2 * len(jobs) * cols * aux * cols,
            bytes_accessed=2 * cols * (blocks * aux + count * aux + len(jobs) * cols),
            transcendentals=0,
        ),
    )(table, *[p for s in slabs for p in s.pieces], *[p for b in turned for p in b], *earlier, vir_rows, vir_cols)


def chunks_of(rows):
    return [(begin, min(CHUNK, rows - begin)) for begin in range(0, rows, CHUNK)]


def copies_in(sources, held, sems):
    row, index = 0, 0
    for source in sources:
        for begin, size in chunks_of(source.shape[0]):
            yield pltpu.make_async_copy(
                source.at[pl.ds(begin, size)], held.at[pl.ds(row + begin, size)], sems.at[index]
            )
            index += 1
        row += source.shape[0]


def copies_out(held, targets, sems):
    row, index = 0, 0
    for target in targets:
        for begin, size in chunks_of(target.shape[0]):
            yield pltpu.make_async_copy(
                held.at[pl.ds(row + begin, size)], target.at[pl.ds(begin, size)], sems.at[index]
            )
            index += 1
        row += target.shape[0]


def copy_scratch(rows, cols):
    count = len(chunks_of(rows)) + 1
    return [
        pltpu.VMEM((rows, cols), jnp.bfloat16),
        pltpu.SemaphoreType.DMA((count,)),
        pltpu.SemaphoreType.DMA((count,)),
    ]


def copy_through(sources, targets, held, in_sems, out_sems):
    if [x.shape[0] for x in sources] != [x.shape[0] for x in targets]:
        loads, stores = [list(copies_in(sources, held, in_sems))], [list(copies_out(held, targets, out_sems))]
    else:
        loads = [[copy] for copy in copies_in(sources, held, in_sems)]
        stores = [[copy] for copy in copies_out(held, targets, out_sems)]
    for copies in loads:
        for copy in copies:
            copy.start()
    for before, behind in zip(loads, stores):
        for copy in before:
            copy.wait()
        for copy in behind:
            copy.start()
    for copies in stores:
        for copy in copies:
            copy.wait()


def append_call(array, tail, cuts):
    rows, cols = array.shape[0] + tail.shape[0], array.shape[1]
    begins = [0, *cuts, rows]
    sizes = [end - begin for begin, end in zip(begins, begins[1:])]

    def kernel(array_ref, tail_ref, out, *refs):
        pieces, (held, in_sems, out_sems, piece_sems) = refs[: len(sizes)], refs[len(sizes) :]
        loads = list(copies_in([array_ref, tail_ref], held, in_sems))
        stores = list(copies_out(held, [out], out_sems))
        piece_stores = list(copies_out(held, pieces, piece_sems))
        for copy in loads:
            copy.start()
        for load, *behind in zip(loads, stores, piece_stores):
            load.wait()
            for copy in behind:
                copy.start()
        for copy in stores + piece_stores:
            copy.wait()

    scratch = copy_scratch(rows, cols)
    return pl.pallas_call(
        kernel,
        in_specs=[pl.BlockSpec(memory_space=pl.ANY)] * 2,
        out_specs=[pl.BlockSpec(memory_space=pl.ANY)] * (1 + len(sizes)),
        out_shape=[jax.ShapeDtypeStruct((size, cols), array.dtype) for size in (rows, *sizes)],
        scratch_shapes=scratch + scratch[-1:],
        compiler_params=pltpu.CompilerParams(vmem_limit_bytes=VMEM),
    )(array, tail)


def choice_call(flag, a, b, earlier, cuts=(), keep=False):
    rows, cols = a.shape
    begins = [0, *cuts, rows]
    pieces = len(cuts) + 1
    shapes = [(end - begin, cols) for begin, end in zip(begins, begins[1:])]
    kept = [(rows, cols)] if keep else []

    def kernel(flag_ref, a_ref, b_ref, *refs):
        refs = refs[len(earlier) :]
        outs, kept_outs, scratch = refs[:pieces], refs[pieces : pieces + len(kept)], refs[pieces + len(kept) :]
        if keep:
            held, loads, stores, other_held, other_loads, other_stores = scratch
            leads = flag_ref[0] == 1
            ours = list(copies_in([a_ref], held, loads))
            theirs = list(copies_in([b_ref], other_held, other_loads))
            kept_copies = list(copies_out(held, kept_outs, stores))
            ours_out = list(copies_out(held, outs, other_stores))
            theirs_out = list(copies_out(other_held, outs, other_stores))
            for copy in ours:
                copy.start()

            @pl.when(jnp.logical_not(leads))
            def _():
                for copy in theirs:
                    copy.start()

            for load, store, also in zip(ours, kept_copies, ours_out):
                load.wait()
                store.start()
                pl.when(leads)(also.start)

            @pl.when(jnp.logical_not(leads))
            def _():
                for load, store in zip(theirs, theirs_out):
                    load.wait()
                    store.start()

            for store, also in zip(kept_copies, ours_out):
                store.wait()
                also.wait()
        else:
            for value, source in ((1, a_ref), (0, b_ref)):

                @pl.when(flag_ref[0] == value)
                def _(source=source):
                    parts = [source.at[pl.ds(at, out.shape[0])] for at, out in zip(begins, outs)]
                    copy_through(parts, outs, *scratch)

    return pl.pallas_call(
        kernel,
        in_specs=[pl.BlockSpec(memory_space=pltpu.SMEM)]
        + [pl.BlockSpec(memory_space=pl.ANY)] * (2 + len(earlier)),
        out_specs=[pl.BlockSpec(memory_space=pl.ANY)] * (pieces + len(kept)),
        out_shape=[jax.ShapeDtypeStruct(shape, a.dtype) for shape in shapes + kept],
        scratch_shapes=copy_scratch(rows, cols) * (1 + len(kept)),
        compiler_params=pltpu.CompilerParams(vmem_limit_bytes=VMEM),
        cost_estimate=pl.CostEstimate(flops=0, bytes_accessed=2 * a.size * a.dtype.itemsize, transcendentals=0),
    )(flag, a, b, *earlier)


def turn_call(array, rows, earlier):
    cols = array.shape[1]

    def kernel(array_ref, *refs):
        refs[-1][...] = array_ref[...].T

    return pl.pallas_call(
        kernel,
        grid=(rows // CHUNK,),
        in_specs=[pl.BlockSpec((CHUNK, cols), lambda i: (i, 0))]
        + [pl.BlockSpec(memory_space=pl.ANY)] * len(earlier),
        out_specs=pl.BlockSpec((cols, CHUNK), lambda i: (0, i)),
        out_shape=jax.ShapeDtypeStruct((cols, rows), array.dtype),
        compiler_params=pltpu.CompilerParams(vmem_limit_bytes=VMEM),
    )(array, *earlier)


def join_call(earlier):
    def kernel(*refs):
        refs[-1][...] = jnp.zeros_like(refs[-1])

    return pl.pallas_call(
        kernel,
        in_specs=[pl.BlockSpec(memory_space=pl.ANY)] * len(earlier),
        out_specs=pl.BlockSpec(memory_space=pltpu.VMEM),
        out_shape=jax.ShapeDtypeStruct((8, 128), jnp.float32),
    )(*earlier)


def density_call(terms, parts, out_dtype, aux, earlier, rows=None, copied=None, cuts=(), within=None):
    count = len(terms)
    depth = terms[0][0].array.shape[1]
    extra = list(copied or [])
    base = list(within or [])
    total_rows = sum(x.shape[0] for x in extra)
    ends = [0, *cuts, total_rows]
    whole = [jax.ShapeDtypeStruct((b - a, depth), jnp.bfloat16) for a, b in zip(ends, ends[1:]) if extra]
    pieces = [len(t[0].pieces) for t in terms]
    begins = [sum(pieces[:s]) for s in range(count)]
    cols = depth
    begin, length = rows or (0, aux)
    tile = 512
    while length % tile or begin % tile:
        tile //= 2
    steps = length // tile
    moved_by = 0 if within is None else begin // tile
    spans = []
    for part in parts:
        ends = np.cumsum([piece.shape[0] // tile for piece in part])
        shift = begin // tile if ends[-1] == aux // tile else 0
        spans.append([(int(end) - piece.shape[0] // tile - shift, int(end) - shift) for end, piece in zip(ends, part)])
    parts = [p for part in parts for p in part]

    def kernel(*refs):
        sources, refs = refs[: sum(pieces)], refs[sum(pieces) :]
        amps, refs = refs[:count], refs[count + len(earlier) :]
        source, refs = refs[: len(extra)], refs[len(extra) + len(base) :]
        part_refs, out, refs = refs[: len(parts)], refs[len(parts)], refs[len(parts) + 1 :]
        target, refs = refs[: len(whole)], refs[len(whole) :]
        (left, right, left_sems, right_sems), scratch = refs[:4], refs[4:]
        step = pl.program_id(0)
        slot = step % 2

        def amp_copies():
            for s, (_, _, place) in enumerate(terms):
                yield pltpu.make_async_copy(
                    amps[s].at[place], right.at[:, pl.ds(s * depth, depth)], right_sems.at[s]
                )

        def slab_copies(which, start, of=range(count)):
            for s in of:
                end = 0
                for index in range(pieces[s]):
                    source = sources[begins[s] + index]
                    first = end
                    end += source.shape[0] // tile

                    def act(source=source, first=first, s=s):
                        row = pl.multiple_of((begin // tile + which - first) * tile, tile)
                        copy = pltpu.make_async_copy(
                            source.at[pl.ds(row, tile), :],
                            left.at[which % 2, :, pl.ds(s * depth, depth)],
                            left_sems.at[which % 2, s],
                        )
                        copy.start() if start else copy.wait()

                    at = begin // tile + which
                    if pieces[s] == 1:
                        act()
                    else:
                        pl.when(jnp.logical_and(at >= first, at < end))(act)

        @pl.when(step == 0)
        def _():
            for s, copy in enumerate(amp_copies()):
                copy.start()
                slab_copies(step, True, [s])
            if extra:
                for copy in copies_in(source, scratch[0], scratch[1]):
                    copy.start()

        @pl.when(step + 1 < steps)
        def _():
            slab_copies(step + 1, True)

        def finish(total):
            at = 0
            for span in spans:
                part = part_refs[at][...]
                for index in range(1, len(span)):
                    part = jnp.where(step >= span[index][0], part_refs[at + index][...], part)
                total = total + part.astype(jnp.float32)
                at += len(span)
            out[...] = total.astype(out.dtype)

        def product(a, b):
            return lax.dot_general(a, b, (((1,), (1,)), ((), ())), preferred_element_type=jnp.float32)

        @pl.when(step == 0)
        def _():
            total = None
            for s, copy in enumerate(amp_copies()):
                copy.wait()
                slab_copies(step, False, [s])
                at = pl.ds(s * depth, depth)
                term = product(left[0, :, at], right[:, at])
                total = term if total is None else total + term
            finish(total)

        @pl.when(step > 0)
        def _():
            slab_copies(step, False)
            finish(product(left[slot], right[...]))

        if extra:

            @pl.when(step == 1)
            def _():
                for copy in copies_in(source, scratch[0], scratch[1]):
                    copy.wait()
                for copy in copies_out(scratch[0], target, scratch[2]):
                    copy.start()

            @pl.when(step == steps - 1)
            def _():
                for copy in copies_out(scratch[0], target, scratch[2]):
                    copy.wait()

    def rows_of(start, end):
        return pl.BlockSpec((tile, cols), lambda i: (jnp.clip(i - start, 0, end - start - 1), 0))

    bytes_moved = 2 * count * (length * depth + cols * depth)
    bytes_moved += sum(length * cols * p.dtype.itemsize for p in parts)
    return pl.pallas_call(
        kernel,
        grid=(steps,),
        in_specs=[pl.BlockSpec(memory_space=pl.ANY)] * (sum(pieces) + count + len(earlier) + len(extra) + len(base))
        + [rows_of(*ends) for span in spans for ends in span],
        out_specs=[pl.BlockSpec((tile, cols), lambda i: (i + moved_by, 0))]
        + [pl.BlockSpec(memory_space=pl.ANY)] * len(whole),
        out_shape=[jax.ShapeDtypeStruct((length if within is None else aux, cols), out_dtype)]
        + whole,
        input_output_aliases={sum(pieces) + count + len(earlier) + len(extra): 0} if base else {},
        scratch_shapes=[
            pltpu.VMEM((2, tile, count * depth), jnp.bfloat16),
            pltpu.VMEM((cols, count * depth), jnp.bfloat16),
            pltpu.SemaphoreType.DMA((2, count)),
            pltpu.SemaphoreType.DMA((count,)),
            *(copy_scratch(total_rows, depth) if extra else []),
        ],
        compiler_params=pltpu.CompilerParams(vmem_limit_bytes=VMEM),
        cost_estimate=pl.CostEstimate(
            flops=2 * length * depth * cols * count,
            bytes_accessed=(bytes_moved + length * cols * jnp.dtype(out_dtype).itemsize),
            transcendentals=0,
        ),
    )(*[p for t in terms for p in t[0].pieces], *[t[1] for t in terms], *earlier, *extra, *base, *parts)


def paired_plan(three_index, orbital_map, occ_energy, vir_energy, pair_kept):
    blocks = lax.axis_size("wide")
    routes = Routes(blocks)
    here = lax.axis_index("wide")
    side = lax.axis_index("narrow")
    aux, vir_count = three_index.shape[1:]

    def moved(slab, pairs):
        sent = [lax.ppermute(piece, "wide", pairs) for piece in slab.pieces]
        return Slab(sent, routes.moved(slab.ids, pairs), slab.far)

    def swapped(slab):
        return moved(slab, routes.swap)

    flag = jnp.asarray(np.array(routes.lead, np.int32))[here].reshape(1)

    def copied(array, *earlier, cuts=()):
        return choice_call(flag, array, array, earlier, cuts)

    def sibling(array):
        return lax.ppermute(array, "narrow", [(0, 1), (1, 0)])

    plan = jnp.zeros((TAIL, vir_count), jnp.bfloat16)
    plan = plan.at[0, : ROUNDS + 1].set(pair_kept[:, 0].astype(jnp.bfloat16))
    whole, *split = append_call(three_index[0], plan, [aux // 2])
    own = Slab(whole, list(range(blocks)))

    r1 = moved(own, routes.rounds[0])
    own_far = Slab([sibling(piece) for piece in split], own.ids, 1)
    mate = swapped(own)

    labels = jnp.arange(occ_energy.shape[0], dtype=jnp.int32)
    picked = orbital_map[:, None] == labels[None, :]
    energy = jnp.sum(jnp.where(picked, occ_energy[None, :], 0.0), axis=1)

    def table_of(ids):
        ids = np.array(ids, np.int32).T
        places = np.arange(blocks)[:, None]
        back, forth = (places - ids) % blocks, (ids - places) % blocks
        behind = back <= ROUNDS
        known = np.stack([ids, np.where(behind, back, -1), np.where(behind, -1, forth)])
        block, mine, theirs = jnp.asarray(known.astype(np.int32))[:, here]
        places = jnp.arange(blocks, dtype=jnp.int32)[None, :]
        both = jnp.where(places == here, energy[None, :], 0.0)
        both = both + jnp.where(places == block[:, None], energy[None, :], 0.0)
        entries = jnp.arange(ROUNDS + 1, dtype=jnp.int32)[None, :]
        kept = pair_kept[:, 0].astype(jnp.float32)[None, :]
        weight = jnp.sum(jnp.where(entries == mine[:, None], kept, 0.0), axis=1)
        return jnp.stack([jnp.sum(both, axis=1), weight, theirs.astype(jnp.float32)], axis=1)

    vir = jnp.stack(
        [lax.dynamic_slice_in_dim(vir_energy, s * vir_count, vir_count) for s in (side, 1 - side)]
    )
    vir_rows, vir_cols = vir[:, :, None], vir[:, None, :]

    def moved_ids(ids_lead, ids_other, pairs):
        return routes.moved(routes.either(ids_lead, ids_other), pairs)

    def swapped_ids(ids):
        return routes.moved(ids, routes.swap)

    r2_ids = moved_ids(own.ids, r1.ids, routes.rounds[1])
    r3_ids = moved_ids(r2_ids, own.ids, routes.rounds[2])
    r4_ids = routes.moved(r3_ids, routes.rounds[3])
    r5_ids = routes.moved(own.ids, routes.rounds[4])
    all_ids = [own.ids, mate.ids]
    for ids in (r1.ids, r2_ids, r3_ids, r4_ids, r5_ids):
        all_ids += [ids, swapped_ids(ids)]
    table = table_of(all_ids)
    near, far = 0, 1
    rows_near = [own.array[:aux].T]
    stacks = {}

    def amps(jobs, turned, *earlier):
        lines = {slab: all_ids.index(slab.ids) for slab, _ in jobs}
        stack = amplitude_call(jobs, table, lines, turned, vir_rows, vir_cols, earlier)
        for place, job in enumerate(jobs):
            stacks[job] = (stack, place)
        return stack

    def density(slabs, block, parts, dtype, *earlier, rows=None, copied=None, within=None):
        terms = [(slab, *stacks[slab, block]) for slab in slabs]
        out, *copy = density_call(terms, parts, dtype, aux, earlier, rows, copied, (), within)
        return (out, *copy) if copy else out

    f32, bf16 = jnp.float32, jnp.bfloat16
    done = amps([(own, near), (mate, near)], [rows_near])

    parts = own_far.pieces
    sent, kept = choice_call(1 - flag, r1.array, own.array, [parts[0], done], keep=True)
    r1 = Slab(kept, r1.ids)
    sent2 = Slab(sent, routes.either(own.ids, r1.ids))
    r2 = moved(sent2, routes.rounds[1])
    s1 = swapped(r1)
    done = amps([(r1, near), (s1, near)], [rows_near], sent2.array)
    part = density([own, mate, r1, s1], near, [], f32, done)
    cut = parts[0].shape[0]
    rows_far = [turn_call(parts[0], cut, [part])]

    sent, kept = choice_call(flag, r2.array, own.array, [parts[1], *rows_far], keep=True)
    r2 = Slab(kept, r2.ids)
    sent3 = Slab(sent, routes.either(r2.ids, own.ids))
    r3 = moved(sent3, routes.rounds[2])
    s2 = swapped(r2)
    mate_far = swapped(own_far)
    rows_far.append(turn_call(parts[1], aux - cut, [sent3.array]))
    jobs = [(r2, near), (r2, far), (s2, far), (s2, near), (r1, far), (s1, far)]
    done = amps(jobs, [rows_near, rows_far])
    part = density([r2, s2], near, [[part]], f32, done)

    r3 = Slab(copied(r3.array, part), r3.ids)
    r4 = moved(r3, routes.rounds[3])
    s3 = swapped(r3)
    out_part, again = density([r1, s1, r2, s2], far, [], f32, r3.array, copied=own.pieces)
    r5 = moved(Slab(again, own.ids), routes.rounds[4])
    jobs = [(own_far, near), (mate_far, near), (r3, near), (r3, far), (s3, far), (s3, near)]
    done = amps(jobs, [rows_near, rows_far], out_part)

    done = amps([(r4, far)], [rows_near, rows_far], done)
    half = aux // 2
    slabs = [r3, s3, r4]
    sent0, again = density(
        slabs, far, [[out_part]], bf16, done, rows=(0, half), copied=own_far.pieces
    )
    r6 = moved(Slab(again, own.ids, 1), routes.rounds[4])
    sent1 = density(slabs, far, [[out_part]], bf16, sent0, rows=(half, half))
    incoming = [sibling(sent0), sibling(sent1)]
    done = amps([(r4, near)], [rows_near], sent1)
    part = density([own_far, mate_far, r3, s3, r4], near, [[part]], f32, done)

    thirds = [aux // 3, aux // 3 * 2]
    r5 = Slab(copied(r5.array, part, cuts=thirds), r5.ids)
    s5 = swapped(r5)
    done = amps([(r5, near)], [rows_near], *r5.pieces)
    done = join_call([incoming[0], done])
    done = amps([(s5, near)], [rows_near], done)
    part = density([r5, s5], near, [[part]], f32, done)
    r6 = Slab(copied(r6.array, part, cuts=thirds), r6.ids, 1)
    s6 = swapped(r6)
    done = amps([(r6, near)], [rows_near], *r6.pieces)
    done = amps([(s6, near)], [rows_near], done)
    out = []
    for index, piece in enumerate(incoming):
        rows = (index * half, half)
        out = [density([r6, s6], near, [[part], [piece]], f32, done, rows=rows, within=out)]
    return out[0][None]


def solution(mesh):
    wide, narrow = mesh.shape["wide"], mesh.shape["narrow"]
    paired = narrow == 2 and wide % 4 == 0 and wide > 2 * ROUNDS + 1 and ROUNDS == 5

    def per_device(three_index, *rest):
        if paired and three_index.shape[0] == 1:
            return paired_plan(three_index, *rest)
        return ring_plan(three_index, *rest)

    placed = (P("wide", None, "narrow"), P(), P(), P(), P(None, "wide"))
    return jax.shard_map(
        per_device, mesh=mesh, in_specs=placed, out_specs=P("wide", None, "narrow"), check_vma=False
    )
```

```python
import jax
import jax.numpy as jnp
import numpy as np
from jax import lax
from jax.experimental import pallas as pl
from jax.experimental.pallas import tpu as pltpu
from jax.sharding import PartitionSpec as P

ROUNDS = 5
TAIL = 16
CHUNK = 512
VMEM = 52 * 1024 * 1024


def passed_along(array, axis, by):
    length = lax.axis_size(axis)
    return lax.ppermute(array, axis, [(i, (i + by) % length) for i in range(length)])


def block_energy(orbital_map, occ_energy, block_id, occ_count):
    orbits = lax.dynamic_slice_in_dim(orbital_map, block_id * occ_count, occ_count)
    labels = jnp.arange(occ_energy.shape[0], dtype=jnp.int32)
    chosen = orbits[:, None] == labels[None, :]
    return jnp.sum(jnp.where(chosen, occ_energy[None, :], 0.0), axis=1)


def amplitudes(gathered, visiting, left_energy, right_energy, vir_all, vir_local, weight):
    coulomb = jnp.einsum("ipa,jpb->ijab", gathered, visiting, preferred_element_type=jnp.float32)
    denominator = (vir_all[:, None] + vir_local[None, :])[None, None] - (
        left_energy[:, None] + right_energy[None, :]
    )[:, :, None, None]
    return (weight * coulomb / denominator).astype(jnp.bfloat16)


def ring_plan(three_index, orbital_map, occ_energy, vir_energy, pair_kept):
    occ_count = three_index.shape[0]
    vir_count = three_index.shape[2]
    blocks = lax.axis_size("wide")
    own_block = lax.axis_index("wide")
    vir_local = lax.dynamic_slice_in_dim(
        vir_energy, lax.axis_index("narrow") * vir_count, vir_count
    )
    own_energy = block_energy(orbital_map, occ_energy, own_block, occ_count)
    weights = pair_kept.astype(jnp.float32)
    gathered = lax.all_gather(three_index, "narrow", axis=2, tiled=True)
    amplitude = amplitudes(
        gathered, three_index, own_energy, own_energy, vir_energy, vir_local, weights[0, 0]
    )
    forward = jnp.einsum(
        "ijab,jpb->ipa", amplitude, three_index, preferred_element_type=jnp.float32
    )
    visiting = three_index
    stored_amps = []
    for round_index in range(1, ROUNDS + 1):
        visiting = passed_along(visiting, "wide", 1)
        partner = (own_block - round_index) % blocks
        partner_energy = block_energy(orbital_map, occ_energy, partner, occ_count)
        amplitude = amplitudes(
            gathered,
            visiting,
            own_energy,
            partner_energy,
            vir_energy,
            vir_local,
            weights[round_index, 0],
        )
        forward = forward + jnp.einsum(
            "ijab,jpb->ipa", amplitude, visiting, preferred_element_type=jnp.float32
        )
        stored_amps.append(amplitude)
    carried = None
    for round_index in range(1, ROUNDS + 1):
        backward = jnp.einsum(
            "ijab,ipa->jpb",
            stored_amps[round_index - 1],
            gathered,
            preferred_element_type=jnp.float32,
        )
        if round_index > 1:
            carried = passed_along(carried, "wide", 1) + backward
        else:
            carried = backward
    returned = passed_along(carried, "wide", -ROUNDS)
    scattered = lax.psum_scatter(forward, "narrow", scatter_dimension=2, tiled=True)
    return scattered + returned


class Routes:
    def __init__(self, blocks):
        self.blocks = blocks
        everyone = range(blocks)
        self.lead = [self.place(w)[1] == self.place(w)[2] for w in everyone]
        self.swap = [(w, w ^ 1) for w in everyone]
        onward = [(w, self.along_z(w, 1)) for w in everyone]
        backward = [(w, self.along_z(w, -1)) for w in everyone]
        across = [(w, self.across_x(w)) for w in everyone]
        self.rounds = [
            self.either(across, onward),
            self.either(onward, across),
            self.either(across, backward),
            self.either(backward, across),
            self.either(backward, across),
        ]

    def place(self, w):
        return w // 4, (w // 2) % 2, w % 2

    def along_z(self, w, step):
        z, x, core = self.place(w)
        z = (z + (step if x == 1 else -step)) % (self.blocks // 4)
        return (z * 2 + x) * 2 + core

    def across_x(self, w):
        z, x, core = self.place(w)
        return (z * 2 + 1 - x) * 2 + 1 - core

    def either(self, of_lead, of_other):
        return [a if lead else b for lead, a, b in zip(self.lead, of_lead, of_other)]

    def moved(self, ids, pairs):
        out = [0] * self.blocks
        for source, target in pairs:
            out[target] = ids[source]
        return out


class Slab:
    def __init__(self, array, ids, far=0):
        self.pieces = list(array) if isinstance(array, (list, tuple)) else [array]
        self.array = self.pieces[0]
        self.ids = ids
        self.far = far


def pick(step, values):
    out = values[0]
    for index, value in enumerate(values):
        if index and value != values[0]:
            out = jnp.where(step == index, value, out)
    return out


def amplitude_call(jobs, table, lines, turned, vir_rows, vir_cols, earlier):
    slabs = []
    for slab, _ in jobs:
        if slab not in slabs:
            slabs.append(slab)
    count, blocks = len(slabs), len(turned)
    cols, aux = turned[0][0].shape[0], sum(piece.shape[1] for piece in turned[0])
    held_rows = aux + TAIL
    pieces = [len(slab.pieces) for slab in slabs]
    begins = [sum(pieces[:s]) for s in range(count)]
    of_job = [slabs.index(slab) for slab, _ in jobs]
    block_of = [block for _, block in jobs]
    far_of = [slab.far for slab, _ in jobs]
    line_of = [lines[slab] for slab, _ in jobs]
    row_pieces = [len(block) for block in turned]
    chunks = aux // CHUNK
    opens = [t for t in range(len(jobs)) if t == 0 or of_job[t] != of_job[t - 1]]
    half = cols // 2

    def kernel(scalars, *refs):
        sources, refs = refs[: sum(pieces)], refs[sum(pieces) :]
        row_sources, refs = refs[: sum(row_pieces)], refs[sum(row_pieces) + len(earlier) :]
        vir_row, vir_col, out, held, rows, held_sems, row_sems = refs
        step = pl.program_id(0)

        def slab_copies(s):
            row = 0
            for index in range(pieces[s]):
                source = sources[begins[s] + index]
                for begin, size in chunks_of(source.shape[0]):
                    target = held.at[s % 2, pl.ds(row, size), :]
                    yield pltpu.make_async_copy(
                        source.at[pl.ds(begin, size)], target, held_sems.at[s % 2, row // CHUNK]
                    )
                    row += size

        def row_copies(block):
            column = 0
            for source in row_sources[sum(row_pieces[:block]) : sum(row_pieces[: block + 1])]:
                for begin, size in chunks_of(source.shape[1]):
                    target = rows.at[block, :, pl.ds(column, size)]
                    yield pltpu.make_async_copy(
                        source.at[:, pl.ds(begin, size)], target, row_sems.at[block, column // CHUNK]
                    )
                    column += size

        @pl.when(step == 0)
        def _():
            for pair in zip(slab_copies(0), row_copies(block_of[0])):
                for copy in pair:
                    copy.start()
            for copy in list(slab_copies(0))[chunks:]:
                copy.start()
            for block in list(dict.fromkeys(block_of))[1:]:
                for copy in row_copies(block):
                    copy.start()

        for s, t in enumerate(opens):

            @pl.when(step == t)
            def _(s=s):
                if s:
                    for copy in slab_copies(s):
                        copy.wait()
                if s + 1 < count:
                    for copy in slab_copies(s + 1):
                        copy.start()

        for block in list(dict.fromkeys(block_of))[1:]:

            @pl.when(step == block_of.index(block))
            def _(block=block):
                for copy in row_copies(block):
                    copy.wait()

        slot = pick(step, [s % 2 for s in of_job])
        block = pick(step, block_of)
        line = pick(step, line_of)
        @pl.when(step == 0)
        def _():
            for copy in list(slab_copies(0))[chunks:]:
                copy.wait()

        plan = held[slot, aux:, :128].astype(jnp.float32)
        lane = lax.broadcasted_iota(jnp.int32, plan.shape, 1).astype(jnp.float32)
        row = lax.broadcasted_iota(jnp.int32, plan.shape, 0)
        told = jnp.where(jnp.logical_and(row == 0, lane == scalars[line, 2]), plan, 0.0)
        weight = scalars[line, 1] + jnp.sum(told, keepdims=True)

        def finish(part, coulomb):
            denominator = (vir_row[0] + vir_col[0, :, part]) - scalars[line, 0]
            out[0, :, part] = (weight * coulomb / denominator).astype(out.dtype)

        @pl.when(step == 0)
        def _():
            coulomb = None
            for index, pair in enumerate(zip(row_copies(block_of[0]), slab_copies(0))):
                for copy in pair:
                    copy.wait()
                chunk = pl.ds(index * CHUNK, CHUNK)
                term = jnp.dot(
                    rows[block_of[0], :, chunk], held[0, chunk, :], preferred_element_type=jnp.float32
                )
                coulomb = term if coulomb is None else coulomb + term
            finish(pl.ds(0, cols), coulomb)

        @pl.when(step > 0)
        def _():
            for begin in range(0, cols, half):
                part = pl.ds(begin, half)
                finish(part, jnp.dot(rows[block], held[slot, :aux, part], preferred_element_type=jnp.float32))

    return pl.pallas_call(
        kernel,
        grid=(len(jobs),),
        in_specs=[pl.BlockSpec(memory_space=pltpu.SMEM)]
        + [pl.BlockSpec(memory_space=pl.ANY)] * (sum(pieces) + sum(row_pieces) + len(earlier))
        + [
            pl.BlockSpec((1, cols, 1), lambda t: (pick(t, block_of), 0, 0)),
            pl.BlockSpec((1, 1, cols), lambda t: (pick(t, far_of), 0, 0)),
        ],
        out_specs=pl.BlockSpec((1, cols, cols), lambda t: (t, 0, 0)),
        out_shape=jax.ShapeDtypeStruct((len(jobs), cols, cols), jnp.bfloat16),
        scratch_shapes=[
            pltpu.VMEM((2, held_rows, cols), jnp.bfloat16),
            pltpu.VMEM((blocks, cols, aux), jnp.bfloat16),
            pltpu.SemaphoreType.DMA((2, chunks + 1)),
            pltpu.SemaphoreType.DMA((blocks, chunks)),
        ],
        compiler_params=pltpu.CompilerParams(vmem_limit_bytes=VMEM),
        cost_estimate=pl.CostEstimate(
            flops=2 * len(jobs) * cols * aux * cols,
            bytes_accessed=2 * cols * (blocks * aux + count * aux + len(jobs) * cols),
            transcendentals=0,
        ),
    )(table, *[p for s in slabs for p in s.pieces], *[p for b in turned for p in b], *earlier, vir_rows, vir_cols)


def chunks_of(rows):
    return [(begin, min(CHUNK, rows - begin)) for begin in range(0, rows, CHUNK)]


def copies_in(sources, held, sems):
    row, index = 0, 0
    for source in sources:
        for begin, size in chunks_of(source.shape[0]):
            yield pltpu.make_async_copy(
                source.at[pl.ds(begin, size)], held.at[pl.ds(row + begin, size)], sems.at[index]
            )
            index += 1
        row += source.shape[0]


def copies_out(held, targets, sems):
    row, index = 0, 0
    for target in targets:
        for begin, size in chunks_of(target.shape[0]):
            yield pltpu.make_async_copy(
                held.at[pl.ds(row + begin, size)], target.at[pl.ds(begin, size)], sems.at[index]
            )
            index += 1
        row += target.shape[0]


def copy_scratch(rows, cols):
    count = len(chunks_of(rows)) + 1
    return [
        pltpu.VMEM((rows, cols), jnp.bfloat16),
        pltpu.SemaphoreType.DMA((count,)),
        pltpu.SemaphoreType.DMA((count,)),
    ]


def copy_through(sources, targets, held, in_sems, out_sems):
    if [x.shape[0] for x in sources] != [x.shape[0] for x in targets]:
        loads, stores = [list(copies_in(sources, held, in_sems))], [list(copies_out(held, targets, out_sems))]
    else:
        loads = [[copy] for copy in copies_in(sources, held, in_sems)]
        stores = [[copy] for copy in copies_out(held, targets, out_sems)]
    for copies in loads:
        for copy in copies:
            copy.start()
    for before, behind in zip(loads, stores):
        for copy in before:
            copy.wait()
        for copy in behind:
            copy.start()
    for copies in stores:
        for copy in copies:
            copy.wait()


def append_call(array, tail, cuts):
    rows, cols = array.shape[0] + tail.shape[0], array.shape[1]
    begins = [0, *cuts, rows]
    sizes = [end - begin for begin, end in zip(begins, begins[1:])]

    def kernel(array_ref, tail_ref, out, *refs):
        pieces, (held, in_sems, out_sems, piece_sems) = refs[: len(sizes)], refs[len(sizes) :]
        loads = list(copies_in([array_ref, tail_ref], held, in_sems))
        stores = list(copies_out(held, [out], out_sems))
        piece_stores = list(copies_out(held, pieces, piece_sems))
        for copy in loads:
            copy.start()
        for load, *behind in zip(loads, stores, piece_stores):
            load.wait()
            for copy in behind:
                copy.start()
        for copy in stores + piece_stores:
            copy.wait()

    scratch = copy_scratch(rows, cols)
    return pl.pallas_call(
        kernel,
        in_specs=[pl.BlockSpec(memory_space=pl.ANY)] * 2,
        out_specs=[pl.BlockSpec(memory_space=pl.ANY)] * (1 + len(sizes)),
        out_shape=[jax.ShapeDtypeStruct((size, cols), array.dtype) for size in (rows, *sizes)],
        scratch_shapes=scratch + scratch[-1:],
        compiler_params=pltpu.CompilerParams(vmem_limit_bytes=VMEM),
    )(array, tail)


def choice_call(flag, a, b, earlier, cuts=(), keep=False):
    rows, cols = a.shape
    begins = [0, *cuts, rows]
    pieces = len(cuts) + 1
    shapes = [(end - begin, cols) for begin, end in zip(begins, begins[1:])]
    kept = [(rows, cols)] if keep else []

    def kernel(flag_ref, a_ref, b_ref, *refs):
        refs = refs[len(earlier) :]
        outs, kept_outs, scratch = refs[:pieces], refs[pieces : pieces + len(kept)], refs[pieces + len(kept) :]
        if keep:
            held, loads, stores, other_held, other_loads, other_stores = scratch
            leads = flag_ref[0] == 1
            ours = list(copies_in([a_ref], held, loads))
            theirs = list(copies_in([b_ref], other_held, other_loads))
            kept_copies = list(copies_out(held, kept_outs, stores))
            ours_out = list(copies_out(held, outs, other_stores))
            theirs_out = list(copies_out(other_held, outs, other_stores))
            for copy in ours:
                copy.start()

            @pl.when(jnp.logical_not(leads))
            def _():
                for copy in theirs:
                    copy.start()

            for load, store, also in zip(ours, kept_copies, ours_out):
                load.wait()
                store.start()
                pl.when(leads)(also.start)

            @pl.when(jnp.logical_not(leads))
            def _():
                for load, store in zip(theirs, theirs_out):
                    load.wait()
                    store.start()

            for store, also in zip(kept_copies, ours_out):
                store.wait()
                also.wait()
        else:
            for value, source in ((1, a_ref), (0, b_ref)):

                @pl.when(flag_ref[0] == value)
                def _(source=source):
                    parts = [source.at[pl.ds(at, out.shape[0])] for at, out in zip(begins, outs)]
                    copy_through(parts, outs, *scratch)

    return pl.pallas_call(
        kernel,
        in_specs=[pl.BlockSpec(memory_space=pltpu.SMEM)]
        + [pl.BlockSpec(memory_space=pl.ANY)] * (2 + len(earlier)),
        out_specs=[pl.BlockSpec(memory_space=pl.ANY)] * (pieces + len(kept)),
        out_shape=[jax.ShapeDtypeStruct(shape, a.dtype) for shape in shapes + kept],
        scratch_shapes=copy_scratch(rows, cols) * (1 + len(kept)),
        compiler_params=pltpu.CompilerParams(vmem_limit_bytes=VMEM),
        cost_estimate=pl.CostEstimate(flops=0, bytes_accessed=2 * a.size * a.dtype.itemsize, transcendentals=0),
    )(flag, a, b, *earlier)


def turn_call(array, rows, earlier):
    cols = array.shape[1]

    def kernel(array_ref, *refs):
        refs[-1][...] = array_ref[...].T

    return pl.pallas_call(
        kernel,
        grid=(rows // CHUNK,),
        in_specs=[pl.BlockSpec((CHUNK, cols), lambda i: (i, 0))]
        + [pl.BlockSpec(memory_space=pl.ANY)] * len(earlier),
        out_specs=pl.BlockSpec((cols, CHUNK), lambda i: (0, i)),
        out_shape=jax.ShapeDtypeStruct((cols, rows), array.dtype),
        compiler_params=pltpu.CompilerParams(vmem_limit_bytes=VMEM),
    )(array, *earlier)


def join_call(earlier):
    def kernel(*refs):
        refs[-1][...] = jnp.zeros_like(refs[-1])

    return pl.pallas_call(
        kernel,
        in_specs=[pl.BlockSpec(memory_space=pl.ANY)] * len(earlier),
        out_specs=pl.BlockSpec(memory_space=pltpu.VMEM),
        out_shape=jax.ShapeDtypeStruct((8, 128), jnp.float32),
    )(*earlier)


def density_call(terms, parts, out_dtype, aux, earlier, rows=None, copied=None, cuts=()):
    count = len(terms)
    depth = terms[0][0].array.shape[1]
    extra = list(copied or [])
    total_rows = sum(x.shape[0] for x in extra)
    ends = [0, *cuts, total_rows]
    whole = [jax.ShapeDtypeStruct((b - a, depth), jnp.bfloat16) for a, b in zip(ends, ends[1:]) if extra]
    pieces = [len(t[0].pieces) for t in terms]
    begins = [sum(pieces[:s]) for s in range(count)]
    cols = depth
    begin, length = rows or (0, aux)
    tile = 512
    while length % tile or begin % tile:
        tile //= 2
    steps = length // tile
    spans = []
    for part in parts:
        ends = np.cumsum([piece.shape[0] // tile for piece in part])
        shift = begin // tile if ends[-1] == aux // tile else 0
        spans.append([(int(end) - piece.shape[0] // tile - shift, int(end) - shift) for end, piece in zip(ends, part)])
    parts = [p for part in parts for p in part]

    def kernel(*refs):
        sources, refs = refs[: sum(pieces)], refs[sum(pieces) :]
        amps, refs = refs[:count], refs[count + len(earlier) :]
        source, refs = refs[: len(extra)], refs[len(extra) :]
        part_refs, out, refs = refs[: len(parts)], refs[len(parts)], refs[len(parts) + 1 :]
        target, refs = refs[: len(whole)], refs[len(whole) :]
        (left, right, left_sems, right_sems), scratch = refs[:4], refs[4:]
        step = pl.program_id(0)
        slot = step % 2

        def amp_copies():
            for s, (_, _, place) in enumerate(terms):
                yield pltpu.make_async_copy(
                    amps[s].at[place], right.at[:, pl.ds(s * depth, depth)], right_sems.at[s]
                )

        def slab_copies(which, start, of=range(count)):
            for s in of:
                end = 0
                for index in range(pieces[s]):
                    source = sources[begins[s] + index]
                    first = end
                    end += source.shape[0] // tile

                    def act(source=source, first=first, s=s):
                        row = pl.multiple_of((begin // tile + which - first) * tile, tile)
                        copy = pltpu.make_async_copy(
                            source.at[pl.ds(row, tile), :],
                            left.at[which % 2, :, pl.ds(s * depth, depth)],
                            left_sems.at[which % 2, s],
                        )
                        copy.start() if start else copy.wait()

                    at = begin // tile + which
                    if pieces[s] == 1:
                        act()
                    else:
                        pl.when(jnp.logical_and(at >= first, at < end))(act)

        @pl.when(step == 0)
        def _():
            for s, copy in enumerate(amp_copies()):
                copy.start()
                slab_copies(step, True, [s])
            if extra:
                for copy in copies_in(source, scratch[0], scratch[1]):
                    copy.start()

        @pl.when(step + 1 < steps)
        def _():
            slab_copies(step + 1, True)

        def finish(total):
            at = 0
            for span in spans:
                part = part_refs[at][...]
                for index in range(1, len(span)):
                    part = jnp.where(step >= span[index][0], part_refs[at + index][...], part)
                total = total + part.astype(jnp.float32)
                at += len(span)
            out[...] = total.astype(out.dtype)

        def product(a, b):
            return lax.dot_general(a, b, (((1,), (1,)), ((), ())), preferred_element_type=jnp.float32)

        @pl.when(step == 0)
        def _():
            total = None
            for s, copy in enumerate(amp_copies()):
                copy.wait()
                slab_copies(step, False, [s])
                at = pl.ds(s * depth, depth)
                term = product(left[0, :, at], right[:, at])
                total = term if total is None else total + term
            finish(total)

        @pl.when(step > 0)
        def _():
            slab_copies(step, False)
            finish(product(left[slot], right[...]))

        if extra:

            @pl.when(step == 1)
            def _():
                for copy in copies_in(source, scratch[0], scratch[1]):
                    copy.wait()
                for copy in copies_out(scratch[0], target, scratch[2]):
                    copy.start()

            @pl.when(step == steps - 1)
            def _():
                for copy in copies_out(scratch[0], target, scratch[2]):
                    copy.wait()

    def rows_of(start, end):
        return pl.BlockSpec((tile, cols), lambda i: (jnp.clip(i - start, 0, end - start - 1), 0))

    bytes_moved = 2 * count * (length * depth + cols * depth)
    bytes_moved += sum(length * cols * p.dtype.itemsize for p in parts)
    return pl.pallas_call(
        kernel,
        grid=(steps,),
        in_specs=[pl.BlockSpec(memory_space=pl.ANY)] * (sum(pieces) + count + len(earlier) + len(extra))
        + [rows_of(*ends) for span in spans for ends in span],
        out_specs=[pl.BlockSpec((tile, cols), lambda i: (i, 0))]
        + [pl.BlockSpec(memory_space=pl.ANY)] * len(whole),
        out_shape=[jax.ShapeDtypeStruct((length, cols), out_dtype)]
        + whole,
        scratch_shapes=[
            pltpu.VMEM((2, tile, count * depth), jnp.bfloat16),
            pltpu.VMEM((cols, count * depth), jnp.bfloat16),
            pltpu.SemaphoreType.DMA((2, count)),
            pltpu.SemaphoreType.DMA((count,)),
            *(copy_scratch(total_rows, depth) if extra else []),
        ],
        compiler_params=pltpu.CompilerParams(vmem_limit_bytes=VMEM),
        cost_estimate=pl.CostEstimate(
            flops=2 * length * depth * cols * count,
            bytes_accessed=(bytes_moved + length * cols * jnp.dtype(out_dtype).itemsize),
            transcendentals=0,
        ),
    )(*[p for t in terms for p in t[0].pieces], *[t[1] for t in terms], *earlier, *extra, *parts)


def paired_plan(three_index, orbital_map, occ_energy, vir_energy, pair_kept):
    blocks = lax.axis_size("wide")
    routes = Routes(blocks)
    here = lax.axis_index("wide")
    side = lax.axis_index("narrow")
    aux, vir_count = three_index.shape[1:]

    def moved(slab, pairs):
        sent = [lax.ppermute(piece, "wide", pairs) for piece in slab.pieces]
        return Slab(sent, routes.moved(slab.ids, pairs), slab.far)

    def swapped(slab):
        return moved(slab, routes.swap)

    flag = jnp.asarray(np.array(routes.lead, np.int32))[here].reshape(1)

    def copied(array, *earlier, cuts=()):
        return choice_call(flag, array, array, earlier, cuts)

    def sibling(array):
        return lax.ppermute(array, "narrow", [(0, 1), (1, 0)])

    plan = jnp.zeros((TAIL, vir_count), jnp.bfloat16)
    plan = plan.at[0, : ROUNDS + 1].set(pair_kept[:, 0].astype(jnp.bfloat16))
    whole, *split = append_call(three_index[0], plan, [aux // 2])
    own = Slab(whole, list(range(blocks)))

    r1 = moved(own, routes.rounds[0])
    own_far = Slab([sibling(piece) for piece in split], own.ids, 1)
    mate = swapped(own)

    labels = jnp.arange(occ_energy.shape[0], dtype=jnp.int32)
    picked = orbital_map[:, None] == labels[None, :]
    energy = jnp.sum(jnp.where(picked, occ_energy[None, :], 0.0), axis=1)

    def table_of(ids):
        ids = np.array(ids, np.int32).T
        places = np.arange(blocks)[:, None]
        back, forth = (places - ids) % blocks, (ids - places) % blocks
        behind = back <= ROUNDS
        known = np.stack([ids, np.where(behind, back, -1), np.where(behind, -1, forth)])
        block, mine, theirs = jnp.asarray(known.astype(np.int32))[:, here]
        places = jnp.arange(blocks, dtype=jnp.int32)[None, :]
        both = jnp.where(places == here, energy[None, :], 0.0)
        both = both + jnp.where(places == block[:, None], energy[None, :], 0.0)
        entries = jnp.arange(ROUNDS + 1, dtype=jnp.int32)[None, :]
        kept = pair_kept[:, 0].astype(jnp.float32)[None, :]
        weight = jnp.sum(jnp.where(entries == mine[:, None], kept, 0.0), axis=1)
        return jnp.stack([jnp.sum(both, axis=1), weight, theirs.astype(jnp.float32)], axis=1)

    vir = jnp.stack(
        [lax.dynamic_slice_in_dim(vir_energy, s * vir_count, vir_count) for s in (side, 1 - side)]
    )
    vir_rows, vir_cols = vir[:, :, None], vir[:, None, :]

    def moved_ids(ids_lead, ids_other, pairs):
        return routes.moved(routes.either(ids_lead, ids_other), pairs)

    def swapped_ids(ids):
        return routes.moved(ids, routes.swap)

    r2_ids = moved_ids(own.ids, r1.ids, routes.rounds[1])
    r3_ids = moved_ids(r2_ids, own.ids, routes.rounds[2])
    r4_ids = routes.moved(r3_ids, routes.rounds[3])
    r5_ids = routes.moved(own.ids, routes.rounds[4])
    all_ids = [own.ids, mate.ids]
    for ids in (r1.ids, r2_ids, r3_ids, r4_ids, r5_ids):
        all_ids += [ids, swapped_ids(ids)]
    table = table_of(all_ids)
    near, far = 0, 1
    rows_near = [own.array[:aux].T]
    stacks = {}

    def amps(jobs, turned, *earlier):
        lines = {slab: all_ids.index(slab.ids) for slab, _ in jobs}
        stack = amplitude_call(jobs, table, lines, turned, vir_rows, vir_cols, earlier)
        for place, job in enumerate(jobs):
            stacks[job] = (stack, place)
        return stack

    def density(slabs, block, parts, dtype, *earlier, rows=None, copied=None, cuts=()):
        terms = [(slab, *stacks[slab, block]) for slab in slabs]
        out, *copy = density_call(terms, parts, dtype, aux, earlier, rows, copied, cuts)
        return (out, *copy) if copy else out

    f32, bf16 = jnp.float32, jnp.bfloat16
    done = amps([(own, near), (mate, near)], [rows_near])

    parts = own_far.pieces
    sent, kept = choice_call(1 - flag, r1.array, own.array, [parts[0], done], keep=True)
    r1 = Slab(kept, r1.ids)
    sent2 = Slab(sent, routes.either(own.ids, r1.ids))
    r2 = moved(sent2, routes.rounds[1])
    s1 = swapped(r1)
    done = amps([(r1, near), (s1, near)], [rows_near], sent2.array)
    part = density([own, mate, r1, s1], near, [], f32, done)
    cut = parts[0].shape[0]
    rows_far = [turn_call(parts[0], cut, [part])]

    sent, kept = choice_call(flag, r2.array, own.array, [parts[1], *rows_far], keep=True)
    r2 = Slab(kept, r2.ids)
    sent3 = Slab(sent, routes.either(r2.ids, own.ids))
    r3 = moved(sent3, routes.rounds[2])
    s2 = swapped(r2)
    mate_far = swapped(own_far)
    rows_far.append(turn_call(parts[1], aux - cut, [sent3.array]))
    jobs = [(r2, near), (r2, far), (s2, far), (s2, near), (r1, far), (s1, far)]
    done = amps(jobs, [rows_near, rows_far])
    part = density([r2, s2], near, [[part]], f32, done)

    r3 = Slab(copied(r3.array, part), r3.ids)
    r4 = moved(r3, routes.rounds[3])
    s3 = swapped(r3)
    out_part, again = density([r1, s1, r2, s2], far, [], f32, r3.array, copied=own.pieces)
    r5 = moved(Slab(again, own.ids), routes.rounds[4])
    jobs = [(own_far, near), (mate_far, near), (r3, near), (r3, far), (s3, far), (s3, near)]
    done = amps(jobs, [rows_near, rows_far], out_part)

    done = amps([(r4, far)], [rows_near, rows_far], done)
    half = aux // 2
    slabs = [r3, s3, r4]
    sent0, again = density(
        slabs, far, [[out_part]], bf16, done, rows=(0, half), copied=own_far.pieces
    )
    r6 = moved(Slab(again, own.ids, 1), routes.rounds[4])
    sent1 = density(slabs, far, [[out_part]], bf16, sent0, rows=(half, half))
    incoming = [sibling(sent0), sibling(sent1)]
    done = amps([(r4, near)], [rows_near], sent1)
    part = density([own_far, mate_far, r3, s3, r4], near, [[part]], f32, done)

    thirds = [aux // 3, aux // 3 * 2]
    r5 = Slab(copied(r5.array, part, cuts=thirds), r5.ids)
    s5 = swapped(r5)
    done = amps([(r5, near)], [rows_near], *r5.pieces)
    done = join_call([incoming[0], done])
    done = amps([(s5, near)], [rows_near], done)
    part = density([r5, s5], near, [[part]], f32, done)
    r6 = Slab(copied(r6.array, part, cuts=thirds), r6.ids, 1)
    s6 = swapped(r6)
    done = amps([(r6, near)], [rows_near], *r6.pieces)
    done = amps([(s6, near)], [rows_near], done)
    return density([r6, s6], near, [[part], incoming], f32, done)[None]


def solution(mesh):
    wide, narrow = mesh.shape["wide"], mesh.shape["narrow"]
    paired = narrow == 2 and wide % 4 == 0 and wide > 2 * ROUNDS + 1 and ROUNDS == 5

    def per_device(three_index, *rest):
        if paired and three_index.shape[0] == 1:
            return paired_plan(three_index, *rest)
        return ring_plan(three_index, *rest)

    placed = (P("wide", None, "narrow"), P(), P(), P(), P(None, "wide"))
    return jax.shard_map(
        per_device, mesh=mesh, in_specs=placed, out_specs=P("wide", None, "narrow"), check_vma=False
    )
```
